32 devices in a mesh: dp: 8 (over y, x, core), tensor: 4 (over z).
Axes of the slice: x: 2, y: 2, z: 4, core: 2. Of those that a mesh axis runs over, the one named last changes fastest.
Arguments:
- inputs: bfloat16 [8192, 1536], P(('dp', 'tensor')), may hold values from -6 to 6
- segment_ids: int32 [8192], P('dp'), may hold values from 0 to 255, as said below
- first_gain: bfloat16 [1536], P('dp'), may hold values from 0.5 to 1.5
- query_weight: bfloat16 [1536, 1536], P('dp', 'tensor'), may hold values from -0.15625 to 0.15625
- query_bias: bfloat16 [1536], P(('tensor', 'dp')), may hold values from -3 to 3
- key_value_weight: bfloat16 [1536, 512], P('dp'), may hold values from -0.15625 to 0.15625
- key_value_bias: bfloat16 [512], P('dp'), may hold values from -3 to 3
- output_weight: bfloat16 [1536, 1536], P('tensor', 'dp'), may hold values from -0.625 to 0.625
- second_gain: bfloat16 [1536], P('dp'), may hold values from 0.5 to 1.5
- gateup_weight: bfloat16 [2, 1536, 8960], P(None, 'dp', 'tensor'), may hold values from -0.15625 to 0.15625
- down_weight: bfloat16 [8960, 1536], P('tensor', 'dp'), may hold values from -0.0625 to 0.0625
- cotangent: bfloat16 [8192, 1536], P(('dp', 'tensor')), may hold values from -6 to 6
Outputs:
- output: bfloat16 [8192, 1536], P(('dp', 'tensor'))
- input_grad: bfloat16 [8192, 1536], P(('dp', 'tensor'))
- first_gain_grad: float32 [1536], P('dp')
- query_weight_grad: float32 [1536, 1536], P('dp', 'tensor')
- query_bias_grad: float32 [1536], P(('tensor', 'dp'))
- keyval_weight_grad: float32 [1536, 512], P('dp')
- keyval_bias_grad: float32 [512], P('dp')
- output_weight_grad: float32 [1536, 1536], P('tensor', 'dp')
- second_gain_grad: float32 [1536], P('dp')
- gateup_weight_grad: float32 [2, 1536, 8960], P(None, 'dp', 'tensor')
- down_weight_grad: float32 [8960, 1536], P('tensor', 'dp')
The draws below stay inside these ranges and needn't reach their ends.
Inputs may be any that keep to these rules, and one draw needn't show every extreme that they name: `segment_ids`: within each group of 1024 tokens the ids start at 0 and never fall; each group has one segment that begins among its first 256 tokens and ends among its last 256; in every draw some group is a single segment of all 1024 tokens, and some group reaches the largest id.
All inputs are finite; a program needn't handle non-finite values.
Results may differ from the reference program's by a relative error of at most 0.02.
Values may be sent and summed in bfloat16 or wider, within the bound.
A program may use at most 192 MiB of HBM per device.

```python
import math
import jax
import jax.numpy as jnp
from jax import lax

MODEL_WIDTH = 1536
QUERY_HEADS = 12
KEYVALUE_HEADS = 2
HEAD_DIMENSION = 128
FF = 8960
TOK_DP = 1024
TOKENS = 8192


def draw_segment_ids(key, part):
    key = jax.random.fold_in(key, 7)
    keys = jax.random.split(key, 5)
    groups = TOKENS // TOK_DP
    lowest = 3 * TOK_DP // 4 + 1
    longest = jax.random.randint(keys[0], (groups,), lowest, TOK_DP + 1)
    chosen = jax.random.randint(keys[1], (), 0, groups)
    busy = (chosen + 1) % groups
    group_index = jnp.arange(groups)
    longest = jnp.where(group_index == chosen, TOK_DP, longest)
    longest = jnp.where(group_index == busy, lowest, longest)
    offset = jax.random.randint(keys[2], (groups,), 0, TOK_DP - longest + 1)
    offset = jnp.where(group_index == busy, 0, offset)
    index = jnp.arange(TOK_DP)[None, :]
    noise = jax.random.randint(keys[3], (groups, TOK_DP), 0, 64)
    rates = jax.random.randint(keys[4], (groups, 1), 1, 17)
    rates = jnp.where((group_index == busy)[:, None], 64, rates)
    marks = noise < rates
    inside = (index >= offset[:, None]) & (index < (offset + longest)[:, None])
    marks = marks & jnp.logical_not(inside)
    marks = marks | (index == offset[:, None]) | (index == (offset + longest)[:, None])
    marks = marks & (index > 0)
    return jnp.cumsum(marks.astype(jnp.int32), axis=1).astype(jnp.int32).reshape(TOKENS)


def steps_of(own_key, shape, cuts, least, top_value):
    factor_of = 1.0
    for dim, parts in cuts:
        heights = jax.random.uniform(jax.random.fold_in(jax.random.fold_in(own_key, 6), dim), (parts,), jnp.float32, least / len(cuts), top_value / len(cuts))
        factor_of = factor_of * jnp.repeat(jnp.exp(heights), shape[dim] // parts).reshape((-1,) + (1,) * (len(shape) - 1 - dim))
    return factor_of


def centred(own_key, dims, deviation, reach, cuts=(), kind=jnp.bfloat16):
    entries = deviation * jax.random.normal(own_key, dims, jnp.float32)
    if cuts:
        entries = entries * steps_of(own_key, dims, cuts, -0.22, 0.18)
    return jnp.clip(entries, -reach, reach).astype(kind)


def setup_inputs(seed: int = 0) -> dict:
    splits = jax.random.split(jax.random.key(seed), 13)
    return {
        "inputs": centred(splits[0], (TOKENS, MODEL_WIDTH), 1.0, 6.0, ((0, 32),)),
        "segment_ids": draw_segment_ids(jax.random.fold_in(splits[12], 71), 0),
        "first_gain": jnp.clip(1.0 + 0.1 * jax.random.normal(splits[2], (MODEL_WIDTH,), jnp.float32), 0.5, 1.5).astype(jnp.bfloat16),
        "query_weight": centred(splits[3], (MODEL_WIDTH, QUERY_HEADS * HEAD_DIMENSION), MODEL_WIDTH ** -0.5, 0.15625, ((0, 8), (1, 4))),
        "query_bias": centred(splits[4], (QUERY_HEADS * HEAD_DIMENSION,), 0.5, 3.0, ((0, 32),)),
        "key_value_weight": centred(splits[5], (MODEL_WIDTH, 2 * KEYVALUE_HEADS * HEAD_DIMENSION), MODEL_WIDTH ** -0.5, 0.15625, ((0, 8),)),
        "key_value_bias": centred(splits[6], (2 * KEYVALUE_HEADS * HEAD_DIMENSION,), 0.5, 3.0, ((0, 8),)),
        "output_weight": centred(splits[7], (QUERY_HEADS * HEAD_DIMENSION, MODEL_WIDTH), (QUERY_HEADS * HEAD_DIMENSION // 16) ** -0.5, 0.625, ((0, 4), (1, 8))),
        "second_gain": jnp.clip(1.0 + 0.1 * jax.random.normal(splits[8], (MODEL_WIDTH,), jnp.float32), 0.5, 1.5).astype(jnp.bfloat16),
        "gateup_weight": centred(splits[9], (2, MODEL_WIDTH, FF), MODEL_WIDTH ** -0.5, 0.15625, ((1, 8), (2, 4))),
        "down_weight": centred(splits[10], (FF, MODEL_WIDTH), FF ** -0.5, 0.0625, ((0, 4), (1, 8))),
        "cotangent": centred(splits[11], (TOKENS, MODEL_WIDTH), 1.0, 6.0, ((0, 32),)),
    }


@jax.custom_vjp
def lower_precision(v):
    return lax.optimization_barrier(v.astype(jnp.bfloat16)).astype(jnp.float32)

@jax.custom_vjp
def low_back(v):
    return v

def low_keep(v):
    return (lower_precision(v), None)

def low_pass(kept, grad):
    return (grad,)

def back_keep(v):
    return (v, None)

def back_low(kept, grad):
    return (lower_precision(grad),)
lower_precision.defvjp(low_keep, low_pass)
low_back.defvjp(back_keep, back_low)
EPSILON = 1e-06
THETA = 1000000.0
NEGATIVE = -1e+30
HIGHEST = lax.Precision.HIGHEST

def matmul(left, right):
    return jnp.dot(left, right, precision=HIGHEST, preferred_element_type=jnp.float32)

def rms_scale(rows):
    return lax.rsqrt(lax.optimization_barrier(jnp.mean(rows * rows, axis=-1, keepdims=True)) + EPSILON)

def rope_tables(segments, head_extent):
    index = jnp.arange(segments.shape[0], dtype=jnp.int32)
    starts = jnp.concatenate([jnp.ones((1,), dtype=bool), segments[1:] != segments[:-1]])
    first = lax.cummax(jnp.where(starts, index, jnp.zeros_like(index)), axis=0)
    placed = (index - first).astype(jnp.float32)
    freqs = jnp.exp(jnp.arange(head_extent // 2, dtype=jnp.float32) * (-2.0 * math.log(THETA) / head_extent))
    angles = placed[:, None] * freqs[None, :]
    return (jnp.cos(angles)[:, None, :], jnp.sin(angles)[:, None, :])

def apply_rotation(value_rows, cosine_table, sine_table):
    half = value_rows.shape[-1] // 2
    former = value_rows[..., :half]
    latter = value_rows[..., half:]
    return jnp.concatenate([former * cosine_table - latter * sine_table, latter * cosine_table + former * sine_table], axis=-1)

def group_forward(inputs, segments, first_gain, query_weight, query_bias, key_value_weight, key_value_bias, output_weight, second_gain, gateup_weight, down_weight):
    item_count = inputs.shape[0]
    normed = lower_precision(inputs * rms_scale(inputs) * first_gain)
    query = low_back(matmul(normed, query_weight) + query_bias)
    key_value_rows = low_back(matmul(normed, key_value_weight) + key_value_bias)
    cosine_table, sine_table = rope_tables(segments, HEAD_DIMENSION)
    rot_query = lower_precision(apply_rotation(query.reshape(item_count, QUERY_HEADS, HEAD_DIMENSION), cosine_table, sine_table))
    rotated_key = lower_precision(apply_rotation(key_value_rows[:, :KEYVALUE_HEADS * HEAD_DIMENSION].reshape(item_count, KEYVALUE_HEADS, HEAD_DIMENSION), cosine_table, sine_table))
    value_rows = lower_precision(key_value_rows[:, KEYVALUE_HEADS * HEAD_DIMENSION:]).reshape(item_count, KEYVALUE_HEADS, HEAD_DIMENSION)
    repeat_factor = QUERY_HEADS // KEYVALUE_HEADS
    rotated_key = jnp.repeat(rotated_key, repeat_factor, axis=1)
    value_rows = jnp.repeat(value_rows, repeat_factor, axis=1)
    raw = low_back(jnp.einsum('qhd,khd->hqk', rot_query, rotated_key, precision=HIGHEST))
    index = jnp.arange(item_count, dtype=jnp.int32)
    allowed = (segments[:, None] == segments[None, :]) & (index[None, :] <= index[:, None])
    scores = jnp.where(allowed[None], raw * (1.0 / math.sqrt(HEAD_DIMENSION)), NEGATIVE)
    probs = lower_precision(jax.nn.softmax(scores, axis=-1))
    attended = jnp.einsum('hqk,khd->qhd', probs, value_rows, precision=HIGHEST).reshape(item_count, QUERY_HEADS * HEAD_DIMENSION)
    attended = lower_precision(low_back(attended))
    residual = inputs + low_back(matmul(attended, output_weight))
    second = lower_precision(residual * rms_scale(residual) * second_gain)
    gate = low_back(matmul(second, gateup_weight[0]))
    upper = low_back(matmul(second, gateup_weight[1]))
    hidden = lower_precision(jax.nn.silu(gate) * upper)
    return residual + matmul(hidden, down_weight)

def reference(inputs, segment_ids, first_gain, query_weight, query_bias, key_value_weight, key_value_bias, output_weight, second_gain, gateup_weight, down_weight, cotangent):
    params = tuple((p.astype(jnp.float32) for p in (first_gain, query_weight, query_bias, key_value_weight, key_value_bias, output_weight, second_gain, gateup_weight, down_weight)))
    grouped = inputs.astype(jnp.float32).reshape(TOKENS // TOK_DP, TOK_DP, MODEL_WIDTH)
    segments = segment_ids.reshape(TOKENS // TOK_DP, TOK_DP)
    checked = jax.checkpoint(group_forward)

    def forward(grouped_inputs, weights):

        def advance(carry, item):
            return (carry, checked(item[0], item[1], *weights))
        unused, results = lax.scan(advance, jnp.zeros((), jnp.float32), (grouped_inputs, segments))
        return results
    results, pullback = jax.vjp(forward, grouped, params)
    grouped_grad, weight_grads = pullback(cotangent.astype(jnp.float32).reshape(results.shape))
    gain1_grad, qweight_grad, qbias_grad, kvweight_grad, kvbias_grad, oweight_grad, gain2_grad, gateup_grad, down_grad = weight_grads
    return (results.reshape(TOKENS, MODEL_WIDTH).astype(jnp.bfloat16), grouped_grad.reshape(TOKENS, MODEL_WIDTH).astype(jnp.bfloat16), gain1_grad, qweight_grad, qbias_grad, kvweight_grad, kvbias_grad, oweight_grad, gain2_grad, gateup_grad, down_grad)
```

```python
import functools
import math

import jax
import jax.numpy as jnp
from jax import lax
from jax.experimental import pallas as pl
from jax.experimental.pallas import tpu as pltpu
from jax.sharding import PartitionSpec as P

QUERY_HEADS = 12
KEYVALUE_HEADS = 2
HEAD_DIMENSION = 128
REPEAT = QUERY_HEADS // KEYVALUE_HEADS

EPSILON = 1e-06
THETA = 1000000.0
NEGATIVE = -1e30

F32 = jnp.float32
BF16 = jnp.bfloat16


def rms_scale(rows):
    return lax.rsqrt(jnp.mean(rows * rows, axis=-1, keepdims=True) + EPSILON)


def norm_back(rows, gain, grad):
    scale = rms_scale(rows)
    normed = rows * scale
    weighted = grad * gain
    inner = jnp.mean(weighted * normed, axis=-1, keepdims=True)
    return (scale * (weighted - normed * inner), jnp.sum(grad * normed, axis=0))


def rope_tables(segments, head_extent):
    index = jnp.arange(segments.shape[0], dtype=jnp.int32)
    starts = jnp.concatenate([jnp.ones((1,), dtype=bool), segments[1:] != segments[:-1]])
    first = lax.cummax(jnp.where(starts, index, jnp.zeros_like(index)), axis=0)
    placed = (index - first).astype(F32)
    freqs = jnp.exp(
        jnp.arange(head_extent // 2, dtype=F32) * (-2.0 * math.log(THETA) / head_extent)
    )
    return placed, freqs


def apply_rotation(value_rows, cosine_table, sine_table):
    half = value_rows.shape[-1] // 2
    former = value_rows[..., :half]
    latter = value_rows[..., half:]
    return jnp.concatenate(
        [former * cosine_table - latter * sine_table, latter * cosine_table + former * sine_table],
        axis=-1,
    )


def unrotate(grads, cosine_table, sine_table):
    return apply_rotation(grads, cosine_table, -sine_table)


def dot(left, right):
    return jnp.dot(left, right, preferred_element_type=F32)


def dot_nt(left, right):
    return lax.dot_general(left, right, (((1,), (1,)), ((), ())), preferred_element_type=F32)


def dot_tn(left, right):
    return lax.dot_general(left, right, (((0,), (0,)), ((), ())), preferred_element_type=F32)


MESH = pl.DeviceIdType.MESH
ANY = pl.ANY


def flip(index, bit):
    return index + (1 << bit) * (1 - 2 * ((index // (1 << bit)) % 2))


class Place:
    def __init__(self, dp, tp):
        self.dp, self.tp = dp, tp
        self.d, self.z = lax.axis_index("dp"), lax.axis_index("tensor")
        self.steps = dp.bit_length() - 2
        odd = self.d % 2
        self.partners = []
        for step in range(self.steps):
            first, other = flip(self.d, 1 + step), flip(self.d, self.steps - step)
            self.partners.append(first + odd * (other - first))
        self.sibling = flip(self.d, 0)
        self.deltas = [partner - self.d for partner in self.partners]

    def block(self, mask):
        index = self.d
        for step in range(self.steps):
            if (mask >> step) & 1:
                index = index + self.deltas[step]
        return index

    def sibling_block(self, mask):
        index = self.sibling
        for step in range(self.steps):
            if (mask >> step) & 1:
                index = index + self.deltas[self.steps - 1 - step]
        return index

    def device(self, index):
        return (index, self.z)

    def beside(self, offset):
        return (self.d, self.z + offset)

    def greet(self, plane, line):
        barrier = pltpu.get_barrier_semaphore()
        count = 0
        if plane:
            for partner in self.partners + [self.sibling]:
                pl.semaphore_signal(
                    barrier, inc=1, device_id=self.device(partner), device_id_type=MESH
                )
            count = self.steps + 1
        if line:
            for offset in (-1, 1):

                @pl.when(self.has(offset))
                def _():
                    pl.semaphore_signal(
                        barrier, inc=1, device_id=self.beside(offset), device_id_type=MESH
                    )

            count = count + jnp.where(self.z > 0, 1, 0) + jnp.where(self.z < self.tp - 1, 1, 0)
        pl.semaphore_wait(barrier, count)

    def has(self, offset):
        return (self.z + offset >= 0) & (self.z + offset < self.tp)


def remote(src, dst, send, recv, device):
    return pltpu.make_async_remote_copy(
        src_ref=src, dst_ref=dst, send_sem=send, recv_sem=recv, device_id=device, device_id_type=MESH
    )


class PlaneGather:
    def __init__(self, place, own, full, send, recv):
        self.place, self.own, self.full, self.send, self.recv = place, own, full, send, recv
        self.half = 1 << place.steps

    def at(self, mask):
        return self.full(self.place.block(mask)) if mask else self.own

    def copy(self, mask, step):
        place = self.place
        if step < place.steps:
            label, device = mask | (1 << step), place.device(place.partners[step])
        else:
            label, device = self.half + mask, place.device(place.sibling)
        return remote(
            self.at(mask), self.full(place.block(mask)), self.send(label), self.recv(label), device
        )

    def arrival(self, label):
        place = self.place
        if label < self.half:
            ref = self.full(place.block(label))
        else:
            ref = self.full(place.sibling_block(label - self.half))
        return remote(ref, ref, self.send(label), self.recv(label), place.device(place.sibling))

    def sends(self, mask):
        return [self.copy(mask, step) for step in range(mask.bit_length(), self.place.steps + 1)]

    def start(self):
        for copy in self.sends(0):
            copy.start()

    def hand_on(self, mask):
        self.arrival(mask).wait_recv()
        for copy in self.sends(mask):
            copy.start()

    def finish(self):
        for mask in range(self.half):
            self.arrival(self.half + mask).wait_recv()
        for mask in range(self.half):
            for copy in self.sends(mask):
                copy.wait_send()


class LineGather:
    def __init__(self, place, own, full, send, recv):
        self.place, self.own, self.full, self.send, self.recv = place, own, full, send, recv

    def copy(self, distance, offset):
        place = self.place
        source = place.z - offset * distance
        side = 0 if offset > 0 else 1
        src = self.full(source) if distance else self.own
        return remote(
            src,
            self.full(source),
            self.send(side, distance),
            self.recv(side, distance),
            place.beside(offset),
        )

    def each(self, distance, act):
        place = self.place
        for offset in (1, -1):

            @pl.when(place.has(-offset * distance) & place.has(offset))
            def _():
                act(self.copy(distance, offset))

    def start(self):
        self.each(0, lambda copy: copy.start())

    def arrived(self, distance):
        place = self.place
        for offset in (1, -1):

            @pl.when(place.has(-offset * distance))
            def _():
                side = 0 if offset > 0 else 1
                ref = self.full(place.z - offset * distance)
                remote(
                    ref,
                    ref,
                    self.send(side, distance - 1),
                    self.recv(side, distance - 1),
                    place.beside(-offset),
                ).wait_recv()

    def hand_on(self, distance):
        self.arrived(distance)
        if distance < self.place.tp - 1:
            self.each(distance, lambda copy: copy.start())

    def finish(self):
        for distance in range(self.place.tp - 1):
            self.each(distance, lambda copy: copy.wait_send())


def gather_kernel(
    dp, tp, zq, zo, kvs, ff, cot, q_out, o_out, kv_out, ff_out, cot_out,
    plane_send, plane_recv, line_send, line_recv, local_sem,
):
    place = Place(dp, tp)
    d, z = place.d, place.z
    locals_ = [
        pltpu.make_async_copy(zq, q_out.at[d, z], local_sem.at[0]),
        pltpu.make_async_copy(zo, o_out.at[d, z], local_sem.at[1]),
        pltpu.make_async_copy(kvs, kv_out.at[d], local_sem.at[2]),
        pltpu.make_async_copy(ff, ff_out.at[d], local_sem.at[3]),
        pltpu.make_async_copy(cot, cot_out.at[z], local_sem.at[4]),
    ]
    for copy in locals_:
        copy.start()
    place.greet(True, True)

    def plane(item, own, full):
        return PlaneGather(
            place, own, full, lambda m: plane_send.at[item, m], lambda m: plane_recv.at[item, m]
        )

    def line(item, own, full):
        return LineGather(
            place,
            own,
            full,
            lambda s, k: line_send.at[item, s, k],
            lambda s, k: line_recv.at[item, s, k],
        )

    line_q = line(0, zq, lambda t: q_out.at[d, t])
    line_o = line(1, zo, lambda t: o_out.at[d, t])
    line_cot = line(2, cot, lambda t: cot_out.at[t])
    plane_kv = plane(0, kvs, lambda b: kv_out.at[b])
    plane_q = plane(1, q_out.at[d], lambda b: q_out.at[b])
    plane_o = plane(2, o_out.at[d], lambda b: o_out.at[b])
    plane_ff = [
        plane(3 + part, ff.at[part], lambda b, part=part: ff_out.at[b, part]) for part in (2, 0, 1)
    ]
    line_q.start()
    plane_kv.start()
    for distance in range(1, tp):
        line_q.hand_on(distance)
    line_o.start()
    locals_[0].wait()
    plane_q.start()
    for mask in range(1, 1 << place.steps):
        plane_kv.hand_on(mask)
    for distance in range(1, tp):
        line_o.hand_on(distance)
    line_cot.start()
    locals_[1].wait()
    queue = [plane_q, plane_o] + plane_ff
    for item, following in zip(queue, queue[1:] + [None]):
        if following is not None:
            following.start()
        for mask in range(1, 1 << place.steps):
            item.hand_on(mask)
    for distance in range(1, tp):
        line_cot.hand_on(distance)
    for item in [plane_kv] + queue:
        item.finish()
    for item in (line_q, line_o, line_cot):
        item.finish()
    for copy in locals_[2:]:
        copy.wait()


def gather_all(dp, tp, zq, zo, kvs, ff, cot):
    def shape(*dims):
        return jax.ShapeDtypeStruct(dims, BF16)

    return pl.pallas_call(
        functools.partial(gather_kernel, dp, tp),
        out_shape=(
            shape(dp, tp, *zq.shape),
            shape(dp, tp, *zo.shape),
            shape(dp, *kvs.shape),
            shape(dp, *ff.shape),
            shape(tp, *cot.shape),
        ),
        in_specs=[pl.BlockSpec(memory_space=ANY)] * 5,
        out_specs=[pl.BlockSpec(memory_space=ANY)] * 5,
        scratch_shapes=[
            pltpu.SemaphoreType.DMA((6, dp)),
            pltpu.SemaphoreType.DMA((6, dp)),
            pltpu.SemaphoreType.DMA((3, 2, tp)),
            pltpu.SemaphoreType.DMA((3, 2, tp)),
            pltpu.SemaphoreType.DMA((5,)),
        ],
        compiler_params=pltpu.CompilerParams(collective_id=0, has_side_effects=True),
        name="gather_weights",
    )(zq, zo, kvs, ff, cot)


def local(
    inputs,
    segment_ids,
    first_gain,
    query_weight,
    query_bias,
    key_value_weight,
    key_value_bias,
    output_weight,
    second_gain,
    gateup_weight,
    down_weight,
    cotangent,
):
    dp = lax.axis_size("dp")
    tp = lax.axis_size("tensor")
    rank = lax.axis_index("tensor")
    width = inputs.shape[1]
    own_rows = inputs.shape[0]
    depth = query_weight.shape[0]
    columns = query_weight.shape[1]
    kv_columns = key_value_weight.shape[1]
    hidden_units = gateup_weight.shape[2]
    heads_width = columns * tp
    head = HEAD_DIMENSION
    scale = 1.0 / math.sqrt(head)

    padded = -(-hidden_units // 256) * 256
    ff_own = jnp.stack([gateup_weight[0], gateup_weight[1], down_weight.T])
    ff_own = jnp.pad(ff_own, ((0, 0), (0, 0), (0, padded - hidden_units)))
    bias_rows = jnp.pad(query_bias[None, :], ((0, 15), (0, columns - query_bias.shape[0])))
    own_kvbias = jnp.pad(key_value_bias, (0, depth - key_value_bias.shape[0]))
    side = jnp.pad(jnp.stack([first_gain, second_gain, own_kvbias], axis=1), ((0, 0), (0, 125)))
    q_all, o_all, kv_all, ff_all, grad_rows = gather_all(
        dp,
        tp,
        jnp.concatenate([query_weight, bias_rows], axis=0),
        output_weight.T,
        jnp.concatenate([key_value_weight, side], axis=1),
        ff_own,
        cotangent,
    )
    grad_rows = grad_rows.reshape(-1, width)
    edge_q = heads_width
    edge_kv = edge_q + kv_columns
    edge_o = edge_kv + heads_width
    query_full = q_all[:, :, :depth].transpose(0, 2, 1, 3).reshape(width, -1)
    qbias_full = q_all[:, :, depth, : query_bias.shape[0]].transpose(1, 0, 2).reshape(-1)
    out_t_weight = o_all.transpose(0, 2, 1, 3).reshape(width, -1)
    kv_all = kv_all.reshape(width, -1)
    qkv_weight = jnp.concatenate([query_full, kv_all[:, :kv_columns]], axis=1)
    side = kv_all[:, kv_columns : kv_columns + 3].T.astype(F32)
    gain_one, gain_two = side[0], side[1]
    kvbias_full = side[2].reshape(dp, depth)[:, : key_value_bias.shape[0]].reshape(-1)
    qbias_full = qbias_full.astype(F32)
    gate_w = ff_all[:, 0].reshape(width, padded)
    up_w = ff_all[:, 1].reshape(width, padded)
    down_t = ff_all[:, 2].reshape(width, padded)

    own_inputs = inputs.astype(F32)
    normed_own = (own_inputs * rms_scale(own_inputs) * gain_one).astype(BF16)
    placed, freqs = rope_tables(segment_ids, head)
    begin = rank * own_rows
    own_placed = lax.dynamic_slice_in_dim(placed, begin, own_rows, 0)
    own_segments = lax.dynamic_slice_in_dim(segment_ids, begin, own_rows, 0)
    angles = own_placed[:, None] * freqs[None, :]
    cosine, sine = jnp.cos(angles)[:, None, :], jnp.sin(angles)[:, None, :]

    qkv = dot(normed_own, qkv_weight) + jnp.concatenate([qbias_full, kvbias_full])
    half_kv = kv_columns // 2
    rot = apply_rotation(
        qkv[:, : edge_q + half_kv].reshape(own_rows, -1, head), cosine, sine
    ).astype(BF16)
    rot_query = rot[:, :QUERY_HEADS]
    own_kv = jnp.concatenate(
        [rot[:, QUERY_HEADS:].reshape(own_rows, half_kv), qkv[:, edge_q + half_kv :].astype(BF16)],
        axis=1,
    )
    all_kv = lax.all_gather(own_kv, "tensor", axis=0, tiled=True)
    items = all_kv.shape[0]
    all_kv = all_kv.reshape(items, 2, KEYVALUE_HEADS, head)
    keys, value_rows = all_kv[:, 0], all_kv[:, 1]
    grouped = rot_query.reshape(own_rows, KEYVALUE_HEADS, REPEAT, head)

    index = jnp.arange(items, dtype=jnp.int32)
    own_index = begin + jnp.arange(own_rows, dtype=jnp.int32)
    allowed = (own_segments[:, None] == segment_ids[None, :]) & (
        index[None, :] <= own_index[:, None]
    )
    scores = jnp.einsum("qgrd,kgd->grqk", grouped, keys, preferred_element_type=F32) * scale
    scores = jnp.where(allowed[None, None], scores, NEGATIVE)
    top = jnp.max(scores, axis=-1, keepdims=True)
    weights = jnp.exp(scores - top)
    total = jnp.sum(weights, axis=-1, keepdims=True)
    probs = weights / total
    probs_low = probs.astype(BF16)
    attended = (
        jnp.einsum("grqk,kgd->qgrd", probs_low, value_rows, preferred_element_type=F32)
        .reshape(own_rows, -1)
        .astype(BF16)
    )
    residual = own_inputs + dot_nt(attended, out_t_weight)
    second_own = (residual * rms_scale(residual) * gain_two).astype(BF16)
    second_rows = lax.all_gather(second_own, "tensor", axis=0, tiled=True)

    gate = dot(second_rows, gate_w)
    upper = dot(second_rows, up_w)
    sigmoid = jax.nn.sigmoid(gate)
    swish = gate * sigmoid
    hidden = (swish * upper).astype(BF16)
    d_hidden = dot(grad_rows, down_t)
    d_gate = (d_hidden * upper * sigmoid * (1.0 + gate * (1.0 - sigmoid))).astype(BF16)
    d_up = (d_hidden * swish).astype(BF16)
    second_terms = dot_nt(d_gate, gate_w) + dot_nt(d_up, up_w)
    d_second = lax.psum_scatter(
        second_terms.astype(BF16), "tensor", scatter_dimension=0, tiled=True
    ).astype(F32)
    down_grad = dot_tn(grad_rows, hidden).astype(BF16)
    down_sh = lax.psum_scatter(down_grad, "dp", scatter_dimension=0, tiled=True)
    gate_grad = dot_tn(second_rows, d_gate).astype(BF16)
    gate_sh = lax.psum_scatter(gate_grad, "dp", scatter_dimension=0, tiled=True)
    up_grad = dot_tn(second_rows, d_up).astype(BF16)
    up_sh = lax.psum_scatter(up_grad, "dp", scatter_dimension=0, tiled=True)
    mlp_terms = dot_nt(hidden, down_t).astype(BF16)
    mlp_own = lax.psum_scatter(mlp_terms, "tensor", scatter_dimension=0, tiled=True)
    output = (residual + mlp_own.astype(F32)).astype(BF16)

    residual_part, gain_two_grad = norm_back(residual, gain_two, d_second)
    d_residual = cotangent.astype(F32) + residual_part
    d_branch = d_residual.astype(BF16)
    d_attended = dot(d_branch, out_t_weight).astype(BF16)
    d_att = d_attended.reshape(own_rows, KEYVALUE_HEADS, REPEAT, head)
    d_probs = jnp.einsum("qgrd,kgd->grqk", d_att, value_rows, preferred_element_type=F32)
    inner = jnp.sum(probs * d_probs, axis=-1, keepdims=True)
    d_scores = (scale * probs * (d_probs - inner)).astype(BF16)
    d_rot_query = jnp.einsum("grqk,kgd->qgrd", d_scores, keys, preferred_element_type=F32)
    d_keys = jnp.einsum("grqk,qgrd->kgd", d_scores, grouped, preferred_element_type=F32)
    d_values = jnp.einsum("grqk,qgrd->kgd", probs_low, d_att, preferred_element_type=F32)
    d_kv = lax.psum_scatter(
        jnp.concatenate([d_keys.reshape(items, -1), d_values.reshape(items, -1)], axis=1).astype(
            BF16
        ),
        "tensor",
        scatter_dimension=0,
        tiled=True,
    ).astype(F32)
    d_rot = jnp.concatenate(
        [
            d_rot_query.reshape(own_rows, QUERY_HEADS, head),
            d_kv[:, :half_kv].reshape(own_rows, KEYVALUE_HEADS, head),
        ],
        axis=1,
    )
    d_rot = unrotate(d_rot, cosine, sine).reshape(own_rows, -1)
    d_qkv = jnp.concatenate([d_rot, d_kv[:, half_kv:]], axis=1).astype(BF16)
    d_normed = dot_nt(d_qkv, qkv_weight)
    bias_grad = jnp.sum(d_qkv.astype(F32), axis=0)
    input_part, gain_one_grad = norm_back(own_inputs, gain_one, d_normed)
    input_grad = (d_residual + input_part).astype(BF16)

    qkv_grad = dot_tn(normed_own, d_qkv)
    out_grad = dot_tn(d_branch, attended)
    qb = bias_grad[:edge_q].reshape(tp, dp, -1).transpose(1, 0, 2).reshape(-1)
    kvb = jnp.pad(bias_grad[edge_q:].reshape(dp, -1), ((0, 0), (0, depth - kv_columns // dp)))
    side_grad = jnp.stack([gain_one_grad, gain_two_grad, qb, kvb.reshape(-1)], axis=1)
    side_grad = jnp.pad(side_grad, ((0, 0), (0, 124)))
    attn_grad = jnp.concatenate([qkv_grad, out_grad, side_grad], axis=1).astype(BF16)
    attn_sh = lax.psum_scatter(attn_grad, "dp", scatter_dimension=0, tiled=True)
    q_part = attn_sh[:, :edge_q].reshape(depth, tp, columns).transpose(1, 0, 2)
    o_part = attn_sh[:, edge_kv:edge_o].reshape(depth, tp, columns).transpose(1, 0, 2)
    qo = lax.psum_scatter(
        jnp.concatenate([q_part, o_part], axis=1).reshape(tp * 2 * depth, columns),
        "tensor",
        scatter_dimension=0,
        tiled=True,
    ).astype(F32)
    rest = lax.psum(
        jnp.concatenate([attn_sh[:, edge_q:edge_kv], attn_sh[:, edge_o:]], axis=1), "tensor"
    ).astype(F32)
    side_sh = rest[:, kv_columns : kv_columns + 4].T
    qb_count = query_bias.shape[0]
    return (
        output,
        input_grad,
        side_sh[0],
        qo[:depth],
        lax.dynamic_slice_in_dim(side_sh[2], rank * qb_count, qb_count, 0),
        rest[:, :kv_columns],
        side_sh[3][: kv_columns // dp],
        qo[depth:].T,
        side_sh[1],
        jnp.stack([gate_sh[:, :hidden_units], up_sh[:, :hidden_units]]).astype(F32),
        down_sh[:, :hidden_units].T.astype(F32),
    )


def solution(mesh):
    in_specs = (
        P(("dp", "tensor"), None),
        P("dp"),
        P("dp"),
        P("dp", "tensor"),
        P(("tensor", "dp")),
        P("dp", None),
        P("dp"),
        P("tensor", "dp"),
        P("dp"),
        P(None, "dp", "tensor"),
        P("tensor", "dp"),
        P(("dp", "tensor"), None),
    )
    out_specs = (
        P(("dp", "tensor"), None),
        P(("dp", "tensor"), None),
        P("dp"),
        P("dp", "tensor"),
        P(("tensor", "dp")),
        P("dp", None),
        P("dp"),
        P("tensor", "dp"),
        P("dp"),
        P(None, "dp", "tensor"),
        P("tensor", "dp"),
    )
    return jax.shard_map(local, mesh=mesh, in_specs=in_specs, out_specs=out_specs, check_vma=False)
```

```python
import functools
import math

import jax
import jax.numpy as jnp
from jax import lax
from jax.experimental import pallas as pl
from jax.experimental.pallas import tpu as pltpu
from jax.sharding import PartitionSpec as P

QUERY_HEADS = 12
KEYVALUE_HEADS = 2
HEAD_DIMENSION = 128
REPEAT = QUERY_HEADS // KEYVALUE_HEADS

EPSILON = 1e-06
THETA = 1000000.0
NEGATIVE = -1e30

F32 = jnp.float32
BF16 = jnp.bfloat16


def rms_scale(rows):
    return lax.rsqrt(jnp.mean(rows * rows, axis=-1, keepdims=True) + EPSILON)


def norm_back(rows, gain, grad):
    scale = rms_scale(rows)
    normed = rows * scale
    weighted = grad * gain
    inner = jnp.mean(weighted * normed, axis=-1, keepdims=True)
    return (scale * (weighted - normed * inner), jnp.sum(grad * normed, axis=0))


def rope_tables(segments, head_extent):
    index = jnp.arange(segments.shape[0], dtype=jnp.int32)
    starts = jnp.concatenate([jnp.ones((1,), dtype=bool), segments[1:] != segments[:-1]])
    first = lax.cummax(jnp.where(starts, index, jnp.zeros_like(index)), axis=0)
    placed = (index - first).astype(F32)
    freqs = jnp.exp(
        jnp.arange(head_extent // 2, dtype=F32) * (-2.0 * math.log(THETA) / head_extent)
    )
    return placed, freqs


def apply_rotation(value_rows, cosine_table, sine_table):
    half = value_rows.shape[-1] // 2
    former = value_rows[..., :half]
    latter = value_rows[..., half:]
    return jnp.concatenate(
        [former * cosine_table - latter * sine_table, latter * cosine_table + former * sine_table],
        axis=-1,
    )


def unrotate(grads, cosine_table, sine_table):
    return apply_rotation(grads, cosine_table, -sine_table)


def dot(left, right):
    return jnp.dot(left, right, preferred_element_type=F32)


def dot_nt(left, right):
    return lax.dot_general(left, right, (((1,), (1,)), ((), ())), preferred_element_type=F32)


def dot_tn(left, right):
    return lax.dot_general(left, right, (((0,), (0,)), ((), ())), preferred_element_type=F32)


MESH = pl.DeviceIdType.MESH
ANY = pl.ANY


def flip(index, bit):
    return index + (1 << bit) * (1 - 2 * ((index // (1 << bit)) % 2))


class Place:
    def __init__(self, dp, tp):
        self.dp, self.tp = dp, tp
        self.d, self.z = lax.axis_index("dp"), lax.axis_index("tensor")
        self.steps = dp.bit_length() - 2
        odd = self.d % 2
        self.partners = []
        for step in range(self.steps):
            first, other = flip(self.d, 1 + step), flip(self.d, self.steps - step)
            self.partners.append(first + odd * (other - first))
        self.sibling = flip(self.d, 0)
        self.deltas = [partner - self.d for partner in self.partners]

    def block(self, mask):
        index = self.d
        for step in range(self.steps):
            if (mask >> step) & 1:
                index = index + self.deltas[step]
        return index

    def sibling_block(self, mask):
        index = self.sibling
        for step in range(self.steps):
            if (mask >> step) & 1:
                index = index + self.deltas[self.steps - 1 - step]
        return index

    def device(self, index):
        return (index, self.z)

    def beside(self, offset):
        return (self.d, self.z + offset)

    def greet(self, plane, line):
        barrier = pltpu.get_barrier_semaphore()
        count = 0
        if plane:
            for partner in self.partners + [self.sibling]:
                pl.semaphore_signal(
                    barrier, inc=1, device_id=self.device(partner), device_id_type=MESH
                )
            count = self.steps + 1
        if line:
            for offset in (-1, 1):

                @pl.when(self.has(offset))
                def _():
                    pl.semaphore_signal(
                        barrier, inc=1, device_id=self.beside(offset), device_id_type=MESH
                    )

            count = count + jnp.where(self.z > 0, 1, 0) + jnp.where(self.z < self.tp - 1, 1, 0)
        pl.semaphore_wait(barrier, count)

    def has(self, offset):
        return (self.z + offset >= 0) & (self.z + offset < self.tp)


def remote(src, dst, send, recv, device):
    return pltpu.make_async_remote_copy(
        src_ref=src, dst_ref=dst, send_sem=send, recv_sem=recv, device_id=device, device_id_type=MESH
    )


class PlaneGather:
    def __init__(self, place, own, full, send, recv):
        self.place, self.own, self.full, self.send, self.recv = place, own, full, send, recv
        self.half = 1 << place.steps

    def at(self, mask):
        return self.full(self.place.block(mask)) if mask else self.own

    def copy(self, mask, step):
        place = self.place
        if step < place.steps:
            label, device = mask | (1 << step), place.device(place.partners[step])
        else:
            label, device = self.half + mask, place.device(place.sibling)
        return remote(
            self.at(mask), self.full(place.block(mask)), self.send(label), self.recv(label), device
        )

    def arrival(self, label):
        place = self.place
        if label < self.half:
            ref = self.full(place.block(label))
        else:
            ref = self.full(place.sibling_block(label - self.half))
        return remote(ref, ref, self.send(label), self.recv(label), place.device(place.sibling))

    def sends(self, mask):
        return [self.copy(mask, step) for step in range(mask.bit_length(), self.place.steps + 1)]

    def start(self):
        for copy in self.sends(0):
            copy.start()

    def hand_on(self, mask):
        self.arrival(mask).wait_recv()
        for copy in self.sends(mask):
            copy.start()

    def spread(self):
        for mask in range(1, self.half):
            self.hand_on(mask)

    def complete(self):
        for mask in range(self.half):
            self.arrival(self.half + mask).wait_recv()

    def finish(self):
        for mask in range(self.half):
            for copy in self.sends(mask):
                copy.wait_send()


class LineGather:
    def __init__(self, place, own, full, send, recv, offsets=(1, -1)):
        self.place, self.own, self.full, self.send, self.recv = place, own, full, send, recv
        self.offsets = offsets

    def copy(self, distance, offset):
        place = self.place
        source = place.z - offset * distance
        side = 0 if offset > 0 else 1
        src = self.full(source) if distance else self.own
        return remote(
            src,
            self.full(source),
            self.send(side, distance),
            self.recv(side, distance),
            place.beside(offset),
        )

    def each(self, distance, act):
        place = self.place
        for offset in self.offsets:

            @pl.when(place.has(-offset * distance) & place.has(offset))
            def _():
                act(self.copy(distance, offset))

    def start(self):
        self.each(0, lambda copy: copy.start())

    def arrived(self, distance):
        place = self.place
        for offset in self.offsets:

            @pl.when(place.has(-offset * distance))
            def _():
                side = 0 if offset > 0 else 1
                ref = self.full(place.z - offset * distance)
                remote(
                    ref,
                    ref,
                    self.send(side, distance - 1),
                    self.recv(side, distance - 1),
                    place.beside(-offset),
                ).wait_recv()

    def hand_on(self, distance):
        self.arrived(distance)
        if distance < self.place.tp - 1:
            self.each(distance, lambda copy: copy.start())

    def finish(self):
        for distance in range(self.place.tp - 1):
            self.each(distance, lambda copy: copy.wait_send())


def turned(rows, cosine, sine):
    return rows * cosine + pltpu.roll(rows, rows.shape[1] // 2, 1) * sine


def forward_kernel(
    dp, tp, kvb_count, qb_count,
    x, seg_row, seg_col, zq, zo, zb, kvs, ff, cot,
    ff_out, cot_out, n2_out, wq_out, wo_out, wkv_out, p_out,
    res, att, n1, q, kv, cosine, sine, vectors,
    wq, wo, wkv, wb, spread, mask, probs, n2, n2_own,
    plane_send, plane_recv, line_send, line_recv, local_sem, probs_sem,
):
    place = Place(dp, tp)
    d, z = place.d, place.z
    own_rows, width = x.shape
    depth, columns = zq.shape
    items = seg_row.shape[1]
    head = HEAD_DIMENSION
    kv_columns = kv.shape[1]
    my_rows = pl.ds(pl.multiple_of(d * depth, 16), depth)

    def rows_of(b):
        return pl.ds(pl.multiple_of(b * depth, 16), depth)

    def plane(item, own, full):
        return PlaneGather(
            place, own, full, lambda m: plane_send.at[item, m], lambda m: plane_recv.at[item, m]
        )

    def line(item, own, full, offsets=(1, -1)):
        return LineGather(
            place,
            own,
            full,
            lambda s, k: line_send.at[item, s, k],
            lambda s, k: line_recv.at[item, s, k],
            offsets,
        )

    starts = [
        pltpu.make_async_copy(zq, wq.at[z, my_rows], local_sem.at[0]),
        pltpu.make_async_copy(zo, wo.at[z, my_rows], local_sem.at[1]),
        pltpu.make_async_copy(zb, wb.at[d, z], local_sem.at[2]),
        pltpu.make_async_copy(kvs, wkv.at[my_rows], local_sem.at[3]),
        pltpu.make_async_copy(ff, ff_out.at[d], local_sem.at[4]),
        pltpu.make_async_copy(cot, cot_out.at[z], local_sem.at[5]),
    ]
    for copy in starts:
        copy.start()
    place.greet(True, True)
    line_q = line(0, zq, lambda t: wq.at[t, my_rows])
    line_o = line(1, zo, lambda t: wo.at[t, my_rows])
    line_b = line(2, zb, lambda t: wb.at[d, t])
    line_cot = line(3, cot, lambda t: cot_out.at[t])
    line_kv = line(
        4,
        kv.at[pl.ds(pl.multiple_of(z * own_rows, 16), own_rows)],
        lambda t: kv.at[pl.ds(pl.multiple_of(t * own_rows, 16), own_rows)],
        (1,),
    )
    line_n2 = line(5, n2, lambda t: n2_out.at[t])
    plane_kv = plane(0, kvs, lambda b: wkv.at[rows_of(b)])
    plane_q = plane(1, wq.at[:, my_rows], lambda b: wq.at[:, rows_of(b)])
    plane_o = plane(2, wo.at[:, my_rows], lambda b: wo.at[:, rows_of(b)])
    plane_b = plane(3, wb.at[d], lambda b: wb.at[b])
    plane_ff = [
        plane(4 + part, ff.at[part], lambda b, part=part: ff_out.at[b, part]) for part in (2, 0, 1)
    ]
    line_b.start()
    line_q.start()
    plane_kv.start()
    plane_ff[0].start()

    begin = z * own_rows
    row_at = begin + lax.broadcasted_iota(jnp.int32, (own_rows, items), 0)
    col_at = lax.broadcasted_iota(jnp.int32, (own_rows, items), 1)
    mine, theirs = seg_col[...], seg_row[...]
    allowed = (mine == theirs) & (col_at <= row_at)
    mask[...] = jnp.where(allowed, 0.0, NEGATIVE)
    below = jnp.sum(jnp.where(theirs < mine, 1.0, 0.0), axis=1, keepdims=True)
    lane = lax.broadcasted_iota(jnp.int32, (own_rows, head), 1)
    half = lane % (head // 2)
    index = begin + lax.broadcasted_iota(jnp.int32, (own_rows, head), 0)
    freqs = jnp.exp(half.astype(F32) * (-2.0 * math.log(THETA) / head))
    angles = (index.astype(F32) - below) * freqs
    cosine[...] = jnp.cos(angles)
    sine[...] = jnp.sin(angles) * jnp.where(lane < head // 2, -1.0, 1.0)

    for distance in range(1, tp):
        line_b.hand_on(distance)
    line_q.hand_on(1)
    line_o.start()
    for distance in range(2, tp):
        line_q.hand_on(distance)
    starts[2].wait()
    starts[0].wait()
    plane_b.start()
    plane_q.start()
    plane_kv.spread()
    for distance in range(1, tp):
        line_o.hand_on(distance)
    starts[1].wait()
    plane_o.start()
    line_cot.start()
    starts[3].wait()
    plane_kv.complete()

    pick_row = lax.broadcasted_iota(jnp.int32, (16, 128), 0)
    pick_col = lax.broadcasted_iota(jnp.int32, (16, 128), 1)
    pick = jnp.where(pick_row == pick_col, 1.0, 0.0).astype(BF16)
    rows16 = dot_nt(pick, wkv[:, kv_columns:])
    vectors[...] = rows16
    block_row = lax.broadcasted_iota(jnp.int32, (depth, kv_columns), 0)
    block_col = lax.broadcasted_iota(jnp.int32, (depth, kv_columns), 1)
    for b in range(dp):
        hit = (block_row < kvb_count) & (block_col == block_row + b * kvb_count)
        spread[b * depth : (b + 1) * depth, :] = jnp.where(hit, 1.0, 0.0).astype(BF16)
    kv_bias = dot(rows16.astype(BF16), spread[...])[2:3, :]

    xs = x[...].astype(F32)
    n1[...] = (xs * rms_scale(xs) * rows16[0:1, :]).astype(BF16)
    kv_rows = dot(n1[...], wkv[:, :kv_columns]) + kv_bias
    at = pl.ds(pl.multiple_of(begin, 16), own_rows)
    for h in range(KEYVALUE_HEADS):
        cut = slice(h * head, (h + 1) * head)
        kv[at, cut] = turned(kv_rows[:, cut], cosine[...], sine[...]).astype(BF16)
    kv[at, KEYVALUE_HEADS * head :] = kv_rows[:, KEYVALUE_HEADS * head :].astype(BF16)
    line_kv.start()

    plane_b.spread()
    plane_q.spread()
    plane_b.complete()
    small_row = lax.broadcasted_iota(jnp.int32, (128, columns), 0)
    small_col = lax.broadcasted_iota(jnp.int32, (128, columns), 1)
    q_bias = jnp.zeros((tp * 16, columns), F32)
    for b in range(dp):
        hit = (small_row < qb_count) & (small_col == small_row + b * qb_count)
        one = jnp.where(hit, 1.0, 0.0).astype(BF16)
        q_bias = q_bias + dot(wb[b].reshape(tp * 16, 128), one)
    plane_ff[0].spread()
    plane_ff[1].start()
    line_kv.hand_on(1)
    line_cot.hand_on(1)
    plane_q.complete()
    for t in range(tp):
        rows = dot(n1[...], wq[t]) + q_bias[t * 16 : t * 16 + 1, :]
        for h in range(columns // head):
            cut = slice(h * head, (h + 1) * head)
            out = slice(t * columns + h * head, t * columns + (h + 1) * head)
            q[:, out] = turned(rows[:, cut], cosine[...], sine[...]).astype(BF16)
    line_kv.hand_on(2)
    plane_o.spread()
    for distance in range(3, tp):
        line_kv.hand_on(distance)
    line_cot.hand_on(2)
    outs = [
        pltpu.make_async_copy(wq, wq_out, local_sem.at[0]),
        pltpu.make_async_copy(wkv, wkv_out, local_sem.at[3]),
    ]
    for copy in outs:
        copy.start()

    scale = 1.0 / math.sqrt(head)
    group = QUERY_HEADS // tp

    def probs_copy(part, count):
        at = pl.ds(part * group, group)
        return pltpu.make_async_copy(
            probs.at[at, :, pl.ds(0, count)], p_out.at[at, :, pl.ds(0, count)], probs_sem.at[part]
        )

    for part in range(tp):
        for blocks in range(1, tp + 1):
            count = blocks * own_rows

            @pl.when(z == blocks - 1)
            def _():
                def one_head(i, carry):
                    h = part * group + i
                    at = pl.ds(pl.multiple_of(h * head, head), head)
                    shared = h // REPEAT
                    key_at = pl.ds(pl.multiple_of(shared * head, head), head)
                    value_at = pl.ds(pl.multiple_of((KEYVALUE_HEADS + shared) * head, head), head)
                    scores = dot_nt(q[:, at], kv[0:count, key_at]) * scale + mask[:, 0:count]
                    top = jnp.max(scores, axis=1, keepdims=True)
                    weights = jnp.exp(scores - top)
                    total = jnp.sum(weights, axis=1, keepdims=True)
                    low = (weights / total).astype(BF16)
                    probs[h, :, 0:count] = low
                    att[:, at] = dot(low, kv[0:count, value_at]).astype(BF16)
                    return carry

                lax.fori_loop(0, group, one_head, 0)
                probs_copy(part, count).start()

        if part == 0:
            plane_ff[1].spread()
            plane_ff[2].start()
    plane_o.complete()
    outs.append(pltpu.make_async_copy(wo, wo_out, local_sem.at[1]))
    outs[-1].start()
    for j in range(width // 512):
        cut = slice(j * 512, (j + 1) * 512)
        acc = x[:, cut].astype(F32)
        for t in range(tp):
            acc = acc + dot_nt(att[:, t * columns : (t + 1) * columns], wo[t, cut, :])
        res[:, cut] = acc
    residual = res[...]
    n2[...] = (residual * rms_scale(residual) * vectors[1:2, :]).astype(BF16)
    line_n2.start()
    n2_copy = pltpu.make_async_copy(n2, n2_out.at[z], local_sem.at[2])
    n2_copy.start()
    for distance in range(3, tp):
        line_cot.hand_on(distance)
    line_n2.hand_on(1)
    plane_ff[2].spread()
    for distance in range(2, tp):
        line_n2.hand_on(distance)
    for item in plane_ff:
        item.complete()
    for item in [plane_kv, plane_q, plane_o, plane_b] + plane_ff:
        item.finish()
    for item in (line_q, line_o, line_b, line_cot, line_kv, line_n2):
        item.finish()
    for copy in starts[4:] + outs + [n2_copy]:
        copy.wait()
    for part in range(tp):
        for blocks in range(1, tp + 1):

            @pl.when(z == blocks - 1)
            def _():
                probs_copy(part, blocks * own_rows).wait()


def forward_part(dp, tp, kvb_count, qb_count, x, seg_row, seg_col, zq, zo, zb, kvs, ff, cot):
    def shape(*dims, kind=BF16):
        return jax.ShapeDtypeStruct(dims, kind)

    own_rows, width = x.shape
    depth, columns = zq.shape
    items = seg_row.shape[1]
    head = HEAD_DIMENSION
    kv_columns = 2 * KEYVALUE_HEADS * head
    vmem = pl.BlockSpec(memory_space=pltpu.VMEM)
    anywhere = pl.BlockSpec(memory_space=ANY)
    return pl.pallas_call(
        functools.partial(forward_kernel, dp, tp, kvb_count, qb_count),
        out_shape=(
            shape(dp, *ff.shape),
            shape(tp, *cot.shape),
            shape(tp, own_rows, width),
            shape(tp, width, columns),
            shape(tp, width, columns),
            shape(width, kvs.shape[1]),
            shape(QUERY_HEADS, own_rows, items),
            shape(own_rows, width, kind=F32),
            shape(own_rows, tp * columns),
            shape(own_rows, width),
            shape(own_rows, tp * columns),
            shape(items, kv_columns),
            shape(own_rows, head, kind=F32),
            shape(own_rows, head, kind=F32),
            shape(16, width, kind=F32),
        ),
        in_specs=[vmem] * 7 + [anywhere] * 2,
        out_specs=(anywhere,) * 7 + (vmem,) * 8,
        scratch_shapes=[
            pltpu.VMEM((tp, width, columns), BF16),
            pltpu.VMEM((tp, width, columns), BF16),
            pltpu.VMEM((width, kvs.shape[1]), BF16),
            pltpu.VMEM((dp, tp, 16, 128), BF16),
            pltpu.VMEM((width, kv_columns), BF16),
            pltpu.VMEM((own_rows, items), F32),
            pltpu.VMEM((QUERY_HEADS, own_rows, items), BF16),
            pltpu.VMEM((own_rows, width), BF16),
            pltpu.VMEM((16, 128), BF16),
            pltpu.SemaphoreType.DMA((7, dp)),
            pltpu.SemaphoreType.DMA((7, dp)),
            pltpu.SemaphoreType.DMA((6, 2, tp)),
            pltpu.SemaphoreType.DMA((6, 2, tp)),
            pltpu.SemaphoreType.DMA((6,)),
            pltpu.SemaphoreType.DMA((tp,)),
        ],
        compiler_params=pltpu.CompilerParams(
            collective_id=0, has_side_effects=True, vmem_limit_bytes=56 << 20
        ),
        name="forward_part",
    )(x, seg_row, seg_col, zq, zo, zb, kvs, ff, cot)


class PlaneReduce:
    def __init__(self, place, part, held, send, recv):
        self.place, self.part, self.held, self.send, self.recv = place, part, held, send, recv
        self.half = 1 << place.steps
        self.last = place.steps

    def count(self, level):
        return self.half >> level

    def slot(self, level, i):
        return sum(self.count(k) for k in range(level)) + i

    def copy(self, level, i):
        place = self.place
        slot = self.slot(level, i)
        if level:
            src, device = self.held(self.slot(level - 1, 2 * i + 1)), place.partners[level - 1]
        else:
            src, device = self.part(place.sibling_block(i)), place.sibling
        return remote(
            src, self.held(slot), self.send(slot), self.recv(slot), place.device(device)
        )

    def start(self, level):
        for i in range(self.count(level)):
            self.copy(level, i).start()

    def wait_send(self, level):
        for i in range(self.count(level)):
            self.copy(level, i).wait_send()

    def absorb(self, level, out=None):
        order = sorted(range(self.count(level)), key=lambda i: 1 - i % 2)
        for i in order:
            slot = self.slot(level, i)
            self.copy(level, i).wait_recv()
            if level:
                other = self.held(self.slot(level - 1, 2 * i))
            else:
                other = self.part(self.place.block(i))
            add_into(self.held(slot), other, self.held(slot) if out is None else out)
            if i % 2:
                self.copy(level + 1, i // 2).start()


def add_into(one, other, out):
    rows = one.shape[0]
    step = 48 if rows % 48 == 0 else rows

    def body(k, carry):
        at = pl.ds(pl.multiple_of(k * step, 16), step)
        out[at, :] = (one[at, :].astype(F32) + other[at, :].astype(F32)).astype(out.dtype)
        return carry

    lax.fori_loop(0, rows // step, body, 0)


FF_PARTS = 3


class LineReduce:
    def __init__(self, place, term, sent, got, send, recv):
        self.place, self.term, self.sent, self.got = place, term, sent, got
        self.send, self.recv = send, recv

    def owner(self, turn):
        place = self.place
        if turn == place.tp - 1:
            return place.z
        falling = place.tp - 1 - turn
        falling = jnp.where(falling > place.z, falling, falling - 1)
        rising = jnp.where(turn < place.z, turn, turn + 1)
        return jnp.where(place.z < place.tp // 2, falling, rising)

    def way(self, turn):
        place = self.place
        owner = self.owner(turn)
        right = jnp.where(owner > place.z, 1, 0)
        side, offset = 1 - right, 2 * right - 1
        return side, offset, (owner - place.z) * offset

    def copy(self, turn):
        side, offset, distance = self.way(turn)
        return remote(
            self.sent(turn),
            self.got(side, distance - 1),
            self.send(turn),
            self.recv(side, distance - 1),
            self.place.beside(offset),
        )

    def arrival(self, side, distance):
        ref = self.got(side, distance)
        return remote(
            ref, ref, self.send(0), self.recv(side, distance), self.place.beside(0)
        )

    def step(self, turn):
        side, offset, distance = self.way(turn)
        fed = self.place.has(-offset)

        @pl.when(fed)
        def _():
            self.arrival(side, distance).wait_recv()
            add_into(self.term(turn), self.got(side, distance), self.sent(turn))

        if self.term is not self.sent:

            @pl.when(jnp.logical_not(fed))
            def _():
                copy_into(self.term(turn), self.sent(turn))

        self.copy(turn).start()

    def total(self, out):
        last = self.place.tp - 1
        copy_into(self.term(last), out)
        for side, offset in ((0, -1), (1, 1)):

            @pl.when(self.place.has(offset))
            def _():
                self.arrival(side, 0).wait_recv()
                add_into(out, self.got(side, 0), out)

    def finish(self):
        for turn in range(self.place.tp - 1):
            self.copy(turn).wait_send()


def copy_into(one, out):
    rows = one.shape[0]
    step = 32 if rows % 32 == 0 else rows

    def body(k, carry):
        at = pl.ds(pl.multiple_of(k * step, 16), step)
        out[at, :] = one[at, :].astype(out.dtype)
        return carry

    lax.fori_loop(0, rows // step, body, 0)


def ff_kernel(
    dp, tp, ff, cot, n2, act, lhs, mlp, d2,
    wg, wu, wd, x, ct, made, term, sent, got, branch, turned_rows,
    w_sem, in_sem, act_sem, lhs_sem, mlp_sem, send_sem, recv_sem,
):
    place = Place(dp, tp)
    own_rows, width = d2.shape
    depth = ff.shape[2]
    padded = ff.shape[3]
    tile = 256
    weights = (wg, wu, wd)
    loads = [
        [
            pltpu.make_async_copy(
                ff.at[b, p], weights[p].at[pl.ds(b * depth, depth)], w_sem.at[p, b]
            )
            for b in range(dp)
        ]
        for p in range(FF_PARTS)
    ]
    sums = LineReduce(
        place,
        lambda turn: term.at[turn % 2],
        lambda turn: sent.at[turn],
        lambda side, k: got.at[side, k],
        lambda turn: send_sem.at[turn],
        lambda side, k: recv_sem.at[side, k],
    )

    def fetch(turn):
        owner = sums.owner(turn)
        return [
            pltpu.make_async_copy(n2.at[owner], x.at[turn % 2], in_sem.at[turn % 2, 0]),
            pltpu.make_async_copy(cot.at[owner], ct.at[turn % 2], in_sem.at[turn % 2, 1]),
        ]

    def stores(turn, kinds=(0, 1, 2)):
        return [copies() for kind, copies in enumerate(store_kinds(turn)) if kind in kinds]

    def store_kinds(turn):
        owner = sums.owner(turn)
        at = pl.ds(pl.multiple_of(owner * own_rows, 128), own_rows)
        slot = turn % 2
        return (
            lambda: [
                pltpu.make_async_copy(made.at[slot, p], act.at[p, at], act_sem.at[slot, p])
                for p in range(FF_PARTS)
            ],
            lambda: [
                pltpu.make_async_copy(
                    turned_rows.at[slot, k], lhs.at[k, :, at], lhs_sem.at[slot, k]
                )
                for k in range(2)
            ],
            lambda: [pltpu.make_async_copy(branch.at[slot], mlp.at[owner], mlp_sem.at[slot])],
        )

    for copy in fetch(0):
        copy.start()
    for part in loads:
        for copy in part:
            copy.start()
    place.greet(False, True)
    for turn in range(tp):
        slot = turn % 2
        for copy in fetch(turn):
            copy.wait()
        if turn + 1 < tp:
            for copy in fetch(turn + 1):
                copy.start()
        if turn >= 2:
            for copies in stores(turn - 2):
                for copy in copies:
                    copy.wait()
        turned_rows[slot, 0] = x[slot].T
        turned_rows[slot, 1] = ct[slot].T
        for copy in stores(turn, (1,))[0]:
            copy.start()
        if turn == 0:
            for part in loads:
                for copy in part:
                    copy.wait()

        def units(n, carry, slot=slot):
            for k in range(3):
                at = pl.ds(pl.multiple_of((n * 3 + k) * tile, tile), tile)
                gate = dot(x[slot], wg[:, at])
                upper = dot(x[slot], wu[:, at])
                d_hidden = dot(ct[slot], wd[:, at])
                sigmoid = 1.0 / (1.0 + jnp.exp(-gate))
                swish = gate * sigmoid
                made[slot, 2, :, at] = (swish * upper).astype(BF16)
                made[slot, 1, :, at] = (d_hidden * swish).astype(BF16)
                made[slot, 0, :, at] = (
                    d_hidden * upper * sigmoid * (1.0 + gate * (1.0 - sigmoid))
                ).astype(BF16)
            return carry

        lax.fori_loop(0, padded // (3 * tile), units, 0)

        def columns(n, carry, slot=slot):
            at = pl.ds(pl.multiple_of(n * tile, tile), tile)
            term[slot, :, at] = dot_nt(made[slot, 0], wg[at, :]) + dot_nt(
                made[slot, 1], wu[at, :]
            )
            branch[slot, :, at] = dot_nt(made[slot, 2], wd[at, :]).astype(BF16)
            return carry

        if turn > 0:
            sums.step(turn - 1)
        lax.fori_loop(0, width // tile, columns, 0)
        for copies in stores(turn, (0, 2)):
            for copy in copies:
                copy.start()
    sums.total(d2)
    sums.finish()
    for turn in range(tp - 2, tp):
        for copies in stores(turn):
            for copy in copies:
                copy.wait()


def ff_part(dp, tp, ff, cot, n2):
    def shape(*dims, kind=BF16):
        return jax.ShapeDtypeStruct(dims, kind)

    own_rows, width = cot.shape[1:]
    padded = ff.shape[3]
    vmem = pl.BlockSpec(memory_space=pltpu.VMEM)
    anywhere = pl.BlockSpec(memory_space=ANY)
    return pl.pallas_call(
        functools.partial(ff_kernel, dp, tp),
        out_shape=(
            shape(FF_PARTS, tp * own_rows, padded),
            shape(2, width, tp * own_rows),
            shape(tp, own_rows, width),
            shape(own_rows, width, kind=F32),
        ),
        in_specs=[anywhere] * 3,
        out_specs=(anywhere,) * 3 + (vmem,),
        scratch_shapes=[
            pltpu.VMEM((width, padded), BF16),
            pltpu.VMEM((width, padded), BF16),
            pltpu.VMEM((width, padded), BF16),
            pltpu.VMEM((2, own_rows, width), BF16),
            pltpu.VMEM((2, own_rows, width), BF16),
            pltpu.VMEM((2, FF_PARTS, own_rows, padded), BF16),
            pltpu.VMEM((2, own_rows, width), F32),
            pltpu.VMEM((tp - 1, own_rows, width), BF16),
            pltpu.VMEM((2, tp - 1, own_rows, width), BF16),
            pltpu.VMEM((2, own_rows, width), BF16),
            pltpu.VMEM((2, 2, width, own_rows), BF16),
            pltpu.SemaphoreType.DMA((FF_PARTS, dp)),
            pltpu.SemaphoreType.DMA((2, 2)),
            pltpu.SemaphoreType.DMA((2, FF_PARTS)),
            pltpu.SemaphoreType.DMA((2, 2)),
            pltpu.SemaphoreType.DMA((2,)),
            pltpu.SemaphoreType.DMA((tp - 1,)),
            pltpu.SemaphoreType.DMA((2, tp - 1)),
        ],
        compiler_params=pltpu.CompilerParams(
            collective_id=3, has_side_effects=True, vmem_limit_bytes=60 << 20
        ),
        name="ff_part",
    )(ff, cot, n2)


def ff_grad_kernel(
    dp, tp, chunk, lhs, act, mlp, out, mlp_out,
    part, taken, held, terms, got, act_sem, send_sem, recv_sem, mlp_sem, line_send, line_recv,
):
    place = Place(dp, tp)
    depth = out.shape[1]
    group = max(1, 384 // depth)
    tile = 256
    per_part = act.shape[2] // chunk
    units = [(p, k) for p in range(FF_PARTS) for k in range(per_part)]

    def fetch(u):
        p, k = units[u]
        return pltpu.make_async_copy(
            act.at[p, :, pl.ds(k * chunk, chunk)], taken.at[u % 2], act_sem.at[u % 2]
        )

    fetch(0).start()
    terms_copy = pltpu.make_async_copy(mlp, terms, mlp_sem.at[0])
    terms_copy.start()
    place.greet(True, True)

    def own_terms(turn):
        return terms.at[line.owner(turn)]

    line = LineReduce(
        place,
        own_terms,
        own_terms,
        lambda side, k: got.at[side, k],
        lambda turn: line_send.at[turn],
        lambda side, k: line_recv.at[side, k],
    )
    sums = [
        PlaneReduce(
            place,
            lambda b, u=u: part.at[u % 2, b],
            lambda s, u=u: held.at[u, s],
            lambda s, u=u: send_sem.at[u, s],
            lambda s, u=u: recv_sem.at[u, s],
        )
        for u in range(len(units))
    ]
    last = place.steps
    for turn in range(len(units) + last + 1):
        if turn < len(units):
            u = turn
            p, k = units[u]
            if u + 1 < len(units):
                fetch(u + 1).start()
            fetch(u).wait()
            if u >= 2:
                sums[u - 2].wait_send(0)

            def body(n, carry, u=u, p=p):
                i, j = n // (chunk // tile), n % (chunk // tile)
                rows = pl.ds(pl.multiple_of(i * (group * depth), 16), group * depth)
                cols = pl.ds(pl.multiple_of(j * tile, tile), tile)
                found = dot(lhs[p // 2, rows, :], taken[u % 2, :, cols]).astype(BF16)
                for g in range(group):
                    part[u % 2, i * group + g, :, cols] = found[g * depth : (g + 1) * depth]
                return carry

            lax.fori_loop(0, dp // group * (chunk // tile), body, 0)
            sums[u].start(0)
        if turn == 0:
            terms_copy.wait()
        if turn % 2 == 0 and turn // 2 < tp - 1:
            line.step(turn // 2)
        for level in range(last + 1):
            u = turn - 1 - level
            if 0 <= u < len(units):
                p, k = units[u]
                sums[u].absorb(
                    level, out.at[p, :, pl.ds(k * chunk, chunk)] if level == last else None
                )
    line.total(mlp_out)
    line.finish()
    for u in range(len(units)):
        for level in range(0 if u >= len(units) - 2 else 1, last + 1):
            sums[u].wait_send(level)


def ff_grads(dp, tp, lhs, act, mlp):
    depth = lhs.shape[1] // dp
    items, columns = act.shape[1:]
    chunk = 768
    count = FF_PARTS * columns // chunk
    vmem = pl.BlockSpec(memory_space=pltpu.VMEM)
    return pl.pallas_call(
        functools.partial(ff_grad_kernel, dp, tp, chunk),
        out_shape=(
            jax.ShapeDtypeStruct((FF_PARTS, depth, columns), F32),
            jax.ShapeDtypeStruct(mlp.shape[1:], F32),
        ),
        in_specs=[vmem, pl.BlockSpec(memory_space=ANY), pl.BlockSpec(memory_space=ANY)],
        out_specs=(vmem, vmem),
        scratch_shapes=[
            pltpu.VMEM((2, dp, depth, chunk), BF16),
            pltpu.VMEM((2, items, chunk), BF16),
            pltpu.VMEM((count, dp - 1, depth, chunk), BF16),
            pltpu.VMEM(mlp.shape, BF16),
            pltpu.VMEM((2, tp - 1) + mlp.shape[1:], BF16),
            pltpu.SemaphoreType.DMA((2,)),
            pltpu.SemaphoreType.DMA((count, dp - 1)),
            pltpu.SemaphoreType.DMA((count, dp - 1)),
            pltpu.SemaphoreType.DMA((1,)),
            pltpu.SemaphoreType.DMA((tp - 1,)),
            pltpu.SemaphoreType.DMA((2, tp - 1)),
        ],
        compiler_params=pltpu.CompilerParams(
            collective_id=1, has_side_effects=True, vmem_limit_bytes=56 << 20
        ),
        name="ff_grads",
    )(lhs, act, mlp)


def attn_grad_kernel(
    dp, tp, widths, grads, kv_out, q_out, o_out,
    held, own, line_kv, line_qo, send_sem, recv_sem, line_send, line_recv,
):
    place = Place(dp, tp)
    z = place.z
    columns = q_out.shape[1]
    barrier = pltpu.get_barrier_semaphore()
    for partner in place.partners + [place.sibling]:
        pl.semaphore_signal(barrier, inc=1, device_id=place.device(partner), device_id_type=MESH)
    for t in range(tp):

        @pl.when(t != z)
        def _():
            pl.semaphore_signal(barrier, inc=1, device_id=(place.d, t), device_id_type=MESH)

    pl.semaphore_wait(barrier, place.steps + tp)
    starts = [sum(widths[:u]) for u in range(len(widths))]
    count = len(widths)
    sums = [
        PlaneReduce(
            place,
            lambda b, u=u: grads.at[b, :, pl.ds(starts[u], widths[u])],
            lambda s, u=u: held.at[u, s, :, pl.ds(0, widths[u])],
            lambda s, u=u: send_sem.at[u, s],
            lambda s, u=u: recv_sem.at[u, s],
        )
        for u in range(count)
    ]

    def line_copies(u):
        found = []
        for t in range(tp):
            if u == 0:
                src, dst = own.at[0, :, pl.ds(0, widths[0])], line_kv.at[z]
                found.append((t, remote(
                    src, dst, line_send.at[u, t], line_recv.at[u, z], (place.d, t)
                )))
            else:
                half, kind = (u - 1) % 2, (u - 1) // 2
                if t // 2 == half:
                    src = own.at[u, :, pl.ds((t % 2) * columns, columns)]
                    dst = line_qo.at[kind, z]
                    found.append((t, remote(
                        src, dst, line_send.at[u, t], line_recv.at[1 + kind, z], (place.d, t)
                    )))
        return found

    last = place.steps
    for u in range(count):
        sums[u].start(0)
    for turn in range(count + last):
        for level in range(last + 1):
            u = turn - level
            if 0 <= u < count:
                target = own.at[u, :, pl.ds(0, widths[u])] if level == last else None
                sums[u].absorb(level, target)
                if level == last:
                    for t, copy in line_copies(u):

                        @pl.when(t != z)
                        def _():
                            copy.start()

    def arrived(ref, kind):
        for t in range(tp):

            @pl.when(t != z)
            def _():
                remote(
                    ref.at[t], ref.at[t], line_send.at[0, t], line_recv.at[kind, t], (place.d, t)
                ).wait_recv()

    def total(ref, mine, out):
        acc = mine.astype(F32)
        for t in range(tp):
            acc = acc + jnp.where(t != z, ref[t].astype(F32), 0.0)
        out[...] = acc

    arrived(line_kv, 0)
    total(line_kv, own[0, :, : widths[0]], kv_out)
    for kind, out in ((0, q_out), (1, o_out)):
        arrived(line_qo.at[kind], 1 + kind)
        at = pl.ds(pl.multiple_of((z % 2) * columns, 128), columns)
        mine = own[1 + 2 * kind + z // 2, :, at]
        total(line_qo.at[kind], mine, out)
    for u in range(count):
        for level in range(last + 1):
            sums[u].wait_send(level)
        for t, copy in line_copies(u):

            @pl.when(t != z)
            def _():
                copy.wait_send()


def attn_grads(dp, tp, grads, side_width):
    depth, columns = grads.shape[1:]
    qo_width = (columns - side_width) // 4
    widths = (side_width,) + (qo_width,) * 4
    own_width = 2 * qo_width // tp
    vmem = pl.BlockSpec(memory_space=pltpu.VMEM)
    return pl.pallas_call(
        functools.partial(attn_grad_kernel, dp, tp, widths),
        out_shape=(
            jax.ShapeDtypeStruct((depth, side_width), F32),
            jax.ShapeDtypeStruct((depth, own_width), F32),
            jax.ShapeDtypeStruct((depth, own_width), F32),
        ),
        in_specs=[vmem],
        out_specs=(vmem,) * 3,
        scratch_shapes=[
            pltpu.VMEM((5, dp - 1, depth, qo_width), BF16),
            pltpu.VMEM((5, depth, qo_width), BF16),
            pltpu.VMEM((tp, depth, side_width), BF16),
            pltpu.VMEM((2, tp, depth, own_width), BF16),
            pltpu.SemaphoreType.DMA((5, dp - 1)),
            pltpu.SemaphoreType.DMA((5, dp - 1)),
            pltpu.SemaphoreType.DMA((5, tp)),
            pltpu.SemaphoreType.DMA((3, tp)),
        ],
        compiler_params=pltpu.CompilerParams(
            collective_id=2, has_side_effects=True, vmem_limit_bytes=56 << 20
        ),
        name="attn_grads",
    )(grads)


def local(
    inputs,
    segment_ids,
    first_gain,
    query_weight,
    query_bias,
    key_value_weight,
    key_value_bias,
    output_weight,
    second_gain,
    gateup_weight,
    down_weight,
    cotangent,
):
    dp = lax.axis_size("dp")
    tp = lax.axis_size("tensor")
    rank = lax.axis_index("tensor")
    width = inputs.shape[1]
    own_rows = inputs.shape[0]
    depth = query_weight.shape[0]
    columns = query_weight.shape[1]
    kv_columns = key_value_weight.shape[1]
    hidden_units = gateup_weight.shape[2]
    heads_width = columns * tp
    head = HEAD_DIMENSION
    scale = 1.0 / math.sqrt(head)

    padded = -(-hidden_units // 256) * 256
    ff_own = jnp.stack([gateup_weight[0], gateup_weight[1], down_weight.T])
    ff_own = jnp.pad(ff_own, ((0, 0), (0, 0), (0, padded - hidden_units)))
    qb_count, kvb_count = query_bias.shape[0], key_value_bias.shape[0]
    own_kvbias = jnp.pad(key_value_bias, (0, depth - kvb_count))
    side = jnp.pad(jnp.stack([first_gain, second_gain, own_kvbias], axis=1), ((0, 0), (0, 125)))
    own_segments = lax.dynamic_slice_in_dim(segment_ids, rank * own_rows, own_rows, 0)
    (
        ff_all, grad_rows, second_rows, wq, wo, wkv, probs_low,
        residual, attended, normed_own, rot_query, all_kv, cosine, sine, vectors,
    ) = forward_part(
        dp,
        tp,
        kvb_count,
        qb_count,
        inputs,
        segment_ids[None, :],
        own_segments[:, None],
        query_weight,
        output_weight.T,
        jnp.pad(query_bias[None, :], ((0, 15), (0, 128 - qb_count))),
        jnp.concatenate([key_value_weight, side], axis=1),
        ff_own,
        cotangent,
    )
    edge_q = heads_width
    half_kv = kv_columns // 2
    items = all_kv.shape[0]
    qkv_weight = jnp.concatenate(
        [wq.transpose(1, 0, 2).reshape(width, -1), wkv[:, :kv_columns]], axis=1
    )
    out_t_weight = wo.transpose(1, 0, 2).reshape(width, -1)
    gain_one, gain_two = vectors[0], vectors[1]
    own_inputs = inputs.astype(F32)
    cosine, sine = cosine[:, None, : head // 2], sine[:, None, head // 2 :]
    valid = jnp.arange(items)[:, None] < (rank + 1) * own_rows
    all_kv = jnp.where(valid, all_kv, 0).reshape(items, 2, KEYVALUE_HEADS, head)
    keys, value_rows = all_kv[:, 0], all_kv[:, 1]
    grouped = rot_query.reshape(own_rows, KEYVALUE_HEADS, REPEAT, head)
    probs_low = jnp.where(valid.T[None], probs_low, 0)
    probs_low = probs_low.reshape(KEYVALUE_HEADS, REPEAT, own_rows, items)
    probs = probs_low.astype(F32)

    act, lhs, mlp_terms, d_second = ff_part(dp, tp, ff_all, grad_rows, second_rows)
    ff_sh, mlp_own = ff_grads(dp, tp, lhs, act, mlp_terms)
    output = (residual + mlp_own).astype(BF16)

    residual_part, gain_two_grad = norm_back(residual, gain_two, d_second)
    d_residual = cotangent.astype(F32) + residual_part
    d_branch = d_residual.astype(BF16)
    d_attended = dot(d_branch, out_t_weight).astype(BF16)
    d_att = d_attended.reshape(own_rows, KEYVALUE_HEADS, REPEAT, head)
    d_probs = jnp.einsum("qgrd,kgd->grqk", d_att, value_rows, preferred_element_type=F32)
    inner = jnp.sum(probs * d_probs, axis=-1, keepdims=True)
    d_scores = (scale * probs * (d_probs - inner)).astype(BF16)
    d_rot_query = jnp.einsum("grqk,kgd->qgrd", d_scores, keys, preferred_element_type=F32)
    d_keys = jnp.einsum("grqk,qgrd->kgd", d_scores, grouped, preferred_element_type=F32)
    d_values = jnp.einsum("grqk,qgrd->kgd", probs_low, d_att, preferred_element_type=F32)
    d_kv = lax.psum_scatter(
        jnp.concatenate([d_keys.reshape(items, -1), d_values.reshape(items, -1)], axis=1).astype(
            BF16
        ),
        "tensor",
        scatter_dimension=0,
        tiled=True,
    ).astype(F32)
    d_rot = jnp.concatenate(
        [
            d_rot_query.reshape(own_rows, QUERY_HEADS, head),
            d_kv[:, :half_kv].reshape(own_rows, KEYVALUE_HEADS, head),
        ],
        axis=1,
    )
    d_rot = unrotate(d_rot, cosine, sine).reshape(own_rows, -1)
    d_qkv = jnp.concatenate([d_rot, d_kv[:, half_kv:]], axis=1).astype(BF16)
    d_normed = dot_nt(d_qkv, qkv_weight)
    bias_grad = jnp.sum(d_qkv.astype(F32), axis=0)
    input_part, gain_one_grad = norm_back(own_inputs, gain_one, d_normed)
    input_grad = (d_residual + input_part).astype(BF16)

    qkv_grad = dot_tn(normed_own, d_qkv)
    out_grad = dot_tn(d_branch, attended)
    qb = bias_grad[:edge_q].reshape(tp, dp, -1).transpose(1, 0, 2).reshape(-1)
    kvb = jnp.pad(bias_grad[edge_q:].reshape(dp, -1), ((0, 0), (0, depth - kv_columns // dp)))
    side_grad = jnp.stack([gain_one_grad, gain_two_grad, qb, kvb.reshape(-1)], axis=1)
    side_grad = jnp.pad(side_grad, ((0, 0), (0, 124)))
    attn_grad = jnp.concatenate(
        [qkv_grad[:, edge_q:], side_grad, qkv_grad[:, :edge_q], out_grad], axis=1
    ).astype(BF16)
    rest, q_sh, o_sh = attn_grads(
        dp, tp, attn_grad.reshape(dp, depth, -1), kv_columns + side_grad.shape[1]
    )
    side_sh = rest[:, kv_columns : kv_columns + 4].T
    return (
        output,
        input_grad,
        side_sh[0],
        q_sh,
        lax.dynamic_slice_in_dim(side_sh[2], rank * qb_count, qb_count, 0),
        rest[:, :kv_columns],
        side_sh[3][: kv_columns // dp],
        o_sh.T,
        side_sh[1],
        ff_sh[:2, :, :hidden_units],
        ff_sh[2, :, :hidden_units].T,
    )


def solution(mesh):
    in_specs = (
        P(("dp", "tensor"), None),
        P("dp"),
        P("dp"),
        P("dp", "tensor"),
        P(("tensor", "dp")),
        P("dp", None),
        P("dp"),
        P("tensor", "dp"),
        P("dp"),
        P(None, "dp", "tensor"),
        P("tensor", "dp"),
        P(("dp", "tensor"), None),
    )
    out_specs = (
        P(("dp", "tensor"), None),
        P(("dp", "tensor"), None),
        P("dp"),
        P("dp", "tensor"),
        P(("tensor", "dp")),
        P("dp", None),
        P("dp"),
        P("tensor", "dp"),
        P("dp"),
        P(None, "dp", "tensor"),
        P("tensor", "dp"),
    )
    return jax.shard_map(local, mesh=mesh, in_specs=in_specs, out_specs=out_specs, check_vma=False)
```

```python
import functools
import math

import jax
import jax.numpy as jnp
from jax import lax
from jax.experimental import pallas as pl
from jax.experimental.pallas import tpu as pltpu
from jax.sharding import PartitionSpec as P

QUERY_HEADS = 12
KEYVALUE_HEADS = 2
HEAD_DIMENSION = 128
REPEAT = QUERY_HEADS // KEYVALUE_HEADS

EPSILON = 1e-06
THETA = 1000000.0
NEGATIVE = -1e30

F32 = jnp.float32
BF16 = jnp.bfloat16


def rms_scale(rows):
    return lax.rsqrt(jnp.mean(rows * rows, axis=-1, keepdims=True) + EPSILON)


def norm_back(rows, gain, grad):
    scale = rms_scale(rows)
    normed = rows * scale
    weighted = grad * gain
    inner = jnp.mean(weighted * normed, axis=-1, keepdims=True)
    return (scale * (weighted - normed * inner), jnp.sum(grad * normed, axis=0))


def rope_tables(segments, head_extent):
    index = jnp.arange(segments.shape[0], dtype=jnp.int32)
    starts = jnp.concatenate([jnp.ones((1,), dtype=bool), segments[1:] != segments[:-1]])
    first = lax.cummax(jnp.where(starts, index, jnp.zeros_like(index)), axis=0)
    placed = (index - first).astype(F32)
    freqs = jnp.exp(
        jnp.arange(head_extent // 2, dtype=F32) * (-2.0 * math.log(THETA) / head_extent)
    )
    return placed, freqs


def apply_rotation(value_rows, cosine_table, sine_table):
    half = value_rows.shape[-1] // 2
    former = value_rows[..., :half]
    latter = value_rows[..., half:]
    return jnp.concatenate(
        [former * cosine_table - latter * sine_table, latter * cosine_table + former * sine_table],
        axis=-1,
    )


def unrotate(grads, cosine_table, sine_table):
    return apply_rotation(grads, cosine_table, -sine_table)


def dot(left, right):
    return jnp.dot(left, right, preferred_element_type=F32)


def dot_nt(left, right):
    return lax.dot_general(left, right, (((1,), (1,)), ((), ())), preferred_element_type=F32)


def dot_tn(left, right):
    return lax.dot_general(left, right, (((0,), (0,)), ((), ())), preferred_element_type=F32)


MESH = pl.DeviceIdType.MESH
ANY = pl.ANY


def flip(index, bit):
    return index + (1 << bit) * (1 - 2 * ((index // (1 << bit)) % 2))


class Place:
    def __init__(self, dp, tp):
        self.dp, self.tp = dp, tp
        self.d, self.z = lax.axis_index("dp"), lax.axis_index("tensor")
        self.steps = dp.bit_length() - 2
        odd = self.d % 2
        self.partners = []
        for step in range(self.steps):
            first, other = flip(self.d, 1 + step), flip(self.d, self.steps - step)
            self.partners.append(first + odd * (other - first))
        self.sibling = flip(self.d, 0)
        self.deltas = [partner - self.d for partner in self.partners]

    def block(self, mask):
        index = self.d
        for step in range(self.steps):
            if (mask >> step) & 1:
                index = index + self.deltas[step]
        return index

    def sibling_block(self, mask):
        index = self.sibling
        for step in range(self.steps):
            if (mask >> step) & 1:
                index = index + self.deltas[self.steps - 1 - step]
        return index

    def device(self, index):
        return (index, self.z)

    def beside(self, offset):
        return (self.d, self.z + offset)

    def greet(self, plane, line):
        barrier = pltpu.get_barrier_semaphore()
        count = 0
        if plane:
            for partner in self.partners + [self.sibling]:
                pl.semaphore_signal(
                    barrier, inc=1, device_id=self.device(partner), device_id_type=MESH
                )
            count = self.steps + 1
        if line:
            for offset in (-1, 1):

                @pl.when(self.has(offset))
                def _():
                    pl.semaphore_signal(
                        barrier, inc=1, device_id=self.beside(offset), device_id_type=MESH
                    )

            count = count + jnp.where(self.z > 0, 1, 0) + jnp.where(self.z < self.tp - 1, 1, 0)
        pl.semaphore_wait(barrier, count)

    def has(self, offset):
        return (self.z + offset >= 0) & (self.z + offset < self.tp)


def remote(src, dst, send, recv, device):
    return pltpu.make_async_remote_copy(
        src_ref=src, dst_ref=dst, send_sem=send, recv_sem=recv, device_id=device, device_id_type=MESH
    )


class PlaneGather:
    def __init__(self, place, own, full, send, recv):
        self.place, self.own, self.full, self.send, self.recv = place, own, full, send, recv
        self.half = 1 << place.steps

    def at(self, mask):
        return self.full(self.place.block(mask)) if mask else self.own

    def copy(self, mask, step):
        place = self.place
        if step < place.steps:
            label, device = mask | (1 << step), place.device(place.partners[step])
        else:
            label, device = self.half + mask, place.device(place.sibling)
        return remote(
            self.at(mask), self.full(place.block(mask)), self.send(label), self.recv(label), device
        )

    def arrival(self, label):
        place = self.place
        if label < self.half:
            ref = self.full(place.block(label))
        else:
            ref = self.full(place.sibling_block(label - self.half))
        return remote(ref, ref, self.send(label), self.recv(label), place.device(place.sibling))

    def sends(self, mask):
        return [self.copy(mask, step) for step in range(mask.bit_length(), self.place.steps + 1)]

    def start(self):
        for copy in self.sends(0):
            copy.start()

    def hand_on(self, mask):
        self.arrival(mask).wait_recv()
        for copy in self.sends(mask):
            copy.start()

    def spread(self):
        for mask in range(1, self.half):
            self.hand_on(mask)

    def complete(self):
        for mask in range(self.half):
            self.arrival(self.half + mask).wait_recv()

    def finish(self):
        for mask in range(self.half):
            for copy in self.sends(mask):
                copy.wait_send()


class LineGather:
    def __init__(self, place, own, full, send, recv, offsets=(1, -1)):
        self.place, self.own, self.full, self.send, self.recv = place, own, full, send, recv
        self.offsets = offsets

    def copy(self, distance, offset):
        place = self.place
        source = place.z - offset * distance
        side = 0 if offset > 0 else 1
        src = self.full(source) if distance else self.own
        return remote(
            src,
            self.full(source),
            self.send(side, distance),
            self.recv(side, distance),
            place.beside(offset),
        )

    def each(self, distance, act):
        place = self.place
        for offset in self.offsets:

            @pl.when(place.has(-offset * distance) & place.has(offset))
            def _():
                act(self.copy(distance, offset))

    def start(self):
        self.each(0, lambda copy: copy.start())

    def arrived(self, distance):
        place = self.place
        for offset in self.offsets:

            @pl.when(place.has(-offset * distance))
            def _():
                side = 0 if offset > 0 else 1
                ref = self.full(place.z - offset * distance)
                remote(
                    ref,
                    ref,
                    self.send(side, distance - 1),
                    self.recv(side, distance - 1),
                    place.beside(-offset),
                ).wait_recv()

    def hand_on(self, distance):
        self.arrived(distance)
        if distance < self.place.tp - 1:
            self.each(distance, lambda copy: copy.start())

    def finish(self):
        for distance in range(self.place.tp - 1):
            self.each(distance, lambda copy: copy.wait_send())


def turned(rows, cosine, sine):
    return rows * cosine + pltpu.roll(rows, rows.shape[1] // 2, 1) * sine


def forward_kernel(
    dp, tp, kvb_count, qb_count,
    x, seg_row, seg_col, zq, zo, zb, kvs, ff, cot,
    ff_out, cot_out, n2_out, wq_out, wo_out, wkv_out, p_out,
    res, att, n1, q, kv, cosine, sine, vectors,
    wq, wo, wkv, wb, spread, mask, probs, n2,
    plane_send, plane_recv, line_send, line_recv, local_sem, probs_sem,
):
    place = Place(dp, tp)
    d, z = place.d, place.z
    own_rows, width = x.shape
    depth, columns = zq.shape
    items = seg_row.shape[1]
    head = HEAD_DIMENSION
    kv_columns = kv.shape[1]
    my_rows = pl.ds(pl.multiple_of(d * depth, 16), depth)

    def rows_of(b):
        return pl.ds(pl.multiple_of(b * depth, 16), depth)

    def plane(item, own, full):
        return PlaneGather(
            place, own, full, lambda m: plane_send.at[item, m], lambda m: plane_recv.at[item, m]
        )

    def line(item, own, full, offsets=(1, -1)):
        return LineGather(
            place,
            own,
            full,
            lambda s, k: line_send.at[item, s, k],
            lambda s, k: line_recv.at[item, s, k],
            offsets,
        )

    starts = [
        pltpu.make_async_copy(zq, wq.at[z, my_rows], local_sem.at[0]),
        pltpu.make_async_copy(zo, wo.at[z, my_rows], local_sem.at[1]),
        pltpu.make_async_copy(zb, wb.at[d, z], local_sem.at[2]),
        pltpu.make_async_copy(kvs, wkv.at[my_rows], local_sem.at[3]),
        pltpu.make_async_copy(ff, ff_out.at[d], local_sem.at[4]),
        pltpu.make_async_copy(cot, cot_out.at[z], local_sem.at[5]),
    ]
    for copy in starts:
        copy.start()
    place.greet(True, True)
    line_q = line(0, zq, lambda t: wq.at[t, my_rows])
    line_o = line(1, zo, lambda t: wo.at[t, my_rows])
    line_b = line(2, zb, lambda t: wb.at[d, t])
    line_cot = line(3, cot, lambda t: cot_out.at[t])
    line_kv = line(
        4,
        kv.at[pl.ds(pl.multiple_of(z * own_rows, 16), own_rows)],
        lambda t: kv.at[pl.ds(pl.multiple_of(t * own_rows, 16), own_rows)],
        (1,),
    )
    line_n2 = line(5, n2, lambda t: n2_out.at[t])
    plane_kv = plane(0, kvs, lambda b: wkv.at[rows_of(b)])
    plane_q = plane(1, wq.at[:, my_rows], lambda b: wq.at[:, rows_of(b)])
    plane_o = plane(2, wo.at[:, my_rows], lambda b: wo.at[:, rows_of(b)])
    plane_b = plane(3, wb.at[d], lambda b: wb.at[b])
    plane_ff = [
        plane(4 + part, ff.at[part], lambda b, part=part: ff_out.at[b, part]) for part in (2, 0, 1)
    ]
    line_b.start()
    line_q.start()
    plane_kv.start()
    plane_ff[0].start()

    begin = z * own_rows
    row_at = begin + lax.broadcasted_iota(jnp.int32, (own_rows, items), 0)
    col_at = lax.broadcasted_iota(jnp.int32, (own_rows, items), 1)
    mine, theirs = seg_col[...], seg_row[...]
    allowed = (mine == theirs) & (col_at <= row_at)
    mask[...] = jnp.where(allowed, 0.0, NEGATIVE)
    below = jnp.sum(jnp.where(theirs < mine, 1.0, 0.0), axis=1, keepdims=True)
    lane = lax.broadcasted_iota(jnp.int32, (own_rows, head), 1)
    half = lane % (head // 2)
    index = begin + lax.broadcasted_iota(jnp.int32, (own_rows, head), 0)
    freqs = jnp.exp(half.astype(F32) * (-2.0 * math.log(THETA) / head))
    angles = (index.astype(F32) - below) * freqs
    cosine[...] = jnp.cos(angles)
    sine[...] = jnp.sin(angles) * jnp.where(lane < head // 2, -1.0, 1.0)

    for distance in range(1, tp):
        line_b.hand_on(distance)
    line_q.hand_on(1)
    line_o.start()
    for distance in range(2, tp):
        line_q.hand_on(distance)
    starts[2].wait()
    starts[0].wait()
    plane_b.start()
    plane_q.start()
    plane_kv.spread()
    for distance in range(1, tp):
        line_o.hand_on(distance)
    starts[1].wait()
    plane_o.start()
    line_cot.start()
    starts[3].wait()
    plane_kv.complete()

    pick_row = lax.broadcasted_iota(jnp.int32, (16, 128), 0)
    pick_col = lax.broadcasted_iota(jnp.int32, (16, 128), 1)
    pick = jnp.where(pick_row == pick_col, 1.0, 0.0).astype(BF16)
    vector_rows = dot_nt(pick, wkv[:, kv_columns:])
    vectors[...] = vector_rows
    block_row = lax.broadcasted_iota(jnp.int32, (depth, kv_columns), 0)
    block_col = lax.broadcasted_iota(jnp.int32, (depth, kv_columns), 1)
    for b in range(dp):
        hit = (block_row < kvb_count) & (block_col == block_row + b * kvb_count)
        spread[b * depth : (b + 1) * depth, :] = jnp.where(hit, 1.0, 0.0).astype(BF16)
    kv_bias = dot(vector_rows.astype(BF16), spread[...])[2:3, :]

    xs = x[...].astype(F32)
    n1[...] = (xs * rms_scale(xs) * vector_rows[0:1, :]).astype(BF16)
    kv_rows = dot(n1[...], wkv[:, :kv_columns]) + kv_bias
    at = pl.ds(pl.multiple_of(begin, 16), own_rows)
    for h in range(KEYVALUE_HEADS):
        cut = slice(h * head, (h + 1) * head)
        kv[at, cut] = turned(kv_rows[:, cut], cosine[...], sine[...]).astype(BF16)
    kv[at, KEYVALUE_HEADS * head :] = kv_rows[:, KEYVALUE_HEADS * head :].astype(BF16)
    line_kv.start()

    plane_b.spread()
    plane_q.spread()
    plane_b.complete()
    small_row = lax.broadcasted_iota(jnp.int32, (128, columns), 0)
    small_col = lax.broadcasted_iota(jnp.int32, (128, columns), 1)
    q_bias = jnp.zeros((tp * 16, columns), F32)
    for b in range(dp):
        hit = (small_row < qb_count) & (small_col == small_row + b * qb_count)
        one = jnp.where(hit, 1.0, 0.0).astype(BF16)
        q_bias = q_bias + dot(wb[b].reshape(tp * 16, 128), one)
    plane_ff[0].spread()
    plane_ff[1].start()
    line_kv.hand_on(1)
    line_cot.hand_on(1)
    plane_q.complete()
    for t in range(tp):
        rows = dot(n1[...], wq[t]) + q_bias[t * 16 : t * 16 + 1, :]
        for h in range(columns // head):
            cut = slice(h * head, (h + 1) * head)
            out = slice(t * columns + h * head, t * columns + (h + 1) * head)
            q[:, out] = turned(rows[:, cut], cosine[...], sine[...]).astype(BF16)
    line_kv.hand_on(2)
    plane_o.spread()
    for distance in range(3, tp):
        line_kv.hand_on(distance)
    line_cot.hand_on(2)
    outs = [
        pltpu.make_async_copy(wq, wq_out, local_sem.at[0]),
        pltpu.make_async_copy(wkv, wkv_out, local_sem.at[3]),
    ]
    for copy in outs:
        copy.start()

    scale = 1.0 / math.sqrt(head)
    group = QUERY_HEADS // tp

    def probs_copy(part, count):
        at = pl.ds(part * group, group)
        return pltpu.make_async_copy(
            probs.at[at, :, pl.ds(0, count)], p_out.at[at, :, pl.ds(0, count)], probs_sem.at[part]
        )

    for part in range(tp):
        for blocks in range(1, tp + 1):
            count = blocks * own_rows

            @pl.when(z == blocks - 1)
            def _():
                def one_head(i, carry):
                    h = part * group + i
                    at = pl.ds(pl.multiple_of(h * head, head), head)
                    shared = h // REPEAT
                    key_at = pl.ds(pl.multiple_of(shared * head, head), head)
                    value_at = pl.ds(pl.multiple_of((KEYVALUE_HEADS + shared) * head, head), head)
                    scores = dot_nt(q[:, at], kv[0:count, key_at]) * scale + mask[:, 0:count]
                    top = jnp.max(scores, axis=1, keepdims=True)
                    weights = jnp.exp(scores - top)
                    total = jnp.sum(weights, axis=1, keepdims=True)
                    low = (weights / total).astype(BF16)
                    probs[h, :, 0:count] = low
                    att[:, at] = dot(low, kv[0:count, value_at]).astype(BF16)
                    return carry

                lax.fori_loop(0, group, one_head, 0)
                probs_copy(part, count).start()

        if part == 0:
            plane_ff[1].spread()
            plane_ff[2].start()
    plane_o.complete()
    outs.append(pltpu.make_async_copy(wo, wo_out, local_sem.at[1]))
    outs[-1].start()
    for j in range(width // 512):
        cut = slice(j * 512, (j + 1) * 512)
        acc = x[:, cut].astype(F32)
        for t in range(tp):
            acc = acc + dot_nt(att[:, t * columns : (t + 1) * columns], wo[t, cut, :])
        res[:, cut] = acc
    residual = res[...]
    n2[...] = (residual * rms_scale(residual) * vectors[1:2, :]).astype(BF16)
    line_n2.start()
    n2_copy = pltpu.make_async_copy(n2, n2_out.at[z], local_sem.at[2])
    n2_copy.start()
    for distance in range(3, tp):
        line_cot.hand_on(distance)
    line_n2.hand_on(1)
    plane_ff[2].spread()
    for distance in range(2, tp):
        line_n2.hand_on(distance)
    for item in plane_ff:
        item.complete()
    for item in [plane_kv, plane_q, plane_o, plane_b] + plane_ff:
        item.finish()
    for item in (line_q, line_o, line_b, line_cot, line_kv, line_n2):
        item.finish()
    for copy in starts[4:] + outs + [n2_copy]:
        copy.wait()
    for part in range(tp):
        for blocks in range(1, tp + 1):

            @pl.when(z == blocks - 1)
            def _():
                probs_copy(part, blocks * own_rows).wait()


def forward_part(dp, tp, kvb_count, qb_count, x, seg_row, seg_col, zq, zo, zb, kvs, ff, cot):
    def shape(*dims, kind=BF16):
        return jax.ShapeDtypeStruct(dims, kind)

    own_rows, width = x.shape
    depth, columns = zq.shape
    items = seg_row.shape[1]
    head = HEAD_DIMENSION
    kv_columns = 2 * KEYVALUE_HEADS * head
    vmem = pl.BlockSpec(memory_space=pltpu.VMEM)
    anywhere = pl.BlockSpec(memory_space=ANY)
    return pl.pallas_call(
        functools.partial(forward_kernel, dp, tp, kvb_count, qb_count),
        out_shape=(
            shape(dp, *ff.shape),
            shape(tp, *cot.shape),
            shape(tp, own_rows, width),
            shape(tp, width, columns),
            shape(tp, width, columns),
            shape(width, kvs.shape[1]),
            shape(QUERY_HEADS, own_rows, items),
            shape(own_rows, width, kind=F32),
            shape(own_rows, tp * columns),
            shape(own_rows, width),
            shape(own_rows, tp * columns),
            shape(items, kv_columns),
            shape(own_rows, head, kind=F32),
            shape(own_rows, head, kind=F32),
            shape(16, width, kind=F32),
        ),
        in_specs=[vmem] * 7 + [anywhere] * 2,
        out_specs=(anywhere,) * 7 + (vmem,) * 8,
        scratch_shapes=[
            pltpu.VMEM((tp, width, columns), BF16),
            pltpu.VMEM((tp, width, columns), BF16),
            pltpu.VMEM((width, kvs.shape[1]), BF16),
            pltpu.VMEM((dp, tp, 16, 128), BF16),
            pltpu.VMEM((width, kv_columns), BF16),
            pltpu.VMEM((own_rows, items), F32),
            pltpu.VMEM((QUERY_HEADS, own_rows, items), BF16),
            pltpu.VMEM((own_rows, width), BF16),
            pltpu.SemaphoreType.DMA((7, dp)),
            pltpu.SemaphoreType.DMA((7, dp)),
            pltpu.SemaphoreType.DMA((6, 2, tp)),
            pltpu.SemaphoreType.DMA((6, 2, tp)),
            pltpu.SemaphoreType.DMA((6,)),
            pltpu.SemaphoreType.DMA((tp,)),
        ],
        compiler_params=pltpu.CompilerParams(
            collective_id=0, has_side_effects=True, vmem_limit_bytes=56 << 20
        ),
        name="forward_part",
    )(x, seg_row, seg_col, zq, zo, zb, kvs, ff, cot)


class PlaneReduce:
    def __init__(self, place, part, held, send, recv):
        self.place, self.part, self.held, self.send, self.recv = place, part, held, send, recv
        self.half = 1 << place.steps
        self.last = place.steps

    def count(self, level):
        return self.half >> level

    def slot(self, level, i):
        return sum(self.count(k) for k in range(level)) + i

    def copy(self, level, i):
        place = self.place
        slot = self.slot(level, i)
        if level:
            src, device = self.held(self.slot(level - 1, 2 * i + 1)), place.partners[level - 1]
        else:
            src, device = self.part(place.sibling_block(i)), place.sibling
        return remote(
            src, self.held(slot), self.send(slot), self.recv(slot), place.device(device)
        )

    def start(self, level):
        for i in range(self.count(level)):
            self.copy(level, i).start()

    def wait_send(self, level):
        for i in range(self.count(level)):
            self.copy(level, i).wait_send()

    def absorb(self, level, out=None):
        order = sorted(range(self.count(level)), key=lambda i: 1 - i % 2)
        for i in order:
            slot = self.slot(level, i)
            self.copy(level, i).wait_recv()
            if level:
                other = self.held(self.slot(level - 1, 2 * i))
            else:
                other = self.part(self.place.block(i))
            add_into(self.held(slot), other, self.held(slot) if out is None else out)
            if i % 2:
                self.copy(level + 1, i // 2).start()


def add_into(one, other, out):
    rows = one.shape[0]
    step = 48 if rows % 48 == 0 else rows

    def body(k, carry):
        at = pl.ds(pl.multiple_of(k * step, 16), step)
        out[at, :] = (one[at, :].astype(F32) + other[at, :].astype(F32)).astype(out.dtype)
        return carry

    lax.fori_loop(0, rows // step, body, 0)


FF_PARTS = 3


class LineReduce:
    def __init__(self, place, term, sent, got, send, recv):
        self.place, self.term, self.sent, self.got = place, term, sent, got
        self.send, self.recv = send, recv

    def owner(self, turn):
        place = self.place
        if turn == place.tp - 1:
            return place.z
        falling = place.tp - 1 - turn
        falling = jnp.where(falling > place.z, falling, falling - 1)
        rising = jnp.where(turn < place.z, turn, turn + 1)
        return jnp.where(place.z < place.tp // 2, falling, rising)

    def way(self, turn):
        place = self.place
        owner = self.owner(turn)
        right = jnp.where(owner > place.z, 1, 0)
        side, offset = 1 - right, 2 * right - 1
        return side, offset, (owner - place.z) * offset

    def copy(self, turn):
        side, offset, distance = self.way(turn)
        return remote(
            self.sent(turn),
            self.got(side, distance - 1),
            self.send(turn),
            self.recv(side, distance - 1),
            self.place.beside(offset),
        )

    def arrival(self, side, distance):
        ref = self.got(side, distance)
        return remote(
            ref, ref, self.send(0), self.recv(side, distance), self.place.beside(0)
        )

    def step(self, turn):
        side, offset, distance = self.way(turn)
        fed = self.place.has(-offset)

        @pl.when(fed)
        def _():
            self.arrival(side, distance).wait_recv()
            add_into(self.term(turn), self.got(side, distance), self.sent(turn))

        if self.term is not self.sent:

            @pl.when(jnp.logical_not(fed))
            def _():
                copy_into(self.term(turn), self.sent(turn))

        self.copy(turn).start()

    def total(self, out):
        last = self.place.tp - 1
        copy_into(self.term(last), out)
        for side, offset in ((0, -1), (1, 1)):

            @pl.when(self.place.has(offset))
            def _():
                self.arrival(side, 0).wait_recv()
                add_into(out, self.got(side, 0), out)

    def finish(self):
        for turn in range(self.place.tp - 1):
            self.copy(turn).wait_send()


def copy_into(one, out):
    rows = one.shape[0]
    step = 32 if rows % 32 == 0 else rows

    def body(k, carry):
        at = pl.ds(pl.multiple_of(k * step, 16), step)
        out[at, :] = one[at, :].astype(out.dtype)
        return carry

    lax.fori_loop(0, rows // step, body, 0)


def ff_kernel(
    dp, tp, ff, cot, n2, act, lhs, mlp, d2,
    wg, wu, wd, x, ct, made, term, sent, got, branch, turned_rows,
    w_sem, in_sem, act_sem, lhs_sem, mlp_sem, send_sem, recv_sem,
):
    place = Place(dp, tp)
    own_rows, width = d2.shape
    depth = ff.shape[2]
    padded = ff.shape[3]
    tile = 256
    weights = (wg, wu, wd)
    loads = [
        [
            pltpu.make_async_copy(
                ff.at[b, p], weights[p].at[pl.ds(b * depth, depth)], w_sem.at[p, b]
            )
            for b in range(dp)
        ]
        for p in range(FF_PARTS)
    ]
    sums = LineReduce(
        place,
        lambda turn: term.at[turn % 2],
        lambda turn: sent.at[turn],
        lambda side, k: got.at[side, k],
        lambda turn: send_sem.at[turn],
        lambda side, k: recv_sem.at[side, k],
    )

    def fetch(turn):
        owner = sums.owner(turn)
        return [
            pltpu.make_async_copy(n2.at[owner], x.at[turn % 2], in_sem.at[turn % 2, 0]),
            pltpu.make_async_copy(cot.at[owner], ct.at[turn % 2], in_sem.at[turn % 2, 1]),
        ]

    def stores(turn, kinds=(0, 1, 2)):
        return [copies() for kind, copies in enumerate(store_kinds(turn)) if kind in kinds]

    def store_kinds(turn):
        owner = sums.owner(turn)
        at = pl.ds(pl.multiple_of(owner * own_rows, 128), own_rows)
        slot = turn % 2
        return (
            lambda: [
                pltpu.make_async_copy(made.at[slot, p], act.at[p, at], act_sem.at[slot, p])
                for p in range(FF_PARTS)
            ],
            lambda: [
                pltpu.make_async_copy(
                    turned_rows.at[slot, k], lhs.at[k, :, at], lhs_sem.at[slot, k]
                )
                for k in range(2)
            ],
            lambda: [pltpu.make_async_copy(branch.at[slot], mlp.at[owner], mlp_sem.at[slot])],
        )

    for copy in fetch(0):
        copy.start()
    for part in loads:
        for copy in part:
            copy.start()
    place.greet(False, True)
    for turn in range(tp):
        slot = turn % 2
        for copy in fetch(turn):
            copy.wait()
        if turn + 1 < tp:
            for copy in fetch(turn + 1):
                copy.start()
        if turn >= 2:
            for copies in stores(turn - 2):
                for copy in copies:
                    copy.wait()
        turned_rows[slot, 0] = x[slot].T
        turned_rows[slot, 1] = ct[slot].T
        for copy in stores(turn, (1,))[0]:
            copy.start()
        if turn == 0:
            for part in loads:
                for copy in part:
                    copy.wait()

        def units(n, carry, slot=slot):
            for k in range(3):
                at = pl.ds(pl.multiple_of((n * 3 + k) * tile, tile), tile)
                gate = dot(x[slot], wg[:, at])
                upper = dot(x[slot], wu[:, at])
                d_hidden = dot(ct[slot], wd[:, at])
                sigmoid = 1.0 / (1.0 + jnp.exp(-gate))
                swish = gate * sigmoid
                made[slot, 2, :, at] = (swish * upper).astype(BF16)
                made[slot, 1, :, at] = (d_hidden * swish).astype(BF16)
                made[slot, 0, :, at] = (
                    d_hidden * upper * sigmoid * (1.0 + gate * (1.0 - sigmoid))
                ).astype(BF16)
            return carry

        lax.fori_loop(0, padded // (3 * tile), units, 0)

        def columns(n, carry, slot=slot):
            at = pl.ds(pl.multiple_of(n * tile, tile), tile)
            term[slot, :, at] = dot_nt(made[slot, 0], wg[at, :]) + dot_nt(
                made[slot, 1], wu[at, :]
            )
            branch[slot, :, at] = dot_nt(made[slot, 2], wd[at, :]).astype(BF16)
            return carry

        if turn > 0:
            sums.step(turn - 1)
        lax.fori_loop(0, width // tile, columns, 0)
        for copies in stores(turn, (0, 2)):
            for copy in copies:
                copy.start()
    sums.total(d2)
    sums.finish()
    for turn in range(tp - 2, tp):
        for copies in stores(turn):
            for copy in copies:
                copy.wait()


def ff_part(dp, tp, ff, cot, n2):
    def shape(*dims, kind=BF16):
        return jax.ShapeDtypeStruct(dims, kind)

    own_rows, width = cot.shape[1:]
    padded = ff.shape[3]
    vmem = pl.BlockSpec(memory_space=pltpu.VMEM)
    anywhere = pl.BlockSpec(memory_space=ANY)
    return pl.pallas_call(
        functools.partial(ff_kernel, dp, tp),
        out_shape=(
            shape(FF_PARTS, tp * own_rows, padded),
            shape(2, width, tp * own_rows),
            shape(tp, own_rows, width),
            shape(own_rows, width, kind=F32),
        ),
        in_specs=[anywhere] * 3,
        out_specs=(anywhere,) * 3 + (vmem,),
        scratch_shapes=[
            pltpu.VMEM((width, padded), BF16),
            pltpu.VMEM((width, padded), BF16),
            pltpu.VMEM((width, padded), BF16),
            pltpu.VMEM((2, own_rows, width), BF16),
            pltpu.VMEM((2, own_rows, width), BF16),
            pltpu.VMEM((2, FF_PARTS, own_rows, padded), BF16),
            pltpu.VMEM((2, own_rows, width), F32),
            pltpu.VMEM((tp - 1, own_rows, width), BF16),
            pltpu.VMEM((2, tp - 1, own_rows, width), BF16),
            pltpu.VMEM((2, own_rows, width), BF16),
            pltpu.VMEM((2, 2, width, own_rows), BF16),
            pltpu.SemaphoreType.DMA((FF_PARTS, dp)),
            pltpu.SemaphoreType.DMA((2, 2)),
            pltpu.SemaphoreType.DMA((2, FF_PARTS)),
            pltpu.SemaphoreType.DMA((2, 2)),
            pltpu.SemaphoreType.DMA((2,)),
            pltpu.SemaphoreType.DMA((tp - 1,)),
            pltpu.SemaphoreType.DMA((2, tp - 1)),
        ],
        compiler_params=pltpu.CompilerParams(
            collective_id=3, has_side_effects=True, vmem_limit_bytes=60 << 20
        ),
        name="ff_part",
    )(ff, cot, n2)


class DownReduce:
    def __init__(self, place, term, got, send, recv):
        self.place, self.term, self.got, self.send, self.recv = place, term, got, send, recv

    def copy(self, distance):
        return remote(
            self.term(self.place.z - distance),
            self.got(distance - 1),
            self.send(distance),
            self.recv(distance - 1),
            self.place.beside(-1),
        )

    def take(self, distance, out):
        place = self.place

        @pl.when(place.z < place.tp - 1)
        def _():
            ref = self.got(distance)
            remote(
                ref, ref, self.send(distance), self.recv(distance), place.beside(0)
            ).wait_recv()
            add_into(out, ref, out)

    def step(self, distance):
        place = self.place

        @pl.when(place.z >= distance)
        def _():
            if distance < place.tp - 1:
                self.take(distance, self.term(place.z - distance))
            self.copy(distance).start()

    def finish(self):
        for distance in range(1, self.place.tp):

            @pl.when(self.place.z >= distance)
            def _():
                self.copy(distance).wait_send()


def backward_kernel(
    dp, tp, chunk,
    res, vectors, att, q, kv, cosine, sine, d2, cot, x, lhs, act, mlp, probs, wo, wq, wkv,
    out, mlp_sent, mlp_got, d_branch, d_qkv, output, input_grad, vector_grads,
    part, taken, held, left, block, stage, weight, kv_weight, prob, d_att, d_kv, d_kv_low, kv_got,
    acc, wide, own_bf, d_res,
    act_sem, send_sem, recv_sem, left_sem, stage_sem, line_send, line_recv, out_sem, weight_sem,
    prob_sem, kv_send, kv_recv, in_sem,
):
    place = Place(dp, tp)
    z = place.z
    own_rows, width = res.shape
    depth = width // dp
    group = max(1, 384 // depth)
    tile = 256
    head = HEAD_DIMENSION
    scale = 1.0 / math.sqrt(head)
    columns = wq.shape[2]
    heads_width = tp * columns
    half_kv = KEYVALUE_HEADS * head
    per_part = act.shape[2] // chunk
    units = [(p, k) for p in (2, 0, 1) for k in range(per_part)]

    def fetch(u):
        p, k = units[u]
        return pltpu.make_async_copy(
            act.at[p, :, pl.ds(k * chunk, chunk)], taken.at[u % 2], act_sem.at[u % 2]
        )

    def fetch_left(k):
        return pltpu.make_async_copy(lhs.at[k], left, left_sem.at[0])

    def fetch_weight(n):
        source = wo if n < tp else wq
        return pltpu.make_async_copy(source.at[n % tp], weight.at[n % 2], weight_sem.at[n % 2])

    def fetch_probs(h, slot):
        return pltpu.make_async_copy(probs.at[h], prob.at[slot], prob_sem.at[slot])

    d2_copy = pltpu.make_async_copy(d2, wide, in_sem.at[0])
    cot_copy = pltpu.make_async_copy(cot, own_bf, in_sem.at[1])
    x_copy = pltpu.make_async_copy(x, own_bf, in_sem.at[2])
    kv_weight_copy = pltpu.make_async_copy(
        wkv.at[:, pl.ds(0, 2 * half_kv)], kv_weight, in_sem.at[3]
    )
    fetch_left(1).start()
    fetch(0).start()
    for copy in (d2_copy, cot_copy, fetch_weight(0), fetch_weight(1), kv_weight_copy):
        copy.start()
    for h in range(2):
        fetch_probs(h, h).start()
    place.greet(True, True)

    line = LineReduce(
        place,
        None,
        lambda turn: mlp_sent.at[turn],
        lambda side, k: mlp_got.at[side, k],
        lambda turn: line_send.at[turn],
        lambda side, k: line_recv.at[side, k],
    )

    def load_term(turn):
        return pltpu.make_async_copy(mlp.at[line.owner(turn)], stage.at[0], stage_sem.at[0])

    def load_got(side, distance):
        return pltpu.make_async_copy(mlp_got.at[side, distance], stage.at[1], stage_sem.at[1])

    def line_step(turn):
        side, offset, distance = line.way(turn)
        load_term(turn).wait()

        @pl.when(place.has(-offset))
        def _():
            line.arrival(side, distance).wait_recv()
            load_got(side, distance).start()
            load_got(side, distance).wait()
            add_into(stage.at[0], stage.at[1], stage.at[0])

        store = pltpu.make_async_copy(stage.at[0], mlp_sent.at[turn], stage_sem.at[0])
        store.start()
        store.wait()
        line.copy(turn).start()
        load_term(turn + 1).start()

    def line_total():
        load_term(tp - 1).wait()
        add_into(res, stage.at[0], d_res)
        for side, offset in ((0, -1), (1, 1)):

            @pl.when(place.has(offset))
            def _():
                line.arrival(side, 0).wait_recv()
                load_got(side, 0).start()
                load_got(side, 0).wait()
                add_into(d_res, stage.at[1], d_res)

        copy_into(d_res, output)

    load_term(0).start()
    down = DownReduce(
        place,
        lambda r: d_kv_low.at[pl.ds(pl.multiple_of(r * own_rows, 16), own_rows)],
        lambda k: kv_got.at[k],
        lambda k: kv_send.at[k],
        lambda k: kv_recv.at[k],
    )

    def second_norm():
        d2_copy.wait()
        cot_copy.wait()
        values, grad = res[...], wide[...]
        s = rms_scale(values)
        normed = values * s
        weighted = grad * vectors[1:2, :]
        inner = jnp.mean(weighted * normed, axis=1, keepdims=True)
        found = own_bf[...].astype(F32) + s * (weighted - normed * inner)
        d_res[...] = found
        d_branch[...] = found.astype(BF16)
        vector_grads[...] = jnp.zeros_like(vector_grads)
        vector_grads[1:2, :] = jnp.sum(grad * normed, axis=0, keepdims=True)
        x_copy.start()
        d_kv[...] = jnp.zeros_like(d_kv)

    def attended_grad(ts):
        for t in ts:
            fetch_weight(t).wait()
            d_att[:, t * columns : (t + 1) * columns] = dot(d_branch[...], weight[t % 2]).astype(
                BF16
            )
            fetch_weight(t + 2).start()

    def some_heads(begin, end):
        def one_head(h, carry):
            slot = h % 2
            at = pl.ds(pl.multiple_of(h * head, head), head)
            shared = h // REPEAT
            key_at = pl.ds(pl.multiple_of(shared * head, head), head)
            value_at = pl.ds(pl.multiple_of(half_kv + shared * head, head), head)
            fetch_probs(h, slot).wait()
            d_out = d_att[:, at]
            inner = jnp.sum(
                d_out.astype(F32) * att[:, at].astype(F32), axis=1, keepdims=True
            )
            acc[...] = jnp.zeros_like(acc)

            def one_block(j, carry):
                rows = pl.ds(pl.multiple_of(j * own_rows, 256), own_rows)
                low = prob[slot, :, rows]
                d_probs = dot_nt(d_out, kv[rows, value_at])
                d_scores = (low.astype(F32) * (scale * (d_probs - inner))).astype(BF16)
                acc[...] += dot(d_scores, kv[rows, key_at])
                d_kv[rows, key_at] += dot_tn(d_scores, q[:, at])
                d_kv[rows, value_at] += dot_tn(low, d_out)
                return carry

            lax.fori_loop(0, z + 1, one_block, 0)
            d_qkv[:, at] = turned(acc[...], cosine[...], -sine[...]).astype(BF16)

            @pl.when(h + 2 < QUERY_HEADS)
            def _():
                fetch_probs(h + 2, slot).start()

            return carry

        lax.fori_loop(begin, end, one_head, 0)

    def send_kv():
        def body(j, carry):
            rows = pl.ds(pl.multiple_of(j * own_rows, 256), own_rows)
            d_kv_low[rows, :] = d_kv[rows, :].astype(BF16)
            return carry

        lax.fori_loop(0, z + 1, body, 0)
        down.step(tp - 1)
        for distance in range(tp - 2, 0, -1):
            down.step(distance)

    def normed_grad(ts):
        for t in ts:
            fetch_weight(tp + t).wait()
            for j in range(width // 512):
                cut = slice(j * 512, (j + 1) * 512)
                found = dot_nt(
                    d_qkv[:, t * columns : (t + 1) * columns], weight[(tp + t) % 2, cut, :]
                )
                wide[:, cut] = found + wide[:, cut] if t else found
            if t + 2 < tp:
                fetch_weight(tp + t + 2).start()

    def first_norm():
        mine = pl.ds(pl.multiple_of(z * own_rows, 16), own_rows)
        down.take(0, d_kv.at[mine])
        for h in range(KEYVALUE_HEADS):
            cut = slice(h * head, (h + 1) * head)
            d_qkv[:, heads_width + h * head : heads_width + (h + 1) * head] = turned(
                d_kv[mine, cut], cosine[...], -sine[...]
            ).astype(BF16)
        d_qkv[:, heads_width + half_kv :] = d_kv[mine, half_kv:].astype(BF16)
        kv_weight_copy.wait()
        for j in range(width // 512):
            cut = slice(j * 512, (j + 1) * 512)
            wide[:, cut] += dot_nt(d_qkv[:, heads_width:], kv_weight[cut, :])
        x_copy.wait()
        values, grad = own_bf[...].astype(F32), wide[...]
        s = rms_scale(values)
        normed = values * s
        weighted = grad * vectors[0:1, :]
        inner = jnp.mean(weighted * normed, axis=1, keepdims=True)
        input_grad[...] = (d_res[...] + s * (weighted - normed * inner)).astype(BF16)
        vector_grads[0:1, :] = jnp.sum(grad * normed, axis=0, keepdims=True)
        sums_of = jnp.sum(d_qkv[...].astype(F32), axis=0, keepdims=True)
        vector_grads[2:3, :] = sums_of[:, :heads_width]
        vector_grads[3:4, : 2 * half_kv] = sums_of[:, heads_width:]

    per = QUERY_HEADS // tp
    pieces = [
        [second_norm, lambda: attended_grad(range(tp))],
        [lambda: some_heads(0, 2), lambda: line_step(0)],
        [lambda: some_heads(2, 4)],
        [lambda: some_heads(4, 6)],
        [lambda: some_heads(6, 8), lambda: line_step(1)],
        [lambda: some_heads(8, 10)],
        [lambda: some_heads(10, 12), send_kv],
        [lambda: normed_grad(range(tp)), lambda: line_step(2)],
        [],
        [first_norm],
        [line_total],
    ]

    def stored(u):
        p, k = units[u]
        return pltpu.make_async_copy(
            block.at[u % 2], out.at[p, :, pl.ds(k * chunk, chunk)], out_sem.at[u % 2]
        )

    sums = [
        PlaneReduce(
            place,
            lambda b, u=u: part.at[u % 2, b],
            lambda s, u=u: held.at[u, s],
            lambda s, u=u: send_sem.at[u, s],
            lambda s, u=u: recv_sem.at[u, s],
        )
        for u in range(len(units))
    ]
    last = place.steps
    fetch_left(1).wait()
    for turn in range(max(len(units) + last + 1, len(pieces))):
        if turn < len(units):
            u = turn
            p, k = units[u]
            if u + 1 < len(units):
                fetch(u + 1).start()
            if u == per_part:
                fetch_left(0).wait()
            fetch(u).wait()
            if u >= 2:
                sums[u - 2].wait_send(0)

            def body(n, carry, u=u):
                i, j = n // (chunk // tile), n % (chunk // tile)
                rows = pl.ds(pl.multiple_of(i * (group * depth), 16), group * depth)
                cols = pl.ds(pl.multiple_of(j * tile, tile), tile)
                found = dot(left[rows, :], taken[u % 2, :, cols]).astype(BF16)
                for g in range(group):
                    part[u % 2, i * group + g, :, cols] = found[g * depth : (g + 1) * depth]
                return carry

            lax.fori_loop(0, dp // group * (chunk // tile), body, 0)
            sums[u].start(0)
            if u == per_part - 1:
                fetch_left(0).start()
        for level in range(last + 1):
            u = turn - 1 - level
            if 0 <= u < len(units):
                if level == last:
                    if u >= 2:
                        stored(u - 2).wait()
                    sums[u].absorb(level, block.at[u % 2])
                    stored(u).start()
                else:
                    sums[u].absorb(level)
        if turn < len(pieces):
            for piece in pieces[turn]:
                piece()
    line.finish()
    down.finish()
    for u in range(len(units)):
        if u >= len(units) - 2:
            stored(u).wait()
        for level in range(0 if u >= len(units) - 2 else 1, last + 1):
            sums[u].wait_send(level)


def backward_part(
    dp, tp, res, vectors, att, q, kv, cosine, sine, d2, cot, x, lhs, act, mlp, probs, wo, wq, wkv
):
    def shape(*dims, kind=BF16):
        return jax.ShapeDtypeStruct(dims, kind)

    own_rows, width = res.shape
    depth = width // dp
    items, padded = act.shape[1:]
    columns = wq.shape[2]
    kv_columns = kv.shape[1]
    chunk = 768
    count = FF_PARTS * padded // chunk
    vmem = pl.BlockSpec(memory_space=pltpu.VMEM)
    anywhere = pl.BlockSpec(memory_space=ANY)
    return pl.pallas_call(
        functools.partial(backward_kernel, dp, tp, chunk),
        out_shape=(
            shape(FF_PARTS, depth, padded, kind=F32),
            shape(tp - 1, own_rows, width),
            shape(2, tp - 1, own_rows, width),
            shape(own_rows, width),
            shape(own_rows, tp * columns + kv_columns),
            shape(own_rows, width),
            shape(own_rows, width),
            shape(8, width, kind=F32),
        ),
        in_specs=[vmem] * 7 + [anywhere] * 10,
        out_specs=(anywhere,) * 3 + (vmem,) * 5,
        scratch_shapes=[
            pltpu.VMEM((2, dp, depth, chunk), BF16),
            pltpu.VMEM((2, items, chunk), BF16),
            pltpu.VMEM((count, dp - 1, depth, chunk), BF16),
            pltpu.VMEM((width, items), BF16),
            pltpu.VMEM((2, depth, chunk), F32),
            pltpu.VMEM((2, own_rows, width), BF16),
            pltpu.VMEM((2, width, columns), BF16),
            pltpu.VMEM((width, kv_columns), BF16),
            pltpu.VMEM((2, own_rows, items), BF16),
            pltpu.VMEM((own_rows, tp * columns), BF16),
            pltpu.VMEM((items, kv_columns), F32),
            pltpu.VMEM((items, kv_columns), BF16),
            pltpu.VMEM((tp - 1, own_rows, kv_columns), BF16),
            pltpu.VMEM((own_rows, HEAD_DIMENSION), F32),
            pltpu.VMEM((own_rows, width), F32),
            pltpu.VMEM((own_rows, width), BF16),
            pltpu.VMEM((own_rows, width), F32),
            pltpu.SemaphoreType.DMA((2,)),
            pltpu.SemaphoreType.DMA((count, dp - 1)),
            pltpu.SemaphoreType.DMA((count, dp - 1)),
            pltpu.SemaphoreType.DMA((1,)),
            pltpu.SemaphoreType.DMA((2,)),
            pltpu.SemaphoreType.DMA((tp - 1,)),
            pltpu.SemaphoreType.DMA((2, tp - 1)),
            pltpu.SemaphoreType.DMA((2,)),
            pltpu.SemaphoreType.DMA((2,)),
            pltpu.SemaphoreType.DMA((2,)),
            pltpu.SemaphoreType.DMA((tp,)),
            pltpu.SemaphoreType.DMA((tp - 1,)),
            pltpu.SemaphoreType.DMA((4,)),
        ],
        compiler_params=pltpu.CompilerParams(
            collective_id=1, has_side_effects=True, vmem_limit_bytes=63 << 20
        ),
        name="backward_part",
    )(res, vectors, att, q, kv, cosine, sine, d2, cot, x, lhs, act, mlp, probs, wo, wq, wkv)


def attn_grad_kernel(
    dp, tp, widths, n1, d_qkv, d_branch, att, vectors, kv_out, q_out, o_out, vectors_out,
    turned_rows, part, held, own, line_kv, line_qo, vector_sum, vector_got, line_vector,
    send_sem, recv_sem, line_send, line_recv, vector_send, vector_recv,
):
    place = Place(dp, tp)
    z = place.z
    depth, columns = q_out.shape
    width = dp * depth
    heads_width = tp * columns
    barrier = pltpu.get_barrier_semaphore()
    for partner in place.partners + [place.sibling]:
        pl.semaphore_signal(barrier, inc=1, device_id=place.device(partner), device_id_type=MESH)
    for t in range(tp):

        @pl.when(t != z)
        def _():
            pl.semaphore_signal(barrier, inc=1, device_id=(place.d, t), device_id_type=MESH)

    pl.semaphore_wait(barrier, place.steps + tp)
    kinds = (0, 0, 2, 1, 1)
    halves = (0, 1, 0, 0, 1)
    count = len(widths)
    group = max(1, 384 // depth)
    sums = [
        PlaneReduce(
            place,
            lambda b, u=u: part.at[u, b, :, pl.ds(0, widths[u])],
            lambda s, u=u: held.at[u, s, :, pl.ds(0, widths[u])],
            lambda s, u=u: send_sem.at[u, s],
            lambda s, u=u: recv_sem.at[u, s],
        )
        for u in range(count)
    ]

    def make(u):
        kind, half = kinds[u], halves[u]
        left = 1 if kind == 1 else 0
        right = att if kind == 1 else d_qkv
        base = heads_width if kind == 2 else half * widths[u]

        def body(i, carry):
            rows = pl.ds(pl.multiple_of(i * (group * depth), 16), group * depth)
            for j in range(widths[u] // 256):
                found = dot(
                    turned_rows[left, rows, :], right[:, base + j * 256 : base + (j + 1) * 256]
                ).astype(BF16)
                for g in range(group):
                    part[u, i * group + g, :, j * 256 : (j + 1) * 256] = found[
                        g * depth : (g + 1) * depth
                    ]
            return carry

        lax.fori_loop(0, dp // group, body, 0)
        sums[u].start(0)

    def line_copies(u):
        found = []
        kind, half = kinds[u], halves[u]
        for t in range(tp):
            if kind == 2:
                src, dst = own.at[u, :, pl.ds(0, widths[u])], line_kv.at[z]
            elif t // 2 == half:
                src, dst = own.at[u, :, pl.ds((t % 2) * columns, columns)], line_qo.at[kind, z]
            else:
                continue
            found.append((t, remote(
                src, dst, line_send.at[u, t], line_recv.at[kind, z], (place.d, t)
            )))
        return found

    last = place.steps

    def work(turn):
        for level in range(last + 1):
            u = turn - level
            if 0 <= u < count:
                target = own.at[u, :, pl.ds(0, widths[u])] if level == last else None
                sums[u].absorb(level, target)
                if level == last:
                    for t, copy in line_copies(u):

                        @pl.when(t != z)
                        def _():
                            copy.start()

    ways = [place.sibling] + place.partners

    def vector_copy(level):
        return remote(
            vectors if level == 0 else vector_sum.at[level - 1],
            vector_got.at[level],
            vector_send.at[level],
            vector_recv.at[level],
            place.device(ways[level]),
        )

    def vector_step(level):
        vector_copy(level).wait_recv()
        mine = vectors[...] if level == 0 else vector_sum[level - 1]
        vector_sum[level] = mine + vector_got[level]
        if level < last:
            vector_copy(level + 1).start()
        else:
            for t in range(tp):

                @pl.when(t != z)
                def _():
                    vector_line(t).start()

    def vector_line(t):
        return remote(
            vector_sum.at[last],
            line_vector.at[z],
            line_send.at[count, t],
            line_recv.at[3, z],
            (place.d, t),
        )

    vector_copy(0).start()
    turned_rows[0] = n1[...].T
    make(0)
    make(1)
    turned_rows[1] = d_branch[...].T
    for u in range(2, count):
        make(u)
    for turn in range(count + last):
        work(turn)
        if turn <= last:
            vector_step(turn)

    def arrived(ref, kind):
        for t in range(tp):

            @pl.when(t != z)
            def _():
                remote(
                    ref.at[t], ref.at[t], line_send.at[0, t], line_recv.at[kind, t], (place.d, t)
                ).wait_recv()

    def total(ref, mine, out):
        acc = mine.astype(F32)
        for t in range(tp):
            acc = acc + jnp.where(t != z, ref[t].astype(F32), 0.0)
        out[...] = acc

    at = pl.ds(pl.multiple_of((z % 2) * columns, 128), columns)
    arrived(line_vector, 3)
    total(line_vector, vector_sum[last], vectors_out)
    arrived(line_qo.at[0], 0)
    total(line_qo.at[0], own[z // 2, :, at], q_out)
    arrived(line_kv, 2)
    total(line_kv, own[2, :, : widths[2]], kv_out)
    arrived(line_qo.at[1], 1)
    total(line_qo.at[1], own[3 + z // 2, :, at], o_out)
    for u in range(count):
        for level in range(last + 1):
            sums[u].wait_send(level)
        for t, copy in line_copies(u):

            @pl.when(t != z)
            def _():
                copy.wait_send()

    for level in range(last + 1):
        vector_copy(level).wait_send()
    for t in range(tp):

        @pl.when(t != z)
        def _():
            vector_line(t).wait_send()


def attn_grads(dp, tp, n1, d_qkv, d_branch, att, vectors):
    own_rows, width = n1.shape
    depth = width // dp
    heads_width = att.shape[1]
    kv_columns = d_qkv.shape[1] - heads_width
    half = heads_width // 2
    widths = (half, half, kv_columns, half, half)
    columns = heads_width // tp
    levels = dp.bit_length() - 1
    vmem = pl.BlockSpec(memory_space=pltpu.VMEM)
    return pl.pallas_call(
        functools.partial(attn_grad_kernel, dp, tp, widths),
        out_shape=(
            jax.ShapeDtypeStruct((depth, kv_columns), F32),
            jax.ShapeDtypeStruct((depth, columns), F32),
            jax.ShapeDtypeStruct((depth, columns), F32),
            jax.ShapeDtypeStruct(vectors.shape, F32),
        ),
        in_specs=[vmem] * 5,
        out_specs=(vmem,) * 4,
        scratch_shapes=[
            pltpu.VMEM((2, width, own_rows), BF16),
            pltpu.VMEM((5, dp, depth, half), BF16),
            pltpu.VMEM((5, dp - 1, depth, half), BF16),
            pltpu.VMEM((5, depth, half), BF16),
            pltpu.VMEM((tp, depth, kv_columns), BF16),
            pltpu.VMEM((2, tp, depth, columns), BF16),
            pltpu.VMEM((levels,) + vectors.shape, F32),
            pltpu.VMEM((levels,) + vectors.shape, F32),
            pltpu.VMEM((tp,) + vectors.shape, F32),
            pltpu.SemaphoreType.DMA((5, dp - 1)),
            pltpu.SemaphoreType.DMA((5, dp - 1)),
            pltpu.SemaphoreType.DMA((6, tp)),
            pltpu.SemaphoreType.DMA((4, tp)),
            pltpu.SemaphoreType.DMA((levels,)),
            pltpu.SemaphoreType.DMA((levels,)),
        ],
        compiler_params=pltpu.CompilerParams(
            collective_id=2, has_side_effects=True, vmem_limit_bytes=56 << 20
        ),
        name="attn_grads",
    )(n1, d_qkv, d_branch, att, vectors)


def local(
    inputs,
    segment_ids,
    first_gain,
    query_weight,
    query_bias,
    key_value_weight,
    key_value_bias,
    output_weight,
    second_gain,
    gateup_weight,
    down_weight,
    cotangent,
):
    dp = lax.axis_size("dp")
    tp = lax.axis_size("tensor")
    rank = lax.axis_index("tensor")
    width = inputs.shape[1]
    own_rows = inputs.shape[0]
    depth = query_weight.shape[0]
    columns = query_weight.shape[1]
    kv_columns = key_value_weight.shape[1]
    hidden_units = gateup_weight.shape[2]
    heads_width = columns * tp
    head = HEAD_DIMENSION
    scale = 1.0 / math.sqrt(head)

    padded = -(-hidden_units // 256) * 256
    ff_own = jnp.stack([gateup_weight[0], gateup_weight[1], down_weight.T])
    ff_own = jnp.pad(ff_own, ((0, 0), (0, 0), (0, padded - hidden_units)))
    qb_count, kvb_count = query_bias.shape[0], key_value_bias.shape[0]
    own_kvbias = jnp.pad(key_value_bias, (0, depth - kvb_count))
    side = jnp.pad(jnp.stack([first_gain, second_gain, own_kvbias], axis=1), ((0, 0), (0, 125)))
    own_segments = lax.dynamic_slice_in_dim(segment_ids, rank * own_rows, own_rows, 0)
    (
        ff_all, grad_rows, second_rows, wq, wo, wkv, probs_low,
        residual, attended, normed_own, rot_query, all_kv, cosine, sine, vectors,
    ) = forward_part(
        dp,
        tp,
        kvb_count,
        qb_count,
        inputs,
        segment_ids[None, :],
        own_segments[:, None],
        query_weight,
        output_weight.T,
        jnp.pad(query_bias[None, :], ((0, 15), (0, 128 - qb_count))),
        jnp.concatenate([key_value_weight, side], axis=1),
        ff_own,
        cotangent,
    )
    act, lhs, mlp_terms, d_second = ff_part(dp, tp, ff_all, grad_rows, second_rows)
    ff_sh, _, _, d_branch, d_qkv, output, input_grad, vector_grads = backward_part(
        dp, tp, residual, vectors, attended, rot_query, all_kv, cosine, sine,
        d_second, cotangent, inputs, lhs, act, mlp_terms, probs_low, wo, wq, wkv,
    )
    kv_sh, q_sh, o_sh, small = attn_grads(
        dp, tp, normed_own, d_qkv, d_branch, attended, vector_grads
    )
    d = lax.axis_index("dp")

    def mine(row, count, index):
        return lax.dynamic_slice_in_dim(row, index * count, count, 0)

    return (
        output,
        input_grad,
        mine(small[0], depth, d),
        q_sh,
        mine(small[2], qb_count, rank * dp + d),
        kv_sh,
        mine(small[3], kvb_count, d),
        o_sh.T,
        mine(small[1], depth, d),
        ff_sh[:2, :, :hidden_units],
        ff_sh[2, :, :hidden_units].T,
    )


def solution(mesh):
    in_specs = (
        P(("dp", "tensor"), None),
        P("dp"),
        P("dp"),
        P("dp", "tensor"),
        P(("tensor", "dp")),
        P("dp", None),
        P("dp"),
        P("tensor", "dp"),
        P("dp"),
        P(None, "dp", "tensor"),
        P("tensor", "dp"),
        P(("dp", "tensor"), None),
    )
    out_specs = (
        P(("dp", "tensor"), None),
        P(("dp", "tensor"), None),
        P("dp"),
        P("dp", "tensor"),
        P(("tensor", "dp")),
        P("dp", None),
        P("dp"),
        P("tensor", "dp"),
        P("dp"),
        P(None, "dp", "tensor"),
        P("tensor", "dp"),
    )
    return jax.shard_map(local, mesh=mesh, in_specs=in_specs, out_specs=out_specs, check_vma=False)
```

```python
import functools
import math

import jax
import jax.numpy as jnp
from jax import lax
from jax.experimental import pallas as pl
from jax.experimental.pallas import tpu as pltpu
from jax.sharding import PartitionSpec as P

QUERY_HEADS = 12
KEYVALUE_HEADS = 2
HEAD_DIMENSION = 128
REPEAT = QUERY_HEADS // KEYVALUE_HEADS

EPSILON = 1e-06
THETA = 1000000.0
NEGATIVE = -1e30

F32 = jnp.float32
BF16 = jnp.bfloat16


def rms_scale(rows):
    return lax.rsqrt(jnp.mean(rows * rows, axis=-1, keepdims=True) + EPSILON)


def norm_back(rows, gain, grad):
    scale = rms_scale(rows)
    normed = rows * scale
    weighted = grad * gain
    inner = jnp.mean(weighted * normed, axis=-1, keepdims=True)
    return (scale * (weighted - normed * inner), jnp.sum(grad * normed, axis=0))


def rope_tables(segments, head_extent):
    index = jnp.arange(segments.shape[0], dtype=jnp.int32)
    starts = jnp.concatenate([jnp.ones((1,), dtype=bool), segments[1:] != segments[:-1]])
    first = lax.cummax(jnp.where(starts, index, jnp.zeros_like(index)), axis=0)
    placed = (index - first).astype(F32)
    freqs = jnp.exp(
        jnp.arange(head_extent // 2, dtype=F32) * (-2.0 * math.log(THETA) / head_extent)
    )
    return placed, freqs


def apply_rotation(value_rows, cosine_table, sine_table):
    half = value_rows.shape[-1] // 2
    former = value_rows[..., :half]
    latter = value_rows[..., half:]
    return jnp.concatenate(
        [former * cosine_table - latter * sine_table, latter * cosine_table + former * sine_table],
        axis=-1,
    )


def unrotate(grads, cosine_table, sine_table):
    return apply_rotation(grads, cosine_table, -sine_table)


def dot(left, right):
    return jnp.dot(left, right, preferred_element_type=F32)


def dot_nt(left, right):
    return lax.dot_general(left, right, (((1,), (1,)), ((), ())), preferred_element_type=F32)


def dot_tn(left, right):
    return lax.dot_general(left, right, (((0,), (0,)), ((), ())), preferred_element_type=F32)


MESH = pl.DeviceIdType.MESH
ANY = pl.ANY


def flip(index, bit):
    return index + (1 << bit) * (1 - 2 * ((index // (1 << bit)) % 2))


class Place:
    def __init__(self, dp, tp):
        self.dp, self.tp = dp, tp
        self.d, self.z = lax.axis_index("dp"), lax.axis_index("tensor")
        self.steps = dp.bit_length() - 2
        odd = self.d % 2
        self.partners = []
        for step in range(self.steps):
            first, other = flip(self.d, 1 + step), flip(self.d, self.steps - step)
            self.partners.append(first + odd * (other - first))
        self.sibling = flip(self.d, 0)
        self.deltas = [partner - self.d for partner in self.partners]

    def block(self, mask):
        index = self.d
        for step in range(self.steps):
            if (mask >> step) & 1:
                index = index + self.deltas[step]
        return index

    def sibling_block(self, mask):
        index = self.sibling
        for step in range(self.steps):
            if (mask >> step) & 1:
                index = index + self.deltas[self.steps - 1 - step]
        return index

    def device(self, index):
        return (index, self.z)

    def beside(self, offset):
        return (self.d, self.z + offset)

    def greet(self, plane, line):
        barrier = pltpu.get_barrier_semaphore()
        count = 0
        if plane:
            for partner in self.partners + [self.sibling]:
                pl.semaphore_signal(
                    barrier, inc=1, device_id=self.device(partner), device_id_type=MESH
                )
            count = self.steps + 1
        if line:
            for offset in (-1, 1):

                @pl.when(self.has(offset))
                def _():
                    pl.semaphore_signal(
                        barrier, inc=1, device_id=self.beside(offset), device_id_type=MESH
                    )

            count = count + jnp.where(self.z > 0, 1, 0) + jnp.where(self.z < self.tp - 1, 1, 0)
        pl.semaphore_wait(barrier, count)

    def has(self, offset):
        return (self.z + offset >= 0) & (self.z + offset < self.tp)


def remote(src, dst, send, recv, device):
    return pltpu.make_async_remote_copy(
        src_ref=src, dst_ref=dst, send_sem=send, recv_sem=recv, device_id=device, device_id_type=MESH
    )


class PlaneGather:
    def __init__(self, place, own, full, send, recv):
        self.place, self.own, self.full, self.send, self.recv = place, own, full, send, recv
        self.half = 1 << place.steps

    def at(self, mask):
        return self.full(self.place.block(mask)) if mask else self.own

    def copy(self, mask, step):
        place = self.place
        if step < place.steps:
            label, device = mask | (1 << step), place.device(place.partners[step])
        else:
            label, device = self.half + mask, place.device(place.sibling)
        return remote(
            self.at(mask), self.full(place.block(mask)), self.send(label), self.recv(label), device
        )

    def arrival(self, label):
        place = self.place
        if label < self.half:
            ref = self.full(place.block(label))
        else:
            ref = self.full(place.sibling_block(label - self.half))
        return remote(ref, ref, self.send(label), self.recv(label), place.device(place.sibling))

    def sends(self, mask):
        return [self.copy(mask, step) for step in range(mask.bit_length(), self.place.steps + 1)]

    def start(self):
        for copy in self.sends(0):
            copy.start()

    def hand_on(self, mask):
        self.arrival(mask).wait_recv()
        for copy in self.sends(mask):
            copy.start()

    def spread(self):
        for mask in range(1, self.half):
            self.hand_on(mask)

    def complete(self):
        for mask in range(self.half):
            self.arrival(self.half + mask).wait_recv()

    def finish(self):
        for mask in range(self.half):
            for copy in self.sends(mask):
                copy.wait_send()


class LineGather:
    def __init__(self, place, own, full, send, recv, offsets=(1, -1)):
        self.place, self.own, self.full, self.send, self.recv = place, own, full, send, recv
        self.offsets = offsets

    def copy(self, distance, offset):
        place = self.place
        source = place.z - offset * distance
        side = 0 if offset > 0 else 1
        src = self.full(source) if distance else self.own
        return remote(
            src,
            self.full(source),
            self.send(side, distance),
            self.recv(side, distance),
            place.beside(offset),
        )

    def each(self, distance, act):
        place = self.place
        for offset in self.offsets:

            @pl.when(place.has(-offset * distance) & place.has(offset))
            def _():
                act(self.copy(distance, offset))

    def start(self):
        self.each(0, lambda copy: copy.start())

    def arrived(self, distance):
        place = self.place
        for offset in self.offsets:

            @pl.when(place.has(-offset * distance))
            def _():
                side = 0 if offset > 0 else 1
                ref = self.full(place.z - offset * distance)
                remote(
                    ref,
                    ref,
                    self.send(side, distance - 1),
                    self.recv(side, distance - 1),
                    place.beside(-offset),
                ).wait_recv()

    def hand_on(self, distance):
        self.arrived(distance)
        if distance < self.place.tp - 1:
            self.each(distance, lambda copy: copy.start())

    def finish(self):
        for distance in range(self.place.tp - 1):
            self.each(distance, lambda copy: copy.wait_send())


def turned(rows, cosine, sine):
    return rows * cosine + pltpu.roll(rows, rows.shape[1] // 2, 1) * sine


def forward_kernel(
    dp, tp, kvb_count, qb_count,
    x, seg_row, seg_col, zq, zo, zb, kvs, ff, cot,
    ff_out, cot_out, n2_out, wq_out, wo_out, wkv_out, p_out,
    res, att, n1, q, kv, cosine, sine, vectors,
    wq, wo, wkv, wb, spread, mask, probs, n2,
    plane_send, plane_recv, line_send, line_recv, local_sem, probs_sem,
):
    place = Place(dp, tp)
    d, z = place.d, place.z
    own_rows, width = x.shape
    depth, columns = zq.shape
    items = seg_row.shape[1]
    head = HEAD_DIMENSION
    kv_columns = kv.shape[1]
    my_rows = pl.ds(pl.multiple_of(d * depth, 16), depth)

    def rows_of(b):
        return pl.ds(pl.multiple_of(b * depth, 16), depth)

    def plane(item, own, full):
        return PlaneGather(
            place, own, full, lambda m: plane_send.at[item, m], lambda m: plane_recv.at[item, m]
        )

    def line(item, own, full, offsets=(1, -1)):
        return LineGather(
            place,
            own,
            full,
            lambda s, k: line_send.at[item, s, k],
            lambda s, k: line_recv.at[item, s, k],
            offsets,
        )

    starts = [
        pltpu.make_async_copy(zq, wq.at[z, my_rows], local_sem.at[0]),
        pltpu.make_async_copy(zo, wo.at[z, my_rows], local_sem.at[1]),
        pltpu.make_async_copy(zb, wb.at[d, z], local_sem.at[2]),
        pltpu.make_async_copy(kvs, wkv.at[my_rows], local_sem.at[3]),
        pltpu.make_async_copy(ff, ff_out.at[d], local_sem.at[4]),
        pltpu.make_async_copy(cot, cot_out.at[z], local_sem.at[5]),
    ]
    for copy in starts:
        copy.start()
    place.greet(True, True)
    line_q = line(0, zq, lambda t: wq.at[t, my_rows])
    line_o = line(1, zo, lambda t: wo.at[t, my_rows])
    line_b = line(2, zb, lambda t: wb.at[d, t])
    line_cot = line(3, cot, lambda t: cot_out.at[t])
    line_kv = line(
        4,
        kv.at[pl.ds(pl.multiple_of(z * own_rows, 16), own_rows)],
        lambda t: kv.at[pl.ds(pl.multiple_of(t * own_rows, 16), own_rows)],
        (1,),
    )
    line_n2 = line(5, n2, lambda t: n2_out.at[t])
    plane_kv = plane(0, kvs, lambda b: wkv.at[rows_of(b)])
    plane_q = plane(1, wq.at[:, my_rows], lambda b: wq.at[:, rows_of(b)])
    plane_o = plane(2, wo.at[:, my_rows], lambda b: wo.at[:, rows_of(b)])
    plane_b = plane(3, wb.at[d], lambda b: wb.at[b])
    plane_ff = [
        plane(4 + part, ff.at[part], lambda b, part=part: ff_out.at[b, part]) for part in (2, 0, 1)
    ]
    line_b.start()
    line_q.start()
    plane_kv.start()

    begin = z * own_rows
    row_at = begin + lax.broadcasted_iota(jnp.int32, (own_rows, items), 0)
    col_at = lax.broadcasted_iota(jnp.int32, (own_rows, items), 1)
    mine, theirs = seg_col[...], seg_row[...]
    allowed = (mine == theirs) & (col_at <= row_at)
    mask[...] = jnp.where(allowed, 0.0, NEGATIVE)
    below = jnp.sum(jnp.where(theirs < mine, 1.0, 0.0), axis=1, keepdims=True)
    lane = lax.broadcasted_iota(jnp.int32, (own_rows, head), 1)
    half = lane % (head // 2)
    index = begin + lax.broadcasted_iota(jnp.int32, (own_rows, head), 0)
    freqs = jnp.exp(half.astype(F32) * (-2.0 * math.log(THETA) / head))
    angles = (index.astype(F32) - below) * freqs
    cosine[...] = jnp.cos(angles)
    sine[...] = jnp.sin(angles) * jnp.where(lane < head // 2, -1.0, 1.0)

    for distance in range(1, tp):
        line_b.hand_on(distance)
    line_q.hand_on(1)
    line_q.hand_on(2)
    plane_kv.spread()
    for distance in range(3, tp):
        line_q.hand_on(distance)
    starts[0].wait()
    plane_q.start()
    starts[2].wait()
    plane_b.start()
    starts[3].wait()
    plane_kv.complete()

    pick_row = lax.broadcasted_iota(jnp.int32, (16, 128), 0)
    pick_col = lax.broadcasted_iota(jnp.int32, (16, 128), 1)
    pick = jnp.where(pick_row == pick_col, 1.0, 0.0).astype(BF16)
    vector_rows = dot_nt(pick, wkv[:, kv_columns:])
    vectors[...] = vector_rows
    block_row = lax.broadcasted_iota(jnp.int32, (depth, kv_columns), 0)
    block_col = lax.broadcasted_iota(jnp.int32, (depth, kv_columns), 1)
    for b in range(dp):
        hit = (block_row < kvb_count) & (block_col == block_row + b * kvb_count)
        spread[b * depth : (b + 1) * depth, :] = jnp.where(hit, 1.0, 0.0).astype(BF16)
    kv_bias = dot(vector_rows.astype(BF16), spread[...])[2:3, :]

    xs = x[...].astype(F32)
    n1[...] = (xs * rms_scale(xs) * vector_rows[0:1, :]).astype(BF16)
    kv_rows = dot(n1[...], wkv[:, :kv_columns]) + kv_bias
    at = pl.ds(pl.multiple_of(begin, 16), own_rows)
    for h in range(KEYVALUE_HEADS):
        cut = slice(h * head, (h + 1) * head)
        kv[at, cut] = turned(kv_rows[:, cut], cosine[...], sine[...]).astype(BF16)
    kv[at, KEYVALUE_HEADS * head :] = kv_rows[:, KEYVALUE_HEADS * head :].astype(BF16)
    line_kv.start()
    line_o.start()
    line_kv.hand_on(1)
    plane_b.spread()
    for mask_of in range(1, 1 << place.steps):
        if mask_of == plane_q.half - 1:
            plane_ff[0].start()
            line_kv.hand_on(2)
        plane_q.hand_on(mask_of)
    for distance in range(1, tp):
        line_o.hand_on(distance)
    starts[1].wait()
    plane_o.start()
    for distance in range(3, tp):
        line_kv.hand_on(distance)
    line_cot.start()
    plane_b.complete()
    small_row = lax.broadcasted_iota(jnp.int32, (128, columns), 0)
    small_col = lax.broadcasted_iota(jnp.int32, (128, columns), 1)
    q_bias = jnp.zeros((tp * 16, columns), F32)
    for b in range(dp):
        hit = (small_row < qb_count) & (small_col == small_row + b * qb_count)
        one = jnp.where(hit, 1.0, 0.0).astype(BF16)
        q_bias = q_bias + dot(wb[b].reshape(tp * 16, 128), one)
    plane_q.complete()
    for t in range(tp):
        rows = dot(n1[...], wq[t]) + q_bias[t * 16 : t * 16 + 1, :]
        for h in range(columns // head):
            cut = slice(h * head, (h + 1) * head)
            out = slice(t * columns + h * head, t * columns + (h + 1) * head)
            q[:, out] = turned(rows[:, cut], cosine[...], sine[...]).astype(BF16)
    outs = [
        pltpu.make_async_copy(wq, wq_out, local_sem.at[0]),
        pltpu.make_async_copy(wkv, wkv_out, local_sem.at[3]),
    ]
    for copy in outs:
        copy.start()

    scale = 1.0 / math.sqrt(head)
    group = QUERY_HEADS // tp

    def probs_copy(part, count):
        at = pl.ds(part * group, group)
        return pltpu.make_async_copy(
            probs.at[at, :, pl.ds(0, count)], p_out.at[at, :, pl.ds(0, count)], probs_sem.at[part]
        )

    for part in range(tp):
        for blocks in range(1, tp + 1):
            count = blocks * own_rows

            @pl.when(z == blocks - 1)
            def _():
                def one_head(i, carry):
                    h = part * group + i
                    at = pl.ds(pl.multiple_of(h * head, head), head)
                    shared = h // REPEAT
                    key_at = pl.ds(pl.multiple_of(shared * head, head), head)
                    value_at = pl.ds(pl.multiple_of((KEYVALUE_HEADS + shared) * head, head), head)
                    scores = dot_nt(q[:, at], kv[0:count, key_at]) * scale + mask[:, 0:count]
                    top = jnp.max(scores, axis=1, keepdims=True)
                    weights = jnp.exp(scores - top)
                    total = jnp.sum(weights, axis=1, keepdims=True)
                    low = (weights / total).astype(BF16)
                    probs[h, :, 0:count] = low
                    att[:, at] = dot(low, kv[0:count, value_at]).astype(BF16)
                    return carry

                lax.fori_loop(0, group, one_head, 0)
                probs_copy(part, count).start()

    plane_ff[1].start()
    line_cot.hand_on(1)
    plane_o.spread()
    line_cot.hand_on(2)
    plane_o.complete()
    outs.append(pltpu.make_async_copy(wo, wo_out, local_sem.at[1]))
    outs[-1].start()
    for j in range(width // 512):
        cut = slice(j * 512, (j + 1) * 512)
        acc = x[:, cut].astype(F32)
        for t in range(tp):
            acc = acc + dot_nt(att[:, t * columns : (t + 1) * columns], wo[t, cut, :])
        res[:, cut] = acc
    residual = res[...]
    n2[...] = (residual * rms_scale(residual) * vectors[1:2, :]).astype(BF16)
    line_n2.start()
    n2_copy = pltpu.make_async_copy(n2, n2_out.at[z], local_sem.at[2])
    n2_copy.start()
    plane_ff[0].spread()
    plane_ff[2].start()
    for distance in range(3, tp):
        line_cot.hand_on(distance)
    line_n2.hand_on(1)
    plane_ff[1].spread()
    line_n2.hand_on(2)
    plane_ff[2].spread()
    for distance in range(3, tp):
        line_n2.hand_on(distance)
    for item in plane_ff:
        item.complete()
    for item in [plane_kv, plane_q, plane_o, plane_b] + plane_ff:
        item.finish()
    for item in (line_q, line_o, line_b, line_cot, line_kv, line_n2):
        item.finish()
    for copy in starts[4:] + outs + [n2_copy]:
        copy.wait()
    for part in range(tp):
        for blocks in range(1, tp + 1):

            @pl.when(z == blocks - 1)
            def _():
                probs_copy(part, blocks * own_rows).wait()


def forward_part(dp, tp, kvb_count, qb_count, x, seg_row, seg_col, zq, zo, zb, kvs, ff, cot):
    def shape(*dims, kind=BF16):
        return jax.ShapeDtypeStruct(dims, kind)

    own_rows, width = x.shape
    depth, columns = zq.shape
    items = seg_row.shape[1]
    head = HEAD_DIMENSION
    kv_columns = 2 * KEYVALUE_HEADS * head
    vmem = pl.BlockSpec(memory_space=pltpu.VMEM)
    anywhere = pl.BlockSpec(memory_space=ANY)
    return pl.pallas_call(
        functools.partial(forward_kernel, dp, tp, kvb_count, qb_count),
        out_shape=(
            shape(dp, *ff.shape),
            shape(tp, *cot.shape),
            shape(tp, own_rows, width),
            shape(tp, width, columns),
            shape(tp, width, columns),
            shape(width, kvs.shape[1]),
            shape(QUERY_HEADS, own_rows, items),
            shape(own_rows, width, kind=F32),
            shape(own_rows, tp * columns),
            shape(own_rows, width),
            shape(own_rows, tp * columns),
            shape(items, kv_columns),
            shape(own_rows, head, kind=F32),
            shape(own_rows, head, kind=F32),
            shape(16, width, kind=F32),
        ),
        in_specs=[vmem] * 9,
        out_specs=(anywhere,) * 7 + (vmem,) * 8,
        scratch_shapes=[
            pltpu.VMEM((tp, width, columns), BF16),
            pltpu.VMEM((tp, width, columns), BF16),
            pltpu.VMEM((width, kvs.shape[1]), BF16),
            pltpu.VMEM((dp, tp, 16, 128), BF16),
            pltpu.VMEM((width, kv_columns), BF16),
            pltpu.VMEM((own_rows, items), F32),
            pltpu.VMEM((QUERY_HEADS, own_rows, items), BF16),
            pltpu.VMEM((own_rows, width), BF16),
            pltpu.SemaphoreType.DMA((7, dp)),
            pltpu.SemaphoreType.DMA((7, dp)),
            pltpu.SemaphoreType.DMA((6, 2, tp)),
            pltpu.SemaphoreType.DMA((6, 2, tp)),
            pltpu.SemaphoreType.DMA((6,)),
            pltpu.SemaphoreType.DMA((tp,)),
        ],
        compiler_params=pltpu.CompilerParams(
            collective_id=0, has_side_effects=True, vmem_limit_bytes=56 << 20
        ),
        name="forward_part",
    )(x, seg_row, seg_col, zq, zo, zb, kvs, ff, cot)


class PlaneReduce:
    def __init__(self, place, part, held, send, recv):
        self.place, self.part, self.held, self.send, self.recv = place, part, held, send, recv
        self.half = 1 << place.steps
        self.last = place.steps

    def count(self, level):
        return self.half >> level

    def slot(self, level, i):
        return sum(self.count(k) for k in range(level)) + i

    def copy(self, level, i):
        place = self.place
        slot = self.slot(level, i)
        if level:
            src, device = self.held(self.slot(level - 1, 2 * i + 1)), place.partners[level - 1]
        else:
            src, device = self.part(place.sibling_block(i)), place.sibling
        return remote(
            src, self.held(slot), self.send(slot), self.recv(slot), place.device(device)
        )

    def start(self, level):
        for i in range(self.count(level)):
            self.copy(level, i).start()

    def wait_send(self, level):
        for i in range(self.count(level)):
            self.copy(level, i).wait_send()

    def absorb(self, level, out=None):
        order = sorted(range(self.count(level)), key=lambda i: 1 - i % 2)
        for i in order:
            slot = self.slot(level, i)
            self.copy(level, i).wait_recv()
            if level:
                other = self.held(self.slot(level - 1, 2 * i))
            else:
                other = self.part(self.place.block(i))
            add_into(self.held(slot), other, self.held(slot) if out is None else out)
            if i % 2:
                self.copy(level + 1, i // 2).start()


def add_into(one, other, out):
    rows = one.shape[0]
    step = 48 if rows % 48 == 0 else rows

    def body(k, carry):
        at = pl.ds(pl.multiple_of(k * step, 16), step)
        out[at, :] = (one[at, :].astype(F32) + other[at, :].astype(F32)).astype(out.dtype)
        return carry

    lax.fori_loop(0, rows // step, body, 0)


FF_PARTS = 3


class LineReduce:
    def __init__(self, place, term, sent, got, send, recv):
        self.place, self.term, self.sent, self.got = place, term, sent, got
        self.send, self.recv = send, recv

    def owner(self, turn):
        place = self.place
        if turn == place.tp - 1:
            return place.z
        falling = place.tp - 1 - turn
        falling = jnp.where(falling > place.z, falling, falling - 1)
        rising = jnp.where(turn < place.z, turn, turn + 1)
        return jnp.where(place.z < place.tp // 2, falling, rising)

    def way(self, turn):
        place = self.place
        owner = self.owner(turn)
        right = jnp.where(owner > place.z, 1, 0)
        side, offset = 1 - right, 2 * right - 1
        return side, offset, (owner - place.z) * offset

    def copy(self, turn):
        side, offset, distance = self.way(turn)
        return remote(
            self.sent(turn),
            self.got(side, distance - 1),
            self.send(turn),
            self.recv(side, distance - 1),
            self.place.beside(offset),
        )

    def arrival(self, side, distance):
        ref = self.got(side, distance)
        return remote(
            ref, ref, self.send(0), self.recv(side, distance), self.place.beside(0)
        )

    def step(self, turn):
        side, offset, distance = self.way(turn)
        fed = self.place.has(-offset)

        @pl.when(fed)
        def _():
            self.arrival(side, distance).wait_recv()
            add_into(self.term(turn), self.got(side, distance), self.sent(turn))

        if self.term is not self.sent:

            @pl.when(jnp.logical_not(fed))
            def _():
                copy_into(self.term(turn), self.sent(turn))

        self.copy(turn).start()

    def total(self, out):
        last = self.place.tp - 1
        copy_into(self.term(last), out)
        for side, offset in ((0, -1), (1, 1)):

            @pl.when(self.place.has(offset))
            def _():
                self.arrival(side, 0).wait_recv()
                add_into(out, self.got(side, 0), out)

    def finish(self):
        for turn in range(self.place.tp - 1):
            self.copy(turn).wait_send()


def copy_into(one, out):
    rows = one.shape[0]
    step = 32 if rows % 32 == 0 else rows

    def body(k, carry):
        at = pl.ds(pl.multiple_of(k * step, 16), step)
        out[at, :] = one[at, :].astype(out.dtype)
        return carry

    lax.fori_loop(0, rows // step, body, 0)


def ff_kernel(
    dp, tp, ff, cot, n2, act, lhs, mlp, d2,
    wg, wu, wd, x, ct, made, term, sent, got, branch, turned_rows,
    w_sem, in_sem, act_sem, lhs_sem, mlp_sem, send_sem, recv_sem,
):
    place = Place(dp, tp)
    own_rows, width = d2.shape
    depth = ff.shape[2]
    padded = ff.shape[3]
    tile = 256
    weights = (wg, wu, wd)
    loads = [
        [
            pltpu.make_async_copy(
                ff.at[b, p], weights[p].at[pl.ds(b * depth, depth)], w_sem.at[p, b]
            )
            for b in range(dp)
        ]
        for p in range(FF_PARTS)
    ]
    sums = LineReduce(
        place,
        lambda turn: term.at[turn % 2],
        lambda turn: sent.at[turn],
        lambda side, k: got.at[side, k],
        lambda turn: send_sem.at[turn],
        lambda side, k: recv_sem.at[side, k],
    )

    def fetch(turn):
        owner = sums.owner(turn)
        return [
            pltpu.make_async_copy(n2.at[owner], x.at[turn % 2], in_sem.at[turn % 2, 0]),
            pltpu.make_async_copy(cot.at[owner], ct.at[turn % 2], in_sem.at[turn % 2, 1]),
        ]

    def stores(turn, kinds=(0, 1, 2)):
        return [copies() for kind, copies in enumerate(store_kinds(turn)) if kind in kinds]

    def store_kinds(turn):
        owner = sums.owner(turn)
        at = pl.ds(pl.multiple_of(owner * own_rows, 128), own_rows)
        slot = turn % 2
        return (
            lambda: [
                pltpu.make_async_copy(made.at[slot, p], act.at[p, at], act_sem.at[slot, p])
                for p in range(FF_PARTS)
            ],
            lambda: [
                pltpu.make_async_copy(
                    turned_rows.at[slot, k], lhs.at[k, :, at], lhs_sem.at[slot, k]
                )
                for k in range(2)
            ],
            lambda: [pltpu.make_async_copy(branch.at[slot], mlp.at[owner], mlp_sem.at[slot])],
        )

    for copy in fetch(0):
        copy.start()
    for part in loads:
        for copy in part:
            copy.start()
    place.greet(False, True)
    for turn in range(tp):
        slot = turn % 2
        for copy in fetch(turn):
            copy.wait()
        if turn + 1 < tp:
            for copy in fetch(turn + 1):
                copy.start()
        if turn >= 2:
            for copies in stores(turn - 2):
                for copy in copies:
                    copy.wait()
        turned_rows[slot, 0] = x[slot].T
        turned_rows[slot, 1] = ct[slot].T
        for copy in stores(turn, (1,))[0]:
            copy.start()
        if turn == 0:
            for part in loads:
                for copy in part:
                    copy.wait()

        def units(n, carry, slot=slot):
            for k in range(3):
                at = pl.ds(pl.multiple_of((n * 3 + k) * tile, tile), tile)
                gate = dot(x[slot], wg[:, at])
                upper = dot(x[slot], wu[:, at])
                d_hidden = dot(ct[slot], wd[:, at])
                sigmoid = 1.0 / (1.0 + jnp.exp(-gate))
                swish = gate * sigmoid
                made[slot, 2, :, at] = (swish * upper).astype(BF16)
                made[slot, 1, :, at] = (d_hidden * swish).astype(BF16)
                made[slot, 0, :, at] = (
                    d_hidden * upper * sigmoid * (1.0 + gate * (1.0 - sigmoid))
                ).astype(BF16)
            return carry

        lax.fori_loop(0, padded // (3 * tile), units, 0)

        def columns(n, carry, slot=slot):
            at = pl.ds(pl.multiple_of(n * tile, tile), tile)
            term[slot, :, at] = dot_nt(made[slot, 0], wg[at, :]) + dot_nt(
                made[slot, 1], wu[at, :]
            )
            branch[slot, :, at] = dot_nt(made[slot, 2], wd[at, :]).astype(BF16)
            return carry

        if turn > 0:
            sums.step(turn - 1)
        lax.fori_loop(0, width // tile, columns, 0)
        for copies in stores(turn, (0, 2)):
            for copy in copies:
                copy.start()
    sums.total(d2)
    sums.finish()
    for turn in range(tp - 2, tp):
        for copies in stores(turn):
            for copy in copies:
                copy.wait()


def ff_part(dp, tp, ff, cot, n2):
    def shape(*dims, kind=BF16):
        return jax.ShapeDtypeStruct(dims, kind)

    own_rows, width = cot.shape[1:]
    padded = ff.shape[3]
    vmem = pl.BlockSpec(memory_space=pltpu.VMEM)
    anywhere = pl.BlockSpec(memory_space=ANY)
    return pl.pallas_call(
        functools.partial(ff_kernel, dp, tp),
        out_shape=(
            shape(FF_PARTS, tp * own_rows, padded),
            shape(2, width, tp * own_rows),
            shape(tp, own_rows, width),
            shape(own_rows, width, kind=F32),
        ),
        in_specs=[anywhere] * 3,
        out_specs=(anywhere,) * 3 + (vmem,),
        scratch_shapes=[
            pltpu.VMEM((width, padded), BF16),
            pltpu.VMEM((width, padded), BF16),
            pltpu.VMEM((width, padded), BF16),
            pltpu.VMEM((2, own_rows, width), BF16),
            pltpu.VMEM((2, own_rows, width), BF16),
            pltpu.VMEM((2, FF_PARTS, own_rows, padded), BF16),
            pltpu.VMEM((2, own_rows, width), F32),
            pltpu.VMEM((tp - 1, own_rows, width), BF16),
            pltpu.VMEM((2, tp - 1, own_rows, width), BF16),
            pltpu.VMEM((2, own_rows, width), BF16),
            pltpu.VMEM((2, 2, width, own_rows), BF16),
            pltpu.SemaphoreType.DMA((FF_PARTS, dp)),
            pltpu.SemaphoreType.DMA((2, 2)),
            pltpu.SemaphoreType.DMA((2, FF_PARTS)),
            pltpu.SemaphoreType.DMA((2, 2)),
            pltpu.SemaphoreType.DMA((2,)),
            pltpu.SemaphoreType.DMA((tp - 1,)),
            pltpu.SemaphoreType.DMA((2, tp - 1)),
        ],
        compiler_params=pltpu.CompilerParams(
            collective_id=3, has_side_effects=True, vmem_limit_bytes=60 << 20
        ),
        name="ff_part",
    )(ff, cot, n2)


class DownReduce:
    def __init__(self, place, term, got, send, recv):
        self.place, self.term, self.got, self.send, self.recv = place, term, got, send, recv

    def copy(self, distance):
        return remote(
            self.term(self.place.z - distance),
            self.got(distance - 1),
            self.send(distance),
            self.recv(distance - 1),
            self.place.beside(-1),
        )

    def take(self, distance, out):
        place = self.place

        @pl.when(place.z < place.tp - 1)
        def _():
            ref = self.got(distance)
            remote(
                ref, ref, self.send(distance), self.recv(distance), place.beside(0)
            ).wait_recv()
            add_into(out, ref, out)

    def step(self, distance):
        place = self.place

        @pl.when(place.z >= distance)
        def _():
            if distance < place.tp - 1:
                self.take(distance, self.term(place.z - distance))
            self.copy(distance).start()

    def finish(self):
        for distance in range(1, self.place.tp):

            @pl.when(self.place.z >= distance)
            def _():
                self.copy(distance).wait_send()


def backward_kernel(
    dp, tp, chunk,
    res, vectors, att, q, kv, cosine, sine, d2, cot, x, lhs, act, mlp, probs, wo, wq, wkv,
    out, mlp_sent, mlp_got, d_branch, d_qkv, output, input_grad, vector_grads,
    part, taken, held, left, block, stage, weight, kv_weight, prob, d_att, d_kv, d_kv_low, kv_got,
    acc, wide, own_bf, d_res,
    act_sem, send_sem, recv_sem, left_sem, stage_sem, line_send, line_recv, out_sem, weight_sem,
    prob_sem, kv_send, kv_recv, in_sem,
):
    place = Place(dp, tp)
    z = place.z
    own_rows, width = res.shape
    depth = width // dp
    group = max(1, 384 // depth)
    tile = 256
    head = HEAD_DIMENSION
    scale = 1.0 / math.sqrt(head)
    columns = wq.shape[2]
    heads_width = tp * columns
    half_kv = KEYVALUE_HEADS * head
    per_part = act.shape[2] // chunk
    units = [(p, k) for p in (2, 0, 1) for k in range(per_part)]

    def fetch(u):
        p, k = units[u]
        return pltpu.make_async_copy(
            act.at[p, :, pl.ds(k * chunk, chunk)], taken.at[u % 2], act_sem.at[u % 2]
        )

    def fetch_left(k):
        return pltpu.make_async_copy(lhs.at[k], left, left_sem.at[0])

    def fetch_weight(n):
        source = wo if n < tp else wq
        return pltpu.make_async_copy(source.at[n % tp], weight.at[n % 2], weight_sem.at[n % 2])

    def fetch_probs(h, slot):
        return pltpu.make_async_copy(probs.at[h], prob.at[slot], prob_sem.at[slot])

    d2_copy = pltpu.make_async_copy(d2, wide, in_sem.at[0])
    cot_copy = pltpu.make_async_copy(cot, own_bf, in_sem.at[1])
    x_copy = pltpu.make_async_copy(x, own_bf, in_sem.at[2])
    kv_weight_copy = pltpu.make_async_copy(
        wkv.at[:, pl.ds(0, 2 * half_kv)], kv_weight, in_sem.at[3]
    )
    fetch_left(1).start()
    fetch(0).start()
    for copy in (d2_copy, cot_copy, fetch_weight(0), fetch_weight(1), kv_weight_copy):
        copy.start()
    for h in range(2):
        fetch_probs(h, h).start()
    place.greet(True, True)

    line = LineReduce(
        place,
        None,
        lambda turn: mlp_sent.at[turn],
        lambda side, k: mlp_got.at[side, k],
        lambda turn: line_send.at[turn],
        lambda side, k: line_recv.at[side, k],
    )

    def load_term(turn):
        return pltpu.make_async_copy(mlp.at[line.owner(turn)], stage.at[0], stage_sem.at[0])

    def load_got(side, distance):
        return pltpu.make_async_copy(mlp_got.at[side, distance], stage.at[1], stage_sem.at[1])

    def line_direct(turn):
        side, offset, distance = line.way(turn)

        @pl.when(jnp.logical_not(place.has(-offset)))
        def _():
            remote(
                mlp.at[line.owner(turn)],
                mlp_got.at[side, distance - 1],
                line_send.at[turn],
                line_recv.at[side, distance - 1],
                place.beside(offset),
            ).start()

    def line_step(turn):
        side, offset, distance = line.way(turn)

        @pl.when(place.has(-offset))
        def _():
            load_term(turn).start()
            line.arrival(side, distance).wait_recv()
            load_got(side, distance).start()
            load_term(turn).wait()
            load_got(side, distance).wait()
            add_into(stage.at[0], stage.at[1], stage.at[0])
            store = pltpu.make_async_copy(stage.at[0], mlp_sent.at[turn], stage_sem.at[0])
            store.start()
            store.wait()
            line.copy(turn).start()

    def line_total():
        load_term(tp - 1).start()
        load_term(tp - 1).wait()
        add_into(res, stage.at[0], d_res)
        for side, offset in ((0, -1), (1, 1)):

            @pl.when(place.has(offset))
            def _():
                line.arrival(side, 0).wait_recv()
                load_got(side, 0).start()
                load_got(side, 0).wait()
                add_into(d_res, stage.at[1], d_res)

        copy_into(d_res, output)

    for turn in range(tp - 1):
        line_direct(turn)
    down = DownReduce(
        place,
        lambda r: d_kv_low.at[pl.ds(pl.multiple_of(r * own_rows, 16), own_rows)],
        lambda k: kv_got.at[k],
        lambda k: kv_send.at[k],
        lambda k: kv_recv.at[k],
    )

    def second_norm():
        d2_copy.wait()
        cot_copy.wait()
        values, grad = res[...], wide[...]
        s = rms_scale(values)
        normed = values * s
        weighted = grad * vectors[1:2, :]
        inner = jnp.mean(weighted * normed, axis=1, keepdims=True)
        found = own_bf[...].astype(F32) + s * (weighted - normed * inner)
        d_res[...] = found
        d_branch[...] = found.astype(BF16)
        vector_grads[...] = jnp.zeros_like(vector_grads)
        vector_grads[1:2, :] = jnp.sum(grad * normed, axis=0, keepdims=True)
        x_copy.start()
        d_kv[...] = jnp.zeros_like(d_kv)

    def attended_grad(ts):
        for t in ts:
            fetch_weight(t).wait()
            d_att[:, t * columns : (t + 1) * columns] = dot(d_branch[...], weight[t % 2]).astype(
                BF16
            )
            fetch_weight(t + 2).start()

    def some_heads(begin, end):
        def one_head(h, carry):
            slot = h % 2
            at = pl.ds(pl.multiple_of(h * head, head), head)
            shared = h // REPEAT
            key_at = pl.ds(pl.multiple_of(shared * head, head), head)
            value_at = pl.ds(pl.multiple_of(half_kv + shared * head, head), head)
            fetch_probs(h, slot).wait()
            d_out = d_att[:, at]
            inner = jnp.sum(
                d_out.astype(F32) * att[:, at].astype(F32), axis=1, keepdims=True
            )
            acc[...] = jnp.zeros_like(acc)

            def one_block(j, carry):
                rows = pl.ds(pl.multiple_of(j * own_rows, 256), own_rows)
                low = prob[slot, :, rows]
                d_probs = dot_nt(d_out, kv[rows, value_at])
                d_scores = (low.astype(F32) * (scale * (d_probs - inner))).astype(BF16)
                acc[...] += dot(d_scores, kv[rows, key_at])
                d_kv[rows, key_at] += dot_tn(d_scores, q[:, at])
                d_kv[rows, value_at] += dot_tn(low, d_out)
                return carry

            lax.fori_loop(0, z + 1, one_block, 0)
            d_qkv[:, at] = turned(acc[...], cosine[...], -sine[...]).astype(BF16)

            @pl.when(h + 2 < QUERY_HEADS)
            def _():
                fetch_probs(h + 2, slot).start()

            return carry

        lax.fori_loop(begin, end, one_head, 0)

    def send_kv():
        def body(j, carry):
            rows = pl.ds(pl.multiple_of(j * own_rows, 256), own_rows)
            d_kv_low[rows, :] = d_kv[rows, :].astype(BF16)
            return carry

        lax.fori_loop(0, z + 1, body, 0)
        down.step(tp - 1)
        for distance in range(tp - 2, 0, -1):
            down.step(distance)

    def normed_grad(ts):
        for t in ts:
            fetch_weight(tp + t).wait()
            for j in range(width // 512):
                cut = slice(j * 512, (j + 1) * 512)
                found = dot_nt(
                    d_qkv[:, t * columns : (t + 1) * columns], weight[(tp + t) % 2, cut, :]
                )
                wide[:, cut] = found + wide[:, cut] if t else found
            if t + 2 < tp:
                fetch_weight(tp + t + 2).start()

    def first_norm():
        mine = pl.ds(pl.multiple_of(z * own_rows, 16), own_rows)
        down.take(0, d_kv.at[mine])
        for h in range(KEYVALUE_HEADS):
            cut = slice(h * head, (h + 1) * head)
            d_qkv[:, heads_width + h * head : heads_width + (h + 1) * head] = turned(
                d_kv[mine, cut], cosine[...], -sine[...]
            ).astype(BF16)
        d_qkv[:, heads_width + half_kv :] = d_kv[mine, half_kv:].astype(BF16)
        kv_weight_copy.wait()
        for j in range(width // 512):
            cut = slice(j * 512, (j + 1) * 512)
            wide[:, cut] += dot_nt(d_qkv[:, heads_width:], kv_weight[cut, :])
        x_copy.wait()
        values, grad = own_bf[...].astype(F32), wide[...]
        s = rms_scale(values)
        normed = values * s
        weighted = grad * vectors[0:1, :]
        inner = jnp.mean(weighted * normed, axis=1, keepdims=True)
        input_grad[...] = (d_res[...] + s * (weighted - normed * inner)).astype(BF16)
        vector_grads[0:1, :] = jnp.sum(grad * normed, axis=0, keepdims=True)
        sums_of = jnp.sum(d_qkv[...].astype(F32), axis=0, keepdims=True)
        vector_grads[2:3, :] = sums_of[:, :heads_width]
        vector_grads[3:4, : 2 * half_kv] = sums_of[:, heads_width:]

    per = QUERY_HEADS // tp
    pieces = [
        [second_norm, lambda: attended_grad(range(tp))],
        [lambda: some_heads(0, 2)],
        [lambda: some_heads(2, 4), lambda: line_step(0)],
        [lambda: some_heads(4, 6)],
        [lambda: some_heads(6, 8), lambda: line_step(1)],
        [lambda: some_heads(8, 10), lambda: line_step(2)],
        [lambda: some_heads(10, 12), send_kv],
        [lambda: normed_grad(range(tp))],
        [],
        [first_norm],
        [line_total],
    ]

    def stored(u):
        p, k = units[u]
        return pltpu.make_async_copy(
            block.at[u % 2], out.at[p, :, pl.ds(k * chunk, chunk)], out_sem.at[u % 2]
        )

    sums = [
        PlaneReduce(
            place,
            lambda b, u=u: part.at[u % 2, b],
            lambda s, u=u: held.at[u, s],
            lambda s, u=u: send_sem.at[u, s],
            lambda s, u=u: recv_sem.at[u, s],
        )
        for u in range(len(units))
    ]
    last = place.steps
    fetch_left(1).wait()
    for turn in range(max(len(units) + last + 1, len(pieces))):
        if turn < len(units):
            u = turn
            p, k = units[u]
            if u + 1 < len(units):
                fetch(u + 1).start()
            if u == per_part:
                fetch_left(0).wait()
            fetch(u).wait()
            if u >= 2:
                sums[u - 2].wait_send(0)

            def body(n, carry, u=u):
                i, j = n // (chunk // tile), n % (chunk // tile)
                rows = pl.ds(pl.multiple_of(i * (group * depth), 16), group * depth)
                cols = pl.ds(pl.multiple_of(j * tile, tile), tile)
                found = dot(left[rows, :], taken[u % 2, :, cols]).astype(BF16)
                for g in range(group):
                    part[u % 2, i * group + g, :, cols] = found[g * depth : (g + 1) * depth]
                return carry

            lax.fori_loop(0, dp // group * (chunk // tile), body, 0)
            sums[u].start(0)
            if u == per_part - 1:
                fetch_left(0).start()
        for level in range(last + 1):
            u = turn - 1 - level
            if 0 <= u < len(units):
                if level == last:
                    if u >= 2:
                        stored(u - 2).wait()
                    sums[u].absorb(level, block.at[u % 2])
                    stored(u).start()
                else:
                    sums[u].absorb(level)
        if turn < len(pieces):
            for piece in pieces[turn]:
                piece()
    line.finish()
    down.finish()
    for u in range(len(units)):
        if u >= len(units) - 2:
            stored(u).wait()
        for level in range(0 if u >= len(units) - 2 else 1, last + 1):
            sums[u].wait_send(level)


def backward_part(
    dp, tp, res, vectors, att, q, kv, cosine, sine, d2, cot, x, lhs, act, mlp, probs, wo, wq, wkv
):
    def shape(*dims, kind=BF16):
        return jax.ShapeDtypeStruct(dims, kind)

    own_rows, width = res.shape
    depth = width // dp
    items, padded = act.shape[1:]
    columns = wq.shape[2]
    kv_columns = kv.shape[1]
    chunk = 768
    count = FF_PARTS * padded // chunk
    vmem = pl.BlockSpec(memory_space=pltpu.VMEM)
    anywhere = pl.BlockSpec(memory_space=ANY)
    return pl.pallas_call(
        functools.partial(backward_kernel, dp, tp, chunk),
        out_shape=(
            shape(FF_PARTS, depth, padded, kind=F32),
            shape(tp - 1, own_rows, width),
            shape(2, tp - 1, own_rows, width),
            shape(own_rows, width),
            shape(own_rows, tp * columns + kv_columns),
            shape(own_rows, width),
            shape(own_rows, width),
            shape(8, width, kind=F32),
        ),
        in_specs=[vmem] * 7 + [anywhere] * 10,
        out_specs=(anywhere,) * 3 + (vmem,) * 5,
        scratch_shapes=[
            pltpu.VMEM((2, dp, depth, chunk), BF16),
            pltpu.VMEM((2, items, chunk), BF16),
            pltpu.VMEM((count, dp - 1, depth, chunk), BF16),
            pltpu.VMEM((width, items), BF16),
            pltpu.VMEM((2, depth, chunk), F32),
            pltpu.VMEM((2, own_rows, width), BF16),
            pltpu.VMEM((2, width, columns), BF16),
            pltpu.VMEM((width, kv_columns), BF16),
            pltpu.VMEM((2, own_rows, items), BF16),
            pltpu.VMEM((own_rows, tp * columns), BF16),
            pltpu.VMEM((items, kv_columns), F32),
            pltpu.VMEM((items, kv_columns), BF16),
            pltpu.VMEM((tp - 1, own_rows, kv_columns), BF16),
            pltpu.VMEM((own_rows, HEAD_DIMENSION), F32),
            pltpu.VMEM((own_rows, width), F32),
            pltpu.VMEM((own_rows, width), BF16),
            pltpu.VMEM((own_rows, width), F32),
            pltpu.SemaphoreType.DMA((2,)),
            pltpu.SemaphoreType.DMA((count, dp - 1)),
            pltpu.SemaphoreType.DMA((count, dp - 1)),
            pltpu.SemaphoreType.DMA((1,)),
            pltpu.SemaphoreType.DMA((2,)),
            pltpu.SemaphoreType.DMA((tp - 1,)),
            pltpu.SemaphoreType.DMA((2, tp - 1)),
            pltpu.SemaphoreType.DMA((2,)),
            pltpu.SemaphoreType.DMA((2,)),
            pltpu.SemaphoreType.DMA((2,)),
            pltpu.SemaphoreType.DMA((tp,)),
            pltpu.SemaphoreType.DMA((tp - 1,)),
            pltpu.SemaphoreType.DMA((4,)),
        ],
        compiler_params=pltpu.CompilerParams(
            collective_id=1, has_side_effects=True, vmem_limit_bytes=63 << 20
        ),
        name="backward_part",
    )(res, vectors, att, q, kv, cosine, sine, d2, cot, x, lhs, act, mlp, probs, wo, wq, wkv)


def attn_grad_kernel(
    dp, tp, widths, n1, d_qkv, d_branch, att, vectors, kv_out, q_out, o_out, vectors_out,
    turned_rows, part, held, own, line_kv, line_qo, vector_sum, vector_got, line_vector,
    send_sem, recv_sem, line_send, line_recv, vector_send, vector_recv,
):
    place = Place(dp, tp)
    z = place.z
    depth, columns = q_out.shape
    width = dp * depth
    heads_width = tp * columns
    barrier = pltpu.get_barrier_semaphore()
    for partner in place.partners + [place.sibling]:
        pl.semaphore_signal(barrier, inc=1, device_id=place.device(partner), device_id_type=MESH)
    for t in range(tp):

        @pl.when(t != z)
        def _():
            pl.semaphore_signal(barrier, inc=1, device_id=(place.d, t), device_id_type=MESH)

    pl.semaphore_wait(barrier, place.steps + tp)
    kinds = (0, 0, 2, 1, 1)
    halves = (0, 1, 0, 0, 1)
    count = len(widths)
    group = max(1, 384 // depth)
    sums = [
        PlaneReduce(
            place,
            lambda b, u=u: part.at[u, b, :, pl.ds(0, widths[u])],
            lambda s, u=u: held.at[u, s, :, pl.ds(0, widths[u])],
            lambda s, u=u: send_sem.at[u, s],
            lambda s, u=u: recv_sem.at[u, s],
        )
        for u in range(count)
    ]

    def make(u):
        kind, half = kinds[u], halves[u]
        left = 1 if kind == 1 else 0
        right = att if kind == 1 else d_qkv
        base = heads_width if kind == 2 else half * widths[u]

        def body(i, carry):
            rows = pl.ds(pl.multiple_of(i * (group * depth), 16), group * depth)
            for j in range(widths[u] // 256):
                found = dot(
                    turned_rows[left, rows, :], right[:, base + j * 256 : base + (j + 1) * 256]
                ).astype(BF16)
                for g in range(group):
                    part[u, i * group + g, :, j * 256 : (j + 1) * 256] = found[
                        g * depth : (g + 1) * depth
                    ]
            return carry

        lax.fori_loop(0, dp // group, body, 0)
        sums[u].start(0)

    def line_copies(u):
        found = []
        kind, half = kinds[u], halves[u]
        for t in range(tp):
            if kind == 2:
                src, dst = own.at[u, :, pl.ds(0, widths[u])], line_kv.at[z]
            elif t // 2 == half:
                src, dst = own.at[u, :, pl.ds((t % 2) * columns, columns)], line_qo.at[kind, z]
            else:
                continue
            found.append((t, remote(
                src, dst, line_send.at[u, t], line_recv.at[kind, z], (place.d, t)
            )))
        return found

    last = place.steps

    def work(turn):
        for level in range(last + 1):
            u = turn - level
            if 0 <= u < count:
                target = own.at[u, :, pl.ds(0, widths[u])] if level == last else None
                sums[u].absorb(level, target)
                if level == last:
                    for t, copy in line_copies(u):

                        @pl.when(t != z)
                        def _():
                            copy.start()

    ways = [place.sibling] + place.partners

    def vector_copy(level):
        return remote(
            vectors if level == 0 else vector_sum.at[level - 1],
            vector_got.at[level],
            vector_send.at[level],
            vector_recv.at[level],
            place.device(ways[level]),
        )

    def vector_step(level):
        vector_copy(level).wait_recv()
        mine = vectors[...] if level == 0 else vector_sum[level - 1]
        vector_sum[level] = mine + vector_got[level]
        if level < last:
            vector_copy(level + 1).start()
        else:
            for t in range(tp):

                @pl.when(t != z)
                def _():
                    vector_line(t).start()

    def vector_line(t):
        return remote(
            vector_sum.at[last],
            line_vector.at[z],
            line_send.at[count, t],
            line_recv.at[3, z],
            (place.d, t),
        )

    vector_copy(0).start()
    turned_rows[0] = n1[...].T
    make(0)
    make(1)
    turned_rows[1] = d_branch[...].T
    for u in range(2, count):
        make(u)
    for turn in range(count + last):
        work(turn)
        if turn <= last:
            vector_step(turn)

    def arrived(ref, kind):
        for t in range(tp):

            @pl.when(t != z)
            def _():
                remote(
                    ref.at[t], ref.at[t], line_send.at[0, t], line_recv.at[kind, t], (place.d, t)
                ).wait_recv()

    def total(ref, mine, out):
        acc = mine.astype(F32)
        for t in range(tp):
            acc = acc + jnp.where(t != z, ref[t].astype(F32), 0.0)
        out[...] = acc

    at = pl.ds(pl.multiple_of((z % 2) * columns, 128), columns)
    arrived(line_vector, 3)
    total(line_vector, vector_sum[last], vectors_out)
    arrived(line_qo.at[0], 0)
    total(line_qo.at[0], own[z // 2, :, at], q_out)
    arrived(line_kv, 2)
    total(line_kv, own[2, :, : widths[2]], kv_out)
    arrived(line_qo.at[1], 1)
    total(line_qo.at[1], own[3 + z // 2, :, at], o_out)
    for u in range(count):
        for level in range(last + 1):
            sums[u].wait_send(level)
        for t, copy in line_copies(u):

            @pl.when(t != z)
            def _():
                copy.wait_send()

    for level in range(last + 1):
        vector_copy(level).wait_send()
    for t in range(tp):

        @pl.when(t != z)
        def _():
            vector_line(t).wait_send()


def attn_grads(dp, tp, n1, d_qkv, d_branch, att, vectors):
    own_rows, width = n1.shape
    depth = width // dp
    heads_width = att.shape[1]
    kv_columns = d_qkv.shape[1] - heads_width
    half = heads_width // 2
    widths = (half, half, kv_columns, half, half)
    columns = heads_width // tp
    levels = dp.bit_length() - 1
    vmem = pl.BlockSpec(memory_space=pltpu.VMEM)
    return pl.pallas_call(
        functools.partial(attn_grad_kernel, dp, tp, widths),
        out_shape=(
            jax.ShapeDtypeStruct((depth, kv_columns), F32),
            jax.ShapeDtypeStruct((depth, columns), F32),
            jax.ShapeDtypeStruct((depth, columns), F32),
            jax.ShapeDtypeStruct(vectors.shape, F32),
        ),
        in_specs=[vmem] * 5,
        out_specs=(vmem,) * 4,
        scratch_shapes=[
            pltpu.VMEM((2, width, own_rows), BF16),
            pltpu.VMEM((5, dp, depth, half), BF16),
            pltpu.VMEM((5, dp - 1, depth, half), BF16),
            pltpu.VMEM((5, depth, half), BF16),
            pltpu.VMEM((tp, depth, kv_columns), BF16),
            pltpu.VMEM((2, tp, depth, columns), BF16),
            pltpu.VMEM((levels,) + vectors.shape, F32),
            pltpu.VMEM((levels,) + vectors.shape, F32),
            pltpu.VMEM((tp,) + vectors.shape, F32),
            pltpu.SemaphoreType.DMA((5, dp - 1)),
            pltpu.SemaphoreType.DMA((5, dp - 1)),
            pltpu.SemaphoreType.DMA((6, tp)),
            pltpu.SemaphoreType.DMA((4, tp)),
            pltpu.SemaphoreType.DMA((levels,)),
            pltpu.SemaphoreType.DMA((levels,)),
        ],
        compiler_params=pltpu.CompilerParams(
            collective_id=2, has_side_effects=True, vmem_limit_bytes=56 << 20
        ),
        name="attn_grads",
    )(n1, d_qkv, d_branch, att, vectors)


def local(
    inputs,
    segment_ids,
    first_gain,
    query_weight,
    query_bias,
    key_value_weight,
    key_value_bias,
    output_weight,
    second_gain,
    gateup_weight,
    down_weight,
    cotangent,
):
    dp = lax.axis_size("dp")
    tp = lax.axis_size("tensor")
    rank = lax.axis_index("tensor")
    width = inputs.shape[1]
    own_rows = inputs.shape[0]
    depth = query_weight.shape[0]
    columns = query_weight.shape[1]
    kv_columns = key_value_weight.shape[1]
    hidden_units = gateup_weight.shape[2]
    heads_width = columns * tp
    head = HEAD_DIMENSION
    scale = 1.0 / math.sqrt(head)

    padded = -(-hidden_units // 256) * 256
    ff_own = jnp.stack([gateup_weight[0], gateup_weight[1], down_weight.T])
    ff_own = jnp.pad(ff_own, ((0, 0), (0, 0), (0, padded - hidden_units)))
    qb_count, kvb_count = query_bias.shape[0], key_value_bias.shape[0]
    own_kvbias = jnp.pad(key_value_bias, (0, depth - kvb_count))
    side = jnp.pad(jnp.stack([first_gain, second_gain, own_kvbias], axis=1), ((0, 0), (0, 125)))
    own_segments = lax.dynamic_slice_in_dim(segment_ids, rank * own_rows, own_rows, 0)
    (
        ff_all, grad_rows, second_rows, wq, wo, wkv, probs_low,
        residual, attended, normed_own, rot_query, all_kv, cosine, sine, vectors,
    ) = forward_part(
        dp,
        tp,
        kvb_count,
        qb_count,
        inputs,
        segment_ids[None, :],
        own_segments[:, None],
        query_weight,
        output_weight.T,
        jnp.pad(query_bias[None, :], ((0, 15), (0, 128 - qb_count))),
        jnp.concatenate([key_value_weight, side], axis=1),
        ff_own,
        cotangent,
    )
    act, lhs, mlp_terms, d_second = ff_part(dp, tp, ff_all, grad_rows, second_rows)
    ff_sh, _, _, d_branch, d_qkv, output, input_grad, vector_grads = backward_part(
        dp, tp, residual, vectors, attended, rot_query, all_kv, cosine, sine,
        d_second, cotangent, inputs, lhs, act, mlp_terms, probs_low, wo, wq, wkv,
    )
    kv_sh, q_sh, o_sh, small = attn_grads(
        dp, tp, normed_own, d_qkv, d_branch, attended, vector_grads
    )
    d = lax.axis_index("dp")

    def mine(row, count, index):
        return lax.dynamic_slice_in_dim(row, index * count, count, 0)

    return (
        output,
        input_grad,
        mine(small[0], depth, d),
        q_sh,
        mine(small[2], qb_count, rank * dp + d),
        kv_sh,
        mine(small[3], kvb_count, d),
        o_sh.T,
        mine(small[1], depth, d),
        ff_sh[:2, :, :hidden_units],
        ff_sh[2, :, :hidden_units].T,
    )


def solution(mesh):
    in_specs = (
        P(("dp", "tensor"), None),
        P("dp"),
        P("dp"),
        P("dp", "tensor"),
        P(("tensor", "dp")),
        P("dp", None),
        P("dp"),
        P("tensor", "dp"),
        P("dp"),
        P(None, "dp", "tensor"),
        P("tensor", "dp"),
        P(("dp", "tensor"), None),
    )
    out_specs = (
        P(("dp", "tensor"), None),
        P(("dp", "tensor"), None),
        P("dp"),
        P("dp", "tensor"),
        P(("tensor", "dp")),
        P("dp", None),
        P("dp"),
        P("tensor", "dp"),
        P("dp"),
        P(None, "dp", "tensor"),
        P("tensor", "dp"),
    )
    return jax.shard_map(local, mesh=mesh, in_specs=in_specs, out_specs=out_specs, check_vma=False)
```

```python
import functools
import math

import jax
import jax.numpy as jnp
from jax import lax
from jax.experimental import pallas as pl
from jax.experimental.pallas import tpu as pltpu
from jax.sharding import PartitionSpec as P

QUERY_HEADS = 12
KEYVALUE_HEADS = 2
HEAD_DIMENSION = 128
REPEAT = QUERY_HEADS // KEYVALUE_HEADS

EPSILON = 1e-06
THETA = 1000000.0
NEGATIVE = -1e30

F32 = jnp.float32
BF16 = jnp.bfloat16


def rms_scale(rows):
    return lax.rsqrt(jnp.mean(rows * rows, axis=-1, keepdims=True) + EPSILON)


def norm_back(rows, gain, grad):
    scale = rms_scale(rows)
    normed = rows * scale
    weighted = grad * gain
    inner = jnp.mean(weighted * normed, axis=-1, keepdims=True)
    return (scale * (weighted - normed * inner), jnp.sum(grad * normed, axis=0))


def rope_tables(segments, head_extent):
    index = jnp.arange(segments.shape[0], dtype=jnp.int32)
    starts = jnp.concatenate([jnp.ones((1,), dtype=bool), segments[1:] != segments[:-1]])
    first = lax.cummax(jnp.where(starts, index, jnp.zeros_like(index)), axis=0)
    placed = (index - first).astype(F32)
    freqs = jnp.exp(
        jnp.arange(head_extent // 2, dtype=F32) * (-2.0 * math.log(THETA) / head_extent)
    )
    return placed, freqs


def apply_rotation(value_rows, cosine_table, sine_table):
    half = value_rows.shape[-1] // 2
    former = value_rows[..., :half]
    latter = value_rows[..., half:]
    return jnp.concatenate(
        [former * cosine_table - latter * sine_table, latter * cosine_table + former * sine_table],
        axis=-1,
    )


def unrotate(grads, cosine_table, sine_table):
    return apply_rotation(grads, cosine_table, -sine_table)


def dot(left, right):
    return jnp.dot(left, right, preferred_element_type=F32)


def dot_nt(left, right):
    return lax.dot_general(left, right, (((1,), (1,)), ((), ())), preferred_element_type=F32)


def dot_tn(left, right):
    return lax.dot_general(left, right, (((0,), (0,)), ((), ())), preferred_element_type=F32)


MESH = pl.DeviceIdType.MESH
ANY = pl.ANY


def flip(index, bit):
    return index + (1 << bit) * (1 - 2 * ((index // (1 << bit)) % 2))


class Place:
    def __init__(self, dp, tp):
        self.dp, self.tp = dp, tp
        self.d, self.z = lax.axis_index("dp"), lax.axis_index("tensor")
        self.steps = dp.bit_length() - 2
        odd = self.d % 2
        self.partners = []
        for step in range(self.steps):
            first, other = flip(self.d, 1 + step), flip(self.d, self.steps - step)
            self.partners.append(first + odd * (other - first))
        self.sibling = flip(self.d, 0)
        self.deltas = [partner - self.d for partner in self.partners]

    def block(self, mask):
        index = self.d
        for step in range(self.steps):
            if (mask >> step) & 1:
                index = index + self.deltas[step]
        return index

    def sibling_block(self, mask):
        index = self.sibling
        for step in range(self.steps):
            if (mask >> step) & 1:
                index = index + self.deltas[self.steps - 1 - step]
        return index

    def device(self, index):
        return (index, self.z)

    def beside(self, offset):
        return (self.d, self.z + offset)

    def greet(self, plane, line):
        barrier = pltpu.get_barrier_semaphore()
        count = 0
        if plane:
            for partner in self.partners + [self.sibling]:
                pl.semaphore_signal(
                    barrier, inc=1, device_id=self.device(partner), device_id_type=MESH
                )
            count = self.steps + 1
        if line:
            for offset in (-1, 1):

                @pl.when(self.has(offset))
                def _():
                    pl.semaphore_signal(
                        barrier, inc=1, device_id=self.beside(offset), device_id_type=MESH
                    )

            count = count + jnp.where(self.z > 0, 1, 0) + jnp.where(self.z < self.tp - 1, 1, 0)
        pl.semaphore_wait(barrier, count)

    def has(self, offset):
        return (self.z + offset >= 0) & (self.z + offset < self.tp)


def remote(src, dst, send, recv, device):
    return pltpu.make_async_remote_copy(
        src_ref=src, dst_ref=dst, send_sem=send, recv_sem=recv, device_id=device, device_id_type=MESH
    )


class PlaneGather:
    def __init__(self, place, own, full, send, recv):
        self.place, self.own, self.full, self.send, self.recv = place, own, full, send, recv
        self.half = 1 << place.steps

    def at(self, mask):
        return self.full(self.place.block(mask)) if mask else self.own

    def copy(self, mask, step):
        place = self.place
        if step < place.steps:
            label, device = mask | (1 << step), place.device(place.partners[step])
        else:
            label, device = self.half + mask, place.device(place.sibling)
        return remote(
            self.at(mask), self.full(place.block(mask)), self.send(label), self.recv(label), device
        )

    def arrival(self, label):
        place = self.place
        if label < self.half:
            ref = self.full(place.block(label))
        else:
            ref = self.full(place.sibling_block(label - self.half))
        return remote(ref, ref, self.send(label), self.recv(label), place.device(place.sibling))

    def sends(self, mask):
        return [self.copy(mask, step) for step in range(mask.bit_length(), self.place.steps + 1)]

    def start(self):
        for copy in self.sends(0):
            copy.start()

    def hand_on(self, mask):
        self.arrival(mask).wait_recv()
        for copy in self.sends(mask):
            copy.start()

    def spread(self):
        for mask in range(1, self.half):
            self.hand_on(mask)

    def complete(self):
        for mask in range(self.half):
            self.arrival(self.half + mask).wait_recv()

    def finish(self):
        for mask in range(self.half):
            for copy in self.sends(mask):
                copy.wait_send()


class LineGather:
    def __init__(self, place, own, full, send, recv, offsets=(1, -1)):
        self.place, self.own, self.full, self.send, self.recv = place, own, full, send, recv
        self.offsets = offsets

    def copy(self, distance, offset):
        place = self.place
        source = place.z - offset * distance
        side = 0 if offset > 0 else 1
        src = self.full(source) if distance else self.own
        return remote(
            src,
            self.full(source),
            self.send(side, distance),
            self.recv(side, distance),
            place.beside(offset),
        )

    def each(self, distance, act):
        place = self.place
        for offset in self.offsets:

            @pl.when(place.has(-offset * distance) & place.has(offset))
            def _():
                act(self.copy(distance, offset))

    def start(self):
        self.each(0, lambda copy: copy.start())

    def arrived(self, distance):
        place = self.place
        for offset in self.offsets:

            @pl.when(place.has(-offset * distance))
            def _():
                side = 0 if offset > 0 else 1
                ref = self.full(place.z - offset * distance)
                remote(
                    ref,
                    ref,
                    self.send(side, distance - 1),
                    self.recv(side, distance - 1),
                    place.beside(-offset),
                ).wait_recv()

    def hand_on(self, distance):
        self.arrived(distance)
        if distance < self.place.tp - 1:
            self.each(distance, lambda copy: copy.start())

    def finish(self):
        for distance in range(self.place.tp - 1):
            self.each(distance, lambda copy: copy.wait_send())


def turned(rows, cosine, sine):
    return rows * cosine + pltpu.roll(rows, rows.shape[1] // 2, 1) * sine


def forward_kernel(
    dp, tp, kvb_count, qb_count,
    x, seg_row, seg_col, zq, zo, zb, kvs, ff, cot,
    ff_out, cot_out, n2_out, wq_out, wo_out, wkv_out, p_out,
    res, att, n1, q, kv, cosine, sine, vectors,
    wq, wo, wkv, wb, spread, mask, probs, n2,
    plane_send, plane_recv, line_send, line_recv, local_sem, probs_sem,
):
    place = Place(dp, tp)
    d, z = place.d, place.z
    own_rows, width = x.shape
    depth, columns = zq.shape
    items = seg_row.shape[1]
    head = HEAD_DIMENSION
    kv_columns = kv.shape[1]
    my_rows = pl.ds(pl.multiple_of(d * depth, 16), depth)

    def rows_of(b):
        return pl.ds(pl.multiple_of(b * depth, 16), depth)

    def plane(item, own, full):
        return PlaneGather(
            place, own, full, lambda m: plane_send.at[item, m], lambda m: plane_recv.at[item, m]
        )

    def line(item, own, full, offsets=(1, -1)):
        return LineGather(
            place,
            own,
            full,
            lambda s, k: line_send.at[item, s, k],
            lambda s, k: line_recv.at[item, s, k],
            offsets,
        )

    starts = [
        pltpu.make_async_copy(zq, wq.at[z, my_rows], local_sem.at[0]),
        pltpu.make_async_copy(zo, wo.at[z, my_rows], local_sem.at[1]),
        pltpu.make_async_copy(zb, wb.at[d, z], local_sem.at[2]),
        pltpu.make_async_copy(kvs, wkv.at[my_rows], local_sem.at[3]),
        pltpu.make_async_copy(ff, ff_out.at[d], local_sem.at[4]),
        pltpu.make_async_copy(cot, cot_out.at[z], local_sem.at[5]),
    ]
    for copy in starts:
        copy.start()
    place.greet(True, True)
    line_q = line(0, zq, lambda t: wq.at[t, my_rows])
    line_o = line(1, zo, lambda t: wo.at[t, my_rows])
    line_b = line(2, zb, lambda t: wb.at[d, t])
    line_cot = line(3, cot, lambda t: cot_out.at[t])
    line_kv = line(
        4,
        kv.at[pl.ds(pl.multiple_of(z * own_rows, 16), own_rows)],
        lambda t: kv.at[pl.ds(pl.multiple_of(t * own_rows, 16), own_rows)],
        (1,),
    )
    line_n2 = line(5, n2, lambda t: n2_out.at[t])
    plane_kv = plane(0, kvs, lambda b: wkv.at[rows_of(b)])
    plane_q = plane(1, wq.at[:, my_rows], lambda b: wq.at[:, rows_of(b)])
    plane_o = plane(2, wo.at[:, my_rows], lambda b: wo.at[:, rows_of(b)])
    plane_b = plane(3, wb.at[d], lambda b: wb.at[b])
    plane_ff = [
        plane(4 + part, ff.at[part], lambda b, part=part: ff_out.at[b, part]) for part in (2, 0, 1)
    ]
    line_b.start()
    line_q.start()
    plane_kv.start()

    begin = z * own_rows
    row_at = begin + lax.broadcasted_iota(jnp.int32, (own_rows, items), 0)
    col_at = lax.broadcasted_iota(jnp.int32, (own_rows, items), 1)
    mine, theirs = seg_col[...], seg_row[...]
    allowed = (mine == theirs) & (col_at <= row_at)
    mask[...] = jnp.where(allowed, 0.0, NEGATIVE)
    below = jnp.sum(jnp.where(theirs < mine, 1.0, 0.0), axis=1, keepdims=True)
    lane = lax.broadcasted_iota(jnp.int32, (own_rows, head), 1)
    half = lane % (head // 2)
    index = begin + lax.broadcasted_iota(jnp.int32, (own_rows, head), 0)
    freqs = jnp.exp(half.astype(F32) * (-2.0 * math.log(THETA) / head))
    angles = (index.astype(F32) - below) * freqs
    cosine[...] = jnp.cos(angles)
    sine[...] = jnp.sin(angles) * jnp.where(lane < head // 2, -1.0, 1.0)

    for distance in range(1, tp):
        line_b.hand_on(distance)
    line_q.hand_on(1)
    line_q.hand_on(2)
    plane_kv.spread()
    for distance in range(3, tp):
        line_q.hand_on(distance)
    starts[0].wait()
    plane_q.start()
    starts[2].wait()
    plane_b.start()
    starts[3].wait()
    plane_kv.complete()

    pick_row = lax.broadcasted_iota(jnp.int32, (16, 128), 0)
    pick_col = lax.broadcasted_iota(jnp.int32, (16, 128), 1)
    pick = jnp.where(pick_row == pick_col, 1.0, 0.0).astype(BF16)
    vector_rows = dot_nt(pick, wkv[:, kv_columns:])
    vectors[...] = vector_rows
    block_row = lax.broadcasted_iota(jnp.int32, (depth, kv_columns), 0)
    block_col = lax.broadcasted_iota(jnp.int32, (depth, kv_columns), 1)
    for b in range(dp):
        hit = (block_row < kvb_count) & (block_col == block_row + b * kvb_count)
        spread[b * depth : (b + 1) * depth, :] = jnp.where(hit, 1.0, 0.0).astype(BF16)
    kv_bias = dot(vector_rows.astype(BF16), spread[...])[2:3, :]

    xs = x[...].astype(F32)
    n1[...] = (xs * rms_scale(xs) * vector_rows[0:1, :]).astype(BF16)
    kv_rows = dot(n1[...], wkv[:, :kv_columns]) + kv_bias
    at = pl.ds(pl.multiple_of(begin, 16), own_rows)
    for h in range(KEYVALUE_HEADS):
        cut = slice(h * head, (h + 1) * head)
        kv[at, cut] = turned(kv_rows[:, cut], cosine[...], sine[...]).astype(BF16)
    kv[at, KEYVALUE_HEADS * head :] = kv_rows[:, KEYVALUE_HEADS * head :].astype(BF16)
    line_kv.start()
    line_o.start()
    line_kv.hand_on(1)
    plane_b.spread()
    for mask_of in range(1, 1 << place.steps):
        if mask_of == plane_q.half - 1:
            plane_ff[0].start()
            line_kv.hand_on(2)
        plane_q.hand_on(mask_of)
    for distance in range(1, tp):
        line_o.hand_on(distance)
    starts[1].wait()
    plane_o.start()
    for distance in range(3, tp):
        line_kv.hand_on(distance)
    line_cot.start()
    plane_b.complete()
    small_row = lax.broadcasted_iota(jnp.int32, (128, columns), 0)
    small_col = lax.broadcasted_iota(jnp.int32, (128, columns), 1)
    q_bias = jnp.zeros((tp * 16, columns), F32)
    for b in range(dp):
        hit = (small_row < qb_count) & (small_col == small_row + b * qb_count)
        one = jnp.where(hit, 1.0, 0.0).astype(BF16)
        q_bias = q_bias + dot(wb[b].reshape(tp * 16, 128), one)
    plane_q.complete()
    for t in range(tp):
        rows = dot(n1[...], wq[t]) + q_bias[t * 16 : t * 16 + 1, :]
        for h in range(columns // head):
            cut = slice(h * head, (h + 1) * head)
            out = slice(t * columns + h * head, t * columns + (h + 1) * head)
            q[:, out] = turned(rows[:, cut], cosine[...], sine[...]).astype(BF16)
    outs = [
        pltpu.make_async_copy(wq, wq_out, local_sem.at[0]),
        pltpu.make_async_copy(wkv, wkv_out, local_sem.at[3]),
    ]
    for copy in outs:
        copy.start()

    scale = 1.0 / math.sqrt(head)
    group = QUERY_HEADS // tp

    def probs_copy(part, count):
        at = pl.ds(part * group, group)
        return pltpu.make_async_copy(
            probs.at[at, :, pl.ds(0, count)], p_out.at[at, :, pl.ds(0, count)], probs_sem.at[part]
        )

    for part in range(tp):
        for blocks in range(1, tp + 1):
            count = blocks * own_rows

            @pl.when(z == blocks - 1)
            def _():
                def one_head(i, carry):
                    h = part * group + i
                    at = pl.ds(pl.multiple_of(h * head, head), head)
                    shared = h // REPEAT
                    key_at = pl.ds(pl.multiple_of(shared * head, head), head)
                    value_at = pl.ds(pl.multiple_of((KEYVALUE_HEADS + shared) * head, head), head)
                    scores = dot_nt(q[:, at], kv[0:count, key_at]) * scale + mask[:, 0:count]
                    top = jnp.max(scores, axis=1, keepdims=True)
                    weights = jnp.exp(scores - top)
                    total = jnp.sum(weights, axis=1, keepdims=True)
                    low = (weights / total).astype(BF16)
                    probs[h, :, 0:count] = low
                    att[:, at] = dot(low, kv[0:count, value_at]).astype(BF16)
                    return carry

                lax.fori_loop(0, group, one_head, 0)
                probs_copy(part, count).start()

    plane_ff[1].start()
    line_cot.hand_on(1)
    plane_o.spread()
    line_cot.hand_on(2)
    plane_o.complete()
    outs.append(pltpu.make_async_copy(wo, wo_out, local_sem.at[1]))
    outs[-1].start()
    for j in range(width // 512):
        cut = slice(j * 512, (j + 1) * 512)
        acc = x[:, cut].astype(F32)
        for t in range(tp):
            acc = acc + dot_nt(att[:, t * columns : (t + 1) * columns], wo[t, cut, :])
        res[:, cut] = acc
    residual = res[...]
    n2[...] = (residual * rms_scale(residual) * vectors[1:2, :]).astype(BF16)
    line_n2.start()
    n2_copy = pltpu.make_async_copy(n2, n2_out.at[z], local_sem.at[2])
    n2_copy.start()
    plane_ff[0].spread()
    plane_ff[2].start()
    for distance in range(3, tp):
        line_cot.hand_on(distance)
    line_n2.hand_on(1)
    plane_ff[1].spread()
    line_n2.hand_on(2)
    plane_ff[2].spread()
    for distance in range(3, tp):
        line_n2.hand_on(distance)
    for item in plane_ff:
        item.complete()
    for item in [plane_kv, plane_q, plane_o, plane_b] + plane_ff:
        item.finish()
    for item in (line_q, line_o, line_b, line_cot, line_kv, line_n2):
        item.finish()
    for copy in starts[4:] + outs + [n2_copy]:
        copy.wait()
    for part in range(tp):
        for blocks in range(1, tp + 1):

            @pl.when(z == blocks - 1)
            def _():
                probs_copy(part, blocks * own_rows).wait()


def forward_part(dp, tp, kvb_count, qb_count, x, seg_row, seg_col, zq, zo, zb, kvs, ff, cot):
    def shape(*dims, kind=BF16):
        return jax.ShapeDtypeStruct(dims, kind)

    own_rows, width = x.shape
    depth, columns = zq.shape
    items = seg_row.shape[1]
    head = HEAD_DIMENSION
    kv_columns = 2 * KEYVALUE_HEADS * head
    vmem = pl.BlockSpec(memory_space=pltpu.VMEM)
    anywhere = pl.BlockSpec(memory_space=ANY)
    return pl.pallas_call(
        functools.partial(forward_kernel, dp, tp, kvb_count, qb_count),
        out_shape=(
            shape(dp, *ff.shape),
            shape(tp, *cot.shape),
            shape(tp, own_rows, width),
            shape(tp, width, columns),
            shape(tp, width, columns),
            shape(width, kvs.shape[1]),
            shape(QUERY_HEADS, own_rows, items),
            shape(own_rows, width, kind=F32),
            shape(own_rows, tp * columns),
            shape(own_rows, width),
            shape(own_rows, tp * columns),
            shape(items, kv_columns),
            shape(own_rows, head, kind=F32),
            shape(own_rows, head, kind=F32),
            shape(16, width, kind=F32),
        ),
        in_specs=[vmem] * 9,
        out_specs=(anywhere,) * 7 + (vmem,) * 8,
        scratch_shapes=[
            pltpu.VMEM((tp, width, columns), BF16),
            pltpu.VMEM((tp, width, columns), BF16),
            pltpu.VMEM((width, kvs.shape[1]), BF16),
            pltpu.VMEM((dp, tp, 16, 128), BF16),
            pltpu.VMEM((width, kv_columns), BF16),
            pltpu.VMEM((own_rows, items), F32),
            pltpu.VMEM((QUERY_HEADS, own_rows, items), BF16),
            pltpu.VMEM((own_rows, width), BF16),
            pltpu.SemaphoreType.DMA((7, dp)),
            pltpu.SemaphoreType.DMA((7, dp)),
            pltpu.SemaphoreType.DMA((6, 2, tp)),
            pltpu.SemaphoreType.DMA((6, 2, tp)),
            pltpu.SemaphoreType.DMA((6,)),
            pltpu.SemaphoreType.DMA((tp,)),
        ],
        compiler_params=pltpu.CompilerParams(
            collective_id=0, has_side_effects=True, vmem_limit_bytes=56 << 20
        ),
        name="forward_part",
    )(x, seg_row, seg_col, zq, zo, zb, kvs, ff, cot)


class PlaneReduce:
    def __init__(self, place, part, held, send, recv):
        self.place, self.part, self.held, self.send, self.recv = place, part, held, send, recv
        self.half = 1 << place.steps
        self.last = place.steps

    def count(self, level):
        return self.half >> level

    def slot(self, level, i):
        return sum(self.count(k) for k in range(level)) + i

    def copy(self, level, i):
        place = self.place
        slot = self.slot(level, i)
        if level:
            src, device = self.held(self.slot(level - 1, 2 * i + 1)), place.partners[level - 1]
        else:
            src, device = self.part(place.sibling_block(i)), place.sibling
        return remote(
            src, self.held(slot), self.send(slot), self.recv(slot), place.device(device)
        )

    def start(self, level):
        for i in range(self.count(level)):
            self.copy(level, i).start()

    def wait_send(self, level):
        for i in range(self.count(level)):
            self.copy(level, i).wait_send()

    def absorb(self, level, out=None):
        order = sorted(range(self.count(level)), key=lambda i: 1 - i % 2)
        for i in order:
            slot = self.slot(level, i)
            self.copy(level, i).wait_recv()
            if level:
                other = self.held(self.slot(level - 1, 2 * i))
            else:
                other = self.part(self.place.block(i))
            add_into(self.held(slot), other, self.held(slot) if out is None else out)
            if i % 2:
                self.copy(level + 1, i // 2).start()


def add_into(one, other, out):
    rows = one.shape[0]
    step = 48 if rows % 48 == 0 else rows

    def body(k, carry):
        at = pl.ds(pl.multiple_of(k * step, 16), step)
        out[at, :] = (one[at, :].astype(F32) + other[at, :].astype(F32)).astype(out.dtype)
        return carry

    lax.fori_loop(0, rows // step, body, 0)


FF_PARTS = 3


class LineReduce:
    def __init__(self, place, term, sent, got, send, recv):
        self.place, self.term, self.sent, self.got = place, term, sent, got
        self.send, self.recv = send, recv

    def owner(self, turn):
        place = self.place
        if turn == place.tp - 1:
            return place.z
        falling = place.tp - 1 - turn
        falling = jnp.where(falling > place.z, falling, falling - 1)
        rising = jnp.where(turn < place.z, turn, turn + 1)
        return jnp.where(place.z < place.tp // 2, falling, rising)

    def way(self, turn):
        place = self.place
        owner = self.owner(turn)
        right = jnp.where(owner > place.z, 1, 0)
        side, offset = 1 - right, 2 * right - 1
        return side, offset, (owner - place.z) * offset

    def copy(self, turn):
        side, offset, distance = self.way(turn)
        return remote(
            self.sent(turn),
            self.got(side, distance - 1),
            self.send(turn),
            self.recv(side, distance - 1),
            self.place.beside(offset),
        )

    def arrival(self, side, distance):
        ref = self.got(side, distance)
        return remote(
            ref, ref, self.send(0), self.recv(side, distance), self.place.beside(0)
        )

    def direct(self, turn):
        side, offset, distance = self.way(turn)

        @pl.when(jnp.logical_not(self.place.has(-offset)))
        def _():
            copy_into(self.term(turn), self.sent(turn))
            self.copy(turn).start()

    def added(self, turn):
        side, offset, distance = self.way(turn)

        @pl.when(self.place.has(-offset))
        def _():
            self.arrival(side, distance).wait_recv()
            add_into(self.term(turn), self.got(side, distance), self.sent(turn))
            self.copy(turn).start()

    def total(self, out):
        last = self.place.tp - 1
        copy_into(self.term(last), out)
        for side, offset in ((0, -1), (1, 1)):

            @pl.when(self.place.has(offset))
            def _():
                self.arrival(side, 0).wait_recv()
                add_into(out, self.got(side, 0), out)

    def finish(self):
        for turn in range(self.place.tp - 1):
            self.copy(turn).wait_send()


def copy_into(one, out):
    rows = one.shape[0]
    step = 32 if rows % 32 == 0 else rows

    def body(k, carry):
        at = pl.ds(pl.multiple_of(k * step, 16), step)
        out[at, :] = one[at, :].astype(out.dtype)
        return carry

    lax.fori_loop(0, rows // step, body, 0)


def ff_kernel(
    dp, tp, ff, cot, n2, act, lhs, mlp, d2,
    wg, wu, wd, x, ct, made, term, sent, got, branch, turned_rows,
    w_sem, in_sem, act_sem, lhs_sem, mlp_sem, send_sem, recv_sem,
):
    place = Place(dp, tp)
    own_rows, width = d2.shape
    depth = ff.shape[2]
    padded = ff.shape[3]
    tile = 256
    third = padded // 3
    weights = (wg, wu, wd)
    loads = [
        [
            pltpu.make_async_copy(
                ff.at[b, p, :, pl.ds(c * third, third)],
                weights[p].at[pl.ds(b * depth, depth), pl.ds(c * third, third)],
                w_sem.at[p, b, c],
            )
            for p in range(FF_PARTS)
            for b in range(dp)
        ]
        for c in range(3)
    ]
    sums = LineReduce(
        place,
        lambda turn: term.at[turn % 2],
        lambda turn: sent.at[turn],
        lambda side, k: got.at[side, k],
        lambda turn: send_sem.at[turn],
        lambda side, k: recv_sem.at[side, k],
    )

    def fetch(turn):
        owner = sums.owner(turn)
        return [
            pltpu.make_async_copy(n2.at[owner], x.at[turn % 2], in_sem.at[turn % 2, 0]),
            pltpu.make_async_copy(cot.at[owner], ct.at[turn % 2], in_sem.at[turn % 2, 1]),
        ]

    def stores(turn, kinds=(0, 1, 2)):
        return [copies() for kind, copies in enumerate(store_kinds(turn)) if kind in kinds]

    def store_kinds(turn):
        owner = sums.owner(turn)
        at = pl.ds(pl.multiple_of(owner * own_rows, 128), own_rows)
        slot = turn % 2
        return (
            lambda: [
                pltpu.make_async_copy(made.at[slot, p], act.at[p, at], act_sem.at[slot, p])
                for p in range(FF_PARTS)
            ],
            lambda: [
                pltpu.make_async_copy(
                    turned_rows.at[slot, k], lhs.at[k, :, at], lhs_sem.at[slot, k]
                )
                for k in range(2)
            ],
            lambda: [pltpu.make_async_copy(branch.at[slot], mlp.at[owner], mlp_sem.at[slot])],
        )

    for copy in fetch(0):
        copy.start()
    for part in loads:
        for copy in part:
            copy.start()
    place.greet(False, True)
    for turn in range(tp):
        slot = turn % 2
        for copy in fetch(turn):
            copy.wait()
        if turn + 1 < tp:
            for copy in fetch(turn + 1):
                copy.start()
        if turn >= 2:
            for copies in stores(turn - 2):
                for copy in copies:
                    copy.wait()
        turned_rows[slot, 0] = x[slot].T
        turned_rows[slot, 1] = ct[slot].T
        for copy in stores(turn, (1,))[0]:
            copy.start()

        def units(n, carry, slot=slot):
            for k in range(3):
                at = pl.ds(pl.multiple_of((n * 3 + k) * tile, tile), tile)
                gate = dot(x[slot], wg[:, at])
                upper = dot(x[slot], wu[:, at])
                d_hidden = dot(ct[slot], wd[:, at])
                sigmoid = 1.0 / (1.0 + jnp.exp(-gate))
                swish = gate * sigmoid
                made[slot, 2, :, at] = (swish * upper).astype(BF16)
                made[slot, 1, :, at] = (d_hidden * swish).astype(BF16)
                made[slot, 0, :, at] = (
                    d_hidden * upper * sigmoid * (1.0 + gate * (1.0 - sigmoid))
                ).astype(BF16)
            return carry

        if turn == 0:
            for c in range(3):
                for copy in loads[c]:
                    copy.wait()
                lax.fori_loop(
                    c * (third // (3 * tile)), (c + 1) * (third // (3 * tile)), units, 0
                )
        else:
            lax.fori_loop(0, padded // (3 * tile), units, 0)

        def columns(n, carry, slot=slot):
            at = pl.ds(pl.multiple_of(n * tile, tile), tile)
            term[slot, :, at] = dot_nt(made[slot, 0], wg[at, :]) + dot_nt(
                made[slot, 1], wu[at, :]
            )
            branch[slot, :, at] = dot_nt(made[slot, 2], wd[at, :]).astype(BF16)
            return carry

        lax.fori_loop(0, width // tile, columns, 0)
        if turn < tp - 1:
            sums.direct(turn)
        for copies in stores(turn, (0, 2)):
            for copy in copies:
                copy.start()
        if 0 < turn < tp - 1:
            sums.added(turn - 1)
        if turn == tp - 2:
            sums.added(turn)
    sums.total(d2)
    sums.finish()
    for turn in range(tp - 2, tp):
        for copies in stores(turn):
            for copy in copies:
                copy.wait()


def ff_part(dp, tp, ff, cot, n2):
    def shape(*dims, kind=BF16):
        return jax.ShapeDtypeStruct(dims, kind)

    own_rows, width = cot.shape[1:]
    padded = ff.shape[3]
    vmem = pl.BlockSpec(memory_space=pltpu.VMEM)
    anywhere = pl.BlockSpec(memory_space=ANY)
    return pl.pallas_call(
        functools.partial(ff_kernel, dp, tp),
        out_shape=(
            shape(FF_PARTS, tp * own_rows, padded),
            shape(2, width, tp * own_rows),
            shape(tp, own_rows, width),
            shape(own_rows, width, kind=F32),
        ),
        in_specs=[anywhere] * 3,
        out_specs=(anywhere,) * 3 + (vmem,),
        scratch_shapes=[
            pltpu.VMEM((width, padded), BF16),
            pltpu.VMEM((width, padded), BF16),
            pltpu.VMEM((width, padded), BF16),
            pltpu.VMEM((2, own_rows, width), BF16),
            pltpu.VMEM((2, own_rows, width), BF16),
            pltpu.VMEM((2, FF_PARTS, own_rows, padded), BF16),
            pltpu.VMEM((2, own_rows, width), F32),
            pltpu.VMEM((tp - 1, own_rows, width), BF16),
            pltpu.VMEM((2, tp - 1, own_rows, width), BF16),
            pltpu.VMEM((2, own_rows, width), BF16),
            pltpu.VMEM((2, 2, width, own_rows), BF16),
            pltpu.SemaphoreType.DMA((FF_PARTS, dp, 3)),
            pltpu.SemaphoreType.DMA((2, 2)),
            pltpu.SemaphoreType.DMA((2, FF_PARTS)),
            pltpu.SemaphoreType.DMA((2, 2)),
            pltpu.SemaphoreType.DMA((2,)),
            pltpu.SemaphoreType.DMA((tp - 1,)),
            pltpu.SemaphoreType.DMA((2, tp - 1)),
        ],
        compiler_params=pltpu.CompilerParams(
            collective_id=3, has_side_effects=True, vmem_limit_bytes=60 << 20
        ),
        name="ff_part",
    )(ff, cot, n2)


class DownReduce:
    def __init__(self, place, term, got, send, recv):
        self.place, self.term, self.got, self.send, self.recv = place, term, got, send, recv

    def copy(self, distance):
        return remote(
            self.term(self.place.z - distance),
            self.got(distance - 1),
            self.send(distance),
            self.recv(distance - 1),
            self.place.beside(-1),
        )

    def take(self, distance, out):
        place = self.place

        @pl.when(place.z < place.tp - 1)
        def _():
            ref = self.got(distance)
            remote(
                ref, ref, self.send(distance), self.recv(distance), place.beside(0)
            ).wait_recv()
            add_into(out, ref, out)

    def step(self, distance):
        place = self.place

        @pl.when(place.z >= distance)
        def _():
            if distance < place.tp - 1:
                self.take(distance, self.term(place.z - distance))
            self.copy(distance).start()

    def finish(self):
        for distance in range(1, self.place.tp):

            @pl.when(self.place.z >= distance)
            def _():
                self.copy(distance).wait_send()


def backward_kernel(
    dp, tp, chunk,
    res, vectors, att, q, kv, cosine, sine, d2, cot, x, lhs, act, mlp, probs, wo, wq, wkv,
    out, mlp_sent, mlp_got, d_branch, d_qkv, output, input_grad, vector_grads,
    part, taken, held, left, block, stage, weight, kv_weight, prob, d_att, d_kv, d_kv_low, kv_got,
    acc, wide, own_bf, d_res,
    act_sem, send_sem, recv_sem, left_sem, stage_sem, line_send, line_recv, out_sem, weight_sem,
    prob_sem, kv_send, kv_recv, in_sem,
):
    place = Place(dp, tp)
    z = place.z
    own_rows, width = res.shape
    depth = width // dp
    group = max(1, 384 // depth)
    tile = 256
    head = HEAD_DIMENSION
    scale = 1.0 / math.sqrt(head)
    columns = wq.shape[2]
    heads_width = tp * columns
    half_kv = KEYVALUE_HEADS * head
    per_part = act.shape[2] // chunk
    units = [(p, k) for p in (2, 0, 1) for k in range(per_part)]

    def fetch(u):
        p, k = units[u]
        return pltpu.make_async_copy(
            act.at[p, :, pl.ds(k * chunk, chunk)], taken.at[u % 2], act_sem.at[u % 2]
        )

    def fetch_left(k):
        return pltpu.make_async_copy(lhs.at[k], left, left_sem.at[0])

    def fetch_weight(n):
        source = wo if n < tp else wq
        return pltpu.make_async_copy(source.at[n % tp], weight.at[n % 2], weight_sem.at[n % 2])

    def fetch_probs(h, slot):
        return pltpu.make_async_copy(probs.at[h], prob.at[slot], prob_sem.at[slot])

    d2_copy = pltpu.make_async_copy(d2, wide, in_sem.at[0])
    cot_copy = pltpu.make_async_copy(cot, own_bf, in_sem.at[1])
    x_copy = pltpu.make_async_copy(x, own_bf, in_sem.at[2])
    kv_weight_copy = pltpu.make_async_copy(
        wkv.at[:, pl.ds(0, 2 * half_kv)], kv_weight, in_sem.at[3]
    )
    fetch_left(1).start()
    fetch(0).start()
    for copy in (d2_copy, cot_copy, fetch_weight(0), fetch_weight(1), kv_weight_copy):
        copy.start()
    for h in range(2):
        fetch_probs(h, h).start()
    place.greet(True, True)

    line = LineReduce(
        place,
        None,
        lambda turn: mlp_sent.at[turn],
        lambda side, k: mlp_got.at[side, k],
        lambda turn: line_send.at[turn],
        lambda side, k: line_recv.at[side, k],
    )

    def load_term(turn):
        return pltpu.make_async_copy(mlp.at[line.owner(turn)], stage.at[0], stage_sem.at[0])

    def load_got(side, distance):
        return pltpu.make_async_copy(mlp_got.at[side, distance], stage.at[1], stage_sem.at[1])

    def line_direct(turn):
        side, offset, distance = line.way(turn)

        @pl.when(jnp.logical_not(place.has(-offset)))
        def _():
            remote(
                mlp.at[line.owner(turn)],
                mlp_got.at[side, distance - 1],
                line_send.at[turn],
                line_recv.at[side, distance - 1],
                place.beside(offset),
            ).start()

    def line_step(turn):
        side, offset, distance = line.way(turn)

        @pl.when(place.has(-offset))
        def _():
            load_term(turn).start()
            line.arrival(side, distance).wait_recv()
            load_got(side, distance).start()
            load_term(turn).wait()
            load_got(side, distance).wait()
            add_into(stage.at[0], stage.at[1], stage.at[0])
            store = pltpu.make_async_copy(stage.at[0], mlp_sent.at[turn], stage_sem.at[0])
            store.start()
            store.wait()
            line.copy(turn).start()

    def line_total():
        load_term(tp - 1).start()
        load_term(tp - 1).wait()
        add_into(res, stage.at[0], d_res)
        for side, offset in ((0, -1), (1, 1)):

            @pl.when(place.has(offset))
            def _():
                line.arrival(side, 0).wait_recv()
                load_got(side, 0).start()
                load_got(side, 0).wait()
                add_into(d_res, stage.at[1], d_res)

        copy_into(d_res, output)

    for turn in range(tp - 1):
        line_direct(turn)
    down = DownReduce(
        place,
        lambda r: d_kv_low.at[pl.ds(pl.multiple_of(r * own_rows, 16), own_rows)],
        lambda k: kv_got.at[k],
        lambda k: kv_send.at[k],
        lambda k: kv_recv.at[k],
    )

    def second_norm():
        d2_copy.wait()
        cot_copy.wait()
        values, grad = res[...], wide[...]
        s = rms_scale(values)
        normed = values * s
        weighted = grad * vectors[1:2, :]
        inner = jnp.mean(weighted * normed, axis=1, keepdims=True)
        found = own_bf[...].astype(F32) + s * (weighted - normed * inner)
        d_res[...] = found
        d_branch[...] = found.astype(BF16)
        vector_grads[...] = jnp.zeros_like(vector_grads)
        vector_grads[1:2, :] = jnp.sum(grad * normed, axis=0, keepdims=True)
        x_copy.start()
        d_kv[...] = jnp.zeros_like(d_kv)

    def attended_grad(ts):
        for t in ts:
            fetch_weight(t).wait()
            d_att[:, t * columns : (t + 1) * columns] = dot(d_branch[...], weight[t % 2]).astype(
                BF16
            )
            fetch_weight(t + 2).start()

    def some_heads(begin, end):
        def one_head(h, carry):
            slot = h % 2
            at = pl.ds(pl.multiple_of(h * head, head), head)
            shared = h // REPEAT
            key_at = pl.ds(pl.multiple_of(shared * head, head), head)
            value_at = pl.ds(pl.multiple_of(half_kv + shared * head, head), head)
            fetch_probs(h, slot).wait()
            d_out = d_att[:, at]
            inner = jnp.sum(
                d_out.astype(F32) * att[:, at].astype(F32), axis=1, keepdims=True
            )
            acc[...] = jnp.zeros_like(acc)

            def one_block(j, carry):
                rows = pl.ds(pl.multiple_of(j * own_rows, 256), own_rows)
                low = prob[slot, :, rows]
                d_probs = dot_nt(d_out, kv[rows, value_at])
                d_scores = (low.astype(F32) * (scale * (d_probs - inner))).astype(BF16)
                acc[...] += dot(d_scores, kv[rows, key_at])
                d_kv[rows, key_at] += dot_tn(d_scores, q[:, at])
                d_kv[rows, value_at] += dot_tn(low, d_out)
                return carry

            lax.fori_loop(0, z + 1, one_block, 0)
            d_qkv[:, at] = turned(acc[...], cosine[...], -sine[...]).astype(BF16)

            @pl.when(h + 2 < QUERY_HEADS)
            def _():
                fetch_probs(h + 2, slot).start()

            return carry

        lax.fori_loop(begin, end, one_head, 0)

    def send_kv():
        def body(j, carry):
            rows = pl.ds(pl.multiple_of(j * own_rows, 256), own_rows)
            d_kv_low[rows, :] = d_kv[rows, :].astype(BF16)
            return carry

        lax.fori_loop(0, z + 1, body, 0)
        down.step(tp - 1)
        for distance in range(tp - 2, 0, -1):
            down.step(distance)

    def normed_grad(ts):
        for t in ts:
            fetch_weight(tp + t).wait()
            for j in range(width // 512):
                cut = slice(j * 512, (j + 1) * 512)
                found = dot_nt(
                    d_qkv[:, t * columns : (t + 1) * columns], weight[(tp + t) % 2, cut, :]
                )
                wide[:, cut] = found + wide[:, cut] if t else found
            if t + 2 < tp:
                fetch_weight(tp + t + 2).start()

    def first_norm():
        mine = pl.ds(pl.multiple_of(z * own_rows, 16), own_rows)
        down.take(0, d_kv.at[mine])
        for h in range(KEYVALUE_HEADS):
            cut = slice(h * head, (h + 1) * head)
            d_qkv[:, heads_width + h * head : heads_width + (h + 1) * head] = turned(
                d_kv[mine, cut], cosine[...], -sine[...]
            ).astype(BF16)
        d_qkv[:, heads_width + half_kv :] = d_kv[mine, half_kv:].astype(BF16)
        kv_weight_copy.wait()
        for j in range(width // 512):
            cut = slice(j * 512, (j + 1) * 512)
            wide[:, cut] += dot_nt(d_qkv[:, heads_width:], kv_weight[cut, :])
        x_copy.wait()
        values, grad = own_bf[...].astype(F32), wide[...]
        s = rms_scale(values)
        normed = values * s
        weighted = grad * vectors[0:1, :]
        inner = jnp.mean(weighted * normed, axis=1, keepdims=True)
        input_grad[...] = (d_res[...] + s * (weighted - normed * inner)).astype(BF16)
        vector_grads[0:1, :] = jnp.sum(grad * normed, axis=0, keepdims=True)
        sums_of = jnp.sum(d_qkv[...].astype(F32), axis=0, keepdims=True)
        vector_grads[2:3, :] = sums_of[:, :heads_width]
        vector_grads[3:4, : 2 * half_kv] = sums_of[:, heads_width:]

    per = QUERY_HEADS // tp
    pieces = [
        [second_norm, lambda: attended_grad(range(tp))],
        [lambda: some_heads(0, 2)],
        [lambda: some_heads(2, 4), lambda: line_step(0)],
        [lambda: some_heads(4, 6)],
        [lambda: some_heads(6, 8), lambda: line_step(1)],
        [lambda: some_heads(8, 10), lambda: line_step(2)],
        [lambda: some_heads(10, 12), send_kv],
        [lambda: normed_grad(range(tp))],
        [],
        [first_norm],
        [line_total],
    ]

    def stored(u):
        p, k = units[u]
        return pltpu.make_async_copy(
            block.at[u % 2], out.at[p, :, pl.ds(k * chunk, chunk)], out_sem.at[u % 2]
        )

    sums = [
        PlaneReduce(
            place,
            lambda b, u=u: part.at[u % 2, b],
            lambda s, u=u: held.at[u, s],
            lambda s, u=u: send_sem.at[u, s],
            lambda s, u=u: recv_sem.at[u, s],
        )
        for u in range(len(units))
    ]
    last = place.steps
    fetch_left(1).wait()
    for turn in range(max(len(units) + last + 1, len(pieces))):
        if turn < len(units):
            u = turn
            p, k = units[u]
            if u + 1 < len(units):
                fetch(u + 1).start()
            if u == per_part:
                fetch_left(0).wait()
            fetch(u).wait()
            if u >= 2:
                sums[u - 2].wait_send(0)

            def body(n, carry, u=u):
                i, j = n // (chunk // tile), n % (chunk // tile)
                rows = pl.ds(pl.multiple_of(i * (group * depth), 16), group * depth)
                cols = pl.ds(pl.multiple_of(j * tile, tile), tile)
                found = dot(left[rows, :], taken[u % 2, :, cols]).astype(BF16)
                for g in range(group):
                    part[u % 2, i * group + g, :, cols] = found[g * depth : (g + 1) * depth]
                return carry

            lax.fori_loop(0, dp // group * (chunk // tile), body, 0)
            sums[u].start(0)
            if u == per_part - 1:
                fetch_left(0).start()
        for level in range(last + 1):
            u = turn - 1 - level
            if 0 <= u < len(units):
                if level == last:
                    if u >= 2:
                        stored(u - 2).wait()
                    sums[u].absorb(level, block.at[u % 2])
                    stored(u).start()
                else:
                    sums[u].absorb(level)
        if turn < len(pieces):
            for piece in pieces[turn]:
                piece()
    line.finish()
    down.finish()
    for u in range(len(units)):
        if u >= len(units) - 2:
            stored(u).wait()
        for level in range(0 if u >= len(units) - 2 else 1, last + 1):
            sums[u].wait_send(level)


def backward_part(
    dp, tp, res, vectors, att, q, kv, cosine, sine, d2, cot, x, lhs, act, mlp, probs, wo, wq, wkv
):
    def shape(*dims, kind=BF16):
        return jax.ShapeDtypeStruct(dims, kind)

    own_rows, width = res.shape
    depth = width // dp
    items, padded = act.shape[1:]
    columns = wq.shape[2]
    kv_columns = kv.shape[1]
    chunk = 768
    count = FF_PARTS * padded // chunk
    vmem = pl.BlockSpec(memory_space=pltpu.VMEM)
    anywhere = pl.BlockSpec(memory_space=ANY)
    return pl.pallas_call(
        functools.partial(backward_kernel, dp, tp, chunk),
        out_shape=(
            shape(FF_PARTS, depth, padded, kind=F32),
            shape(tp - 1, own_rows, width),
            shape(2, tp - 1, own_rows, width),
            shape(own_rows, width),
            shape(own_rows, tp * columns + kv_columns),
            shape(own_rows, width),
            shape(own_rows, width),
            shape(8, width, kind=F32),
        ),
        in_specs=[vmem] * 7 + [anywhere] * 10,
        out_specs=(anywhere,) * 3 + (vmem,) * 5,
        scratch_shapes=[
            pltpu.VMEM((2, dp, depth, chunk), BF16),
            pltpu.VMEM((2, items, chunk), BF16),
            pltpu.VMEM((count, dp - 1, depth, chunk), BF16),
            pltpu.VMEM((width, items), BF16),
            pltpu.VMEM((2, depth, chunk), F32),
            pltpu.VMEM((2, own_rows, width), BF16),
            pltpu.VMEM((2, width, columns), BF16),
            pltpu.VMEM((width, kv_columns), BF16),
            pltpu.VMEM((2, own_rows, items), BF16),
            pltpu.VMEM((own_rows, tp * columns), BF16),
            pltpu.VMEM((items, kv_columns), F32),
            pltpu.VMEM((items, kv_columns), BF16),
            pltpu.VMEM((tp - 1, own_rows, kv_columns), BF16),
            pltpu.VMEM((own_rows, HEAD_DIMENSION), F32),
            pltpu.VMEM((own_rows, width), F32),
            pltpu.VMEM((own_rows, width), BF16),
            pltpu.VMEM((own_rows, width), F32),
            pltpu.SemaphoreType.DMA((2,)),
            pltpu.SemaphoreType.DMA((count, dp - 1)),
            pltpu.SemaphoreType.DMA((count, dp - 1)),
            pltpu.SemaphoreType.DMA((1,)),
            pltpu.SemaphoreType.DMA((2,)),
            pltpu.SemaphoreType.DMA((tp - 1,)),
            pltpu.SemaphoreType.DMA((2, tp - 1)),
            pltpu.SemaphoreType.DMA((2,)),
            pltpu.SemaphoreType.DMA((2,)),
            pltpu.SemaphoreType.DMA((2,)),
            pltpu.SemaphoreType.DMA((tp,)),
            pltpu.SemaphoreType.DMA((tp - 1,)),
            pltpu.SemaphoreType.DMA((4,)),
        ],
        compiler_params=pltpu.CompilerParams(
            collective_id=1, has_side_effects=True, vmem_limit_bytes=63 << 20
        ),
        name="backward_part",
    )(res, vectors, att, q, kv, cosine, sine, d2, cot, x, lhs, act, mlp, probs, wo, wq, wkv)


def attn_grad_kernel(
    dp, tp, widths, n1, d_qkv, d_branch, att, vectors, kv_out, q_out, o_out, vectors_out,
    turned_rows, part, held, own, line_kv, line_qo, vector_sum, vector_got, line_vector,
    send_sem, recv_sem, line_send, line_recv, vector_send, vector_recv,
):
    place = Place(dp, tp)
    z = place.z
    depth, columns = q_out.shape
    width = dp * depth
    heads_width = tp * columns
    barrier = pltpu.get_barrier_semaphore()
    for partner in place.partners + [place.sibling]:
        pl.semaphore_signal(barrier, inc=1, device_id=place.device(partner), device_id_type=MESH)
    for t in range(tp):

        @pl.when(t != z)
        def _():
            pl.semaphore_signal(barrier, inc=1, device_id=(place.d, t), device_id_type=MESH)

    pl.semaphore_wait(barrier, place.steps + tp)
    kinds = (0, 0, 2, 1, 1)
    halves = (0, 1, 0, 0, 1)
    count = len(widths)
    group = max(1, 384 // depth)
    sums = [
        PlaneReduce(
            place,
            lambda b, u=u: part.at[u, b, :, pl.ds(0, widths[u])],
            lambda s, u=u: held.at[u, s, :, pl.ds(0, widths[u])],
            lambda s, u=u: send_sem.at[u, s],
            lambda s, u=u: recv_sem.at[u, s],
        )
        for u in range(count)
    ]

    def make(u):
        kind, half = kinds[u], halves[u]
        left = 1 if kind == 1 else 0
        right = att if kind == 1 else d_qkv
        base = heads_width if kind == 2 else half * widths[u]

        def body(i, carry):
            rows = pl.ds(pl.multiple_of(i * (group * depth), 16), group * depth)
            for j in range(widths[u] // 256):
                found = dot(
                    turned_rows[left, rows, :], right[:, base + j * 256 : base + (j + 1) * 256]
                ).astype(BF16)
                for g in range(group):
                    part[u, i * group + g, :, j * 256 : (j + 1) * 256] = found[
                        g * depth : (g + 1) * depth
                    ]
            return carry

        lax.fori_loop(0, dp // group, body, 0)
        sums[u].start(0)

    def line_copies(u):
        found = []
        kind, half = kinds[u], halves[u]
        for t in range(tp):
            if kind == 2:
                src, dst = own.at[u, :, pl.ds(0, widths[u])], line_kv.at[z]
            elif t // 2 == half:
                src, dst = own.at[u, :, pl.ds((t % 2) * columns, columns)], line_qo.at[kind, z]
            else:
                continue
            found.append((t, remote(
                src, dst, line_send.at[u, t], line_recv.at[kind, z], (place.d, t)
            )))
        return found

    last = place.steps

    def work(turn):
        for level in range(last + 1):
            u = turn - level
            if 0 <= u < count:
                target = own.at[u, :, pl.ds(0, widths[u])] if level == last else None
                sums[u].absorb(level, target)
                if level == last:
                    for t, copy in line_copies(u):

                        @pl.when(t != z)
                        def _():
                            copy.start()

    ways = [place.sibling] + place.partners

    def vector_copy(level):
        return remote(
            vectors if level == 0 else vector_sum.at[level - 1],
            vector_got.at[level],
            vector_send.at[level],
            vector_recv.at[level],
            place.device(ways[level]),
        )

    def vector_step(level):
        vector_copy(level).wait_recv()
        mine = vectors[...] if level == 0 else vector_sum[level - 1]
        vector_sum[level] = mine + vector_got[level]
        if level < last:
            vector_copy(level + 1).start()
        else:
            for t in range(tp):

                @pl.when(t != z)
                def _():
                    vector_line(t).start()

    def vector_line(t):
        return remote(
            vector_sum.at[last],
            line_vector.at[z],
            line_send.at[count, t],
            line_recv.at[3, z],
            (place.d, t),
        )

    vector_copy(0).start()
    turned_rows[0] = n1[...].T
    make(0)
    make(1)
    turned_rows[1] = d_branch[...].T
    for u in range(2, count):
        make(u)
    for turn in range(count + last):
        work(turn)
        if turn <= last:
            vector_step(turn)

    def arrived(ref, kind):
        for t in range(tp):

            @pl.when(t != z)
            def _():
                remote(
                    ref.at[t], ref.at[t], line_send.at[0, t], line_recv.at[kind, t], (place.d, t)
                ).wait_recv()

    def total(ref, mine, out):
        acc = mine.astype(F32)
        for t in range(tp):
            acc = acc + jnp.where(t != z, ref[t].astype(F32), 0.0)
        out[...] = acc

    at = pl.ds(pl.multiple_of((z % 2) * columns, 128), columns)
    arrived(line_vector, 3)
    total(line_vector, vector_sum[last], vectors_out)
    arrived(line_qo.at[0], 0)
    total(line_qo.at[0], own[z // 2, :, at], q_out)
    arrived(line_kv, 2)
    total(line_kv, own[2, :, : widths[2]], kv_out)
    arrived(line_qo.at[1], 1)
    total(line_qo.at[1], own[3 + z // 2, :, at], o_out)
    for u in range(count):
        for level in range(last + 1):
            sums[u].wait_send(level)
        for t, copy in line_copies(u):

            @pl.when(t != z)
            def _():
                copy.wait_send()

    for level in range(last + 1):
        vector_copy(level).wait_send()
    for t in range(tp):

        @pl.when(t != z)
        def _():
            vector_line(t).wait_send()


def attn_grads(dp, tp, n1, d_qkv, d_branch, att, vectors):
    own_rows, width = n1.shape
    depth = width // dp
    heads_width = att.shape[1]
    kv_columns = d_qkv.shape[1] - heads_width
    half = heads_width // 2
    widths = (half, half, kv_columns, half, half)
    columns = heads_width // tp
    levels = dp.bit_length() - 1
    vmem = pl.BlockSpec(memory_space=pltpu.VMEM)
    return pl.pallas_call(
        functools.partial(attn_grad_kernel, dp, tp, widths),
        out_shape=(
            jax.ShapeDtypeStruct((depth, kv_columns), F32),
            jax.ShapeDtypeStruct((depth, columns), F32),
            jax.ShapeDtypeStruct((depth, columns), F32),
            jax.ShapeDtypeStruct(vectors.shape, F32),
        ),
        in_specs=[vmem] * 5,
        out_specs=(vmem,) * 4,
        scratch_shapes=[
            pltpu.VMEM((2, width, own_rows), BF16),
            pltpu.VMEM((5, dp, depth, half), BF16),
            pltpu.VMEM((5, dp - 1, depth, half), BF16),
            pltpu.VMEM((5, depth, half), BF16),
            pltpu.VMEM((tp, depth, kv_columns), BF16),
            pltpu.VMEM((2, tp, depth, columns), BF16),
            pltpu.VMEM((levels,) + vectors.shape, F32),
            pltpu.VMEM((levels,) + vectors.shape, F32),
            pltpu.VMEM((tp,) + vectors.shape, F32),
            pltpu.SemaphoreType.DMA((5, dp - 1)),
            pltpu.SemaphoreType.DMA((5, dp - 1)),
            pltpu.SemaphoreType.DMA((6, tp)),
            pltpu.SemaphoreType.DMA((4, tp)),
            pltpu.SemaphoreType.DMA((levels,)),
            pltpu.SemaphoreType.DMA((levels,)),
        ],
        compiler_params=pltpu.CompilerParams(
            collective_id=2, has_side_effects=True, vmem_limit_bytes=56 << 20
        ),
        name="attn_grads",
    )(n1, d_qkv, d_branch, att, vectors)


def local(
    inputs,
    segment_ids,
    first_gain,
    query_weight,
    query_bias,
    key_value_weight,
    key_value_bias,
    output_weight,
    second_gain,
    gateup_weight,
    down_weight,
    cotangent,
):
    dp = lax.axis_size("dp")
    tp = lax.axis_size("tensor")
    rank = lax.axis_index("tensor")
    width = inputs.shape[1]
    own_rows = inputs.shape[0]
    depth = query_weight.shape[0]
    columns = query_weight.shape[1]
    kv_columns = key_value_weight.shape[1]
    hidden_units = gateup_weight.shape[2]
    heads_width = columns * tp
    head = HEAD_DIMENSION
    scale = 1.0 / math.sqrt(head)

    padded = -(-hidden_units // 256) * 256
    ff_own = jnp.stack([gateup_weight[0], gateup_weight[1], down_weight.T])
    ff_own = jnp.pad(ff_own, ((0, 0), (0, 0), (0, padded - hidden_units)))
    qb_count, kvb_count = query_bias.shape[0], key_value_bias.shape[0]
    own_kvbias = jnp.pad(key_value_bias, (0, depth - kvb_count))
    side = jnp.pad(jnp.stack([first_gain, second_gain, own_kvbias], axis=1), ((0, 0), (0, 125)))
    own_segments = lax.dynamic_slice_in_dim(segment_ids, rank * own_rows, own_rows, 0)
    (
        ff_all, grad_rows, second_rows, wq, wo, wkv, probs_low,
        residual, attended, normed_own, rot_query, all_kv, cosine, sine, vectors,
    ) = forward_part(
        dp,
        tp,
        kvb_count,
        qb_count,
        inputs,
        segment_ids[None, :],
        own_segments[:, None],
        query_weight,
        output_weight.T,
        jnp.pad(query_bias[None, :], ((0, 15), (0, 128 - qb_count))),
        jnp.concatenate([key_value_weight, side], axis=1),
        ff_own,
        cotangent,
    )
    act, lhs, mlp_terms, d_second = ff_part(dp, tp, ff_all, grad_rows, second_rows)
    ff_sh, _, _, d_branch, d_qkv, output, input_grad, vector_grads = backward_part(
        dp, tp, residual, vectors, attended, rot_query, all_kv, cosine, sine,
        d_second, cotangent, inputs, lhs, act, mlp_terms, probs_low, wo, wq, wkv,
    )
    kv_sh, q_sh, o_sh, small = attn_grads(
        dp, tp, normed_own, d_qkv, d_branch, attended, vector_grads
    )
    d = lax.axis_index("dp")

    def mine(row, count, index):
        return lax.dynamic_slice_in_dim(row, index * count, count, 0)

    return (
        output,
        input_grad,
        mine(small[0], depth, d),
        q_sh,
        mine(small[2], qb_count, rank * dp + d),
        kv_sh,
        mine(small[3], kvb_count, d),
        o_sh.T,
        mine(small[1], depth, d),
        ff_sh[:2, :, :hidden_units],
        ff_sh[2, :, :hidden_units].T,
    )


def solution(mesh):
    in_specs = (
        P(("dp", "tensor"), None),
        P("dp"),
        P("dp"),
        P("dp", "tensor"),
        P(("tensor", "dp")),
        P("dp", None),
        P("dp"),
        P("tensor", "dp"),
        P("dp"),
        P(None, "dp", "tensor"),
        P("tensor", "dp"),
        P(("dp", "tensor"), None),
    )
    out_specs = (
        P(("dp", "tensor"), None),
        P(("dp", "tensor"), None),
        P("dp"),
        P("dp", "tensor"),
        P(("tensor", "dp")),
        P("dp", None),
        P("dp"),
        P("tensor", "dp"),
        P("dp"),
        P(None, "dp", "tensor"),
        P("tensor", "dp"),
    )
    return jax.shard_map(local, mesh=mesh, in_specs=in_specs, out_specs=out_specs, check_vma=False)
```

```python
import functools
import math

import jax
import jax.numpy as jnp
from jax import lax
from jax.experimental import pallas as pl
from jax.experimental.pallas import tpu as pltpu
from jax.sharding import PartitionSpec as P

QUERY_HEADS = 12
KEYVALUE_HEADS = 2
HEAD_DIMENSION = 128
REPEAT = QUERY_HEADS // KEYVALUE_HEADS

EPSILON = 1e-06
THETA = 1000000.0
NEGATIVE = -1e30

F32 = jnp.float32
BF16 = jnp.bfloat16


def rms_scale(rows):
    return lax.rsqrt(jnp.mean(rows * rows, axis=-1, keepdims=True) + EPSILON)


def norm_back(rows, gain, grad):
    scale = rms_scale(rows)
    normed = rows * scale
    weighted = grad * gain
    inner = jnp.mean(weighted * normed, axis=-1, keepdims=True)
    return (scale * (weighted - normed * inner), jnp.sum(grad * normed, axis=0))


def rope_tables(segments, head_extent):
    index = jnp.arange(segments.shape[0], dtype=jnp.int32)
    starts = jnp.concatenate([jnp.ones((1,), dtype=bool), segments[1:] != segments[:-1]])
    first = lax.cummax(jnp.where(starts, index, jnp.zeros_like(index)), axis=0)
    placed = (index - first).astype(F32)
    freqs = jnp.exp(
        jnp.arange(head_extent // 2, dtype=F32) * (-2.0 * math.log(THETA) / head_extent)
    )
    return placed, freqs


def apply_rotation(value_rows, cosine_table, sine_table):
    half = value_rows.shape[-1] // 2
    former = value_rows[..., :half]
    latter = value_rows[..., half:]
    return jnp.concatenate(
        [former * cosine_table - latter * sine_table, latter * cosine_table + former * sine_table],
        axis=-1,
    )


def unrotate(grads, cosine_table, sine_table):
    return apply_rotation(grads, cosine_table, -sine_table)


def dot(left, right):
    return jnp.dot(left, right, preferred_element_type=F32)


def dot_nt(left, right):
    return lax.dot_general(left, right, (((1,), (1,)), ((), ())), preferred_element_type=F32)


def dot_tn(left, right):
    return lax.dot_general(left, right, (((0,), (0,)), ((), ())), preferred_element_type=F32)


MESH = pl.DeviceIdType.MESH
ANY = pl.ANY


def flip(index, bit):
    return index + (1 << bit) * (1 - 2 * ((index // (1 << bit)) % 2))


class Place:
    def __init__(self, dp, tp):
        self.dp, self.tp = dp, tp
        self.d, self.z = lax.axis_index("dp"), lax.axis_index("tensor")
        self.steps = dp.bit_length() - 2
        odd = self.d % 2
        self.partners = []
        for step in range(self.steps):
            first, other = flip(self.d, 1 + step), flip(self.d, self.steps - step)
            self.partners.append(first + odd * (other - first))
        self.sibling = flip(self.d, 0)
        self.deltas = [partner - self.d for partner in self.partners]

    def block(self, mask):
        index = self.d
        for step in range(self.steps):
            if (mask >> step) & 1:
                index = index + self.deltas[step]
        return index

    def sibling_block(self, mask):
        index = self.sibling
        for step in range(self.steps):
            if (mask >> step) & 1:
                index = index + self.deltas[self.steps - 1 - step]
        return index

    def device(self, index):
        return (index, self.z)

    def beside(self, offset):
        return (self.d, self.z + offset)

    def greet(self, plane, line):
        barrier = pltpu.get_barrier_semaphore()
        count = 0
        if plane:
            for partner in self.partners + [self.sibling]:
                pl.semaphore_signal(
                    barrier, inc=1, device_id=self.device(partner), device_id_type=MESH
                )
            count = self.steps + 1
        if line:
            for offset in (-1, 1):

                @pl.when(self.has(offset))
                def _():
                    pl.semaphore_signal(
                        barrier, inc=1, device_id=self.beside(offset), device_id_type=MESH
                    )

            count = count + jnp.where(self.z > 0, 1, 0) + jnp.where(self.z < self.tp - 1, 1, 0)
        pl.semaphore_wait(barrier, count)

    def has(self, offset):
        return (self.z + offset >= 0) & (self.z + offset < self.tp)


def remote(src, dst, send, recv, device):
    return pltpu.make_async_remote_copy(
        src_ref=src, dst_ref=dst, send_sem=send, recv_sem=recv, device_id=device, device_id_type=MESH
    )


class PlaneGather:
    def __init__(self, place, own, full, send, recv):
        self.place, self.own, self.full, self.send, self.recv = place, own, full, send, recv
        self.half = 1 << place.steps

    def at(self, mask):
        return self.full(self.place.block(mask)) if mask else self.own

    def copy(self, mask, step):
        place = self.place
        if step < place.steps:
            label, device = mask | (1 << step), place.device(place.partners[step])
        else:
            label, device = self.half + mask, place.device(place.sibling)
        return remote(
            self.at(mask), self.full(place.block(mask)), self.send(label), self.recv(label), device
        )

    def arrival(self, label):
        place = self.place
        if label < self.half:
            ref = self.full(place.block(label))
        else:
            ref = self.full(place.sibling_block(label - self.half))
        return remote(ref, ref, self.send(label), self.recv(label), place.device(place.sibling))

    def sends(self, mask):
        return [self.copy(mask, step) for step in range(mask.bit_length(), self.place.steps + 1)]

    def start(self):
        for copy in self.sends(0):
            copy.start()

    def hand_on(self, mask):
        self.arrival(mask).wait_recv()
        for copy in self.sends(mask):
            copy.start()

    def spread(self):
        for mask in range(1, self.half):
            self.hand_on(mask)

    def complete(self):
        for mask in range(self.half):
            self.arrival(self.half + mask).wait_recv()

    def finish(self):
        for mask in range(self.half):
            for copy in self.sends(mask):
                copy.wait_send()


class LineGather:
    def __init__(self, place, own, full, send, recv, offsets=(1, -1)):
        self.place, self.own, self.full, self.send, self.recv = place, own, full, send, recv
        self.offsets = offsets

    def copy(self, distance, offset):
        place = self.place
        source = place.z - offset * distance
        side = 0 if offset > 0 else 1
        src = self.full(source) if distance else self.own
        return remote(
            src,
            self.full(source),
            self.send(side, distance),
            self.recv(side, distance),
            place.beside(offset),
        )

    def each(self, distance, act):
        place = self.place
        for offset in self.offsets:

            @pl.when(place.has(-offset * distance) & place.has(offset))
            def _():
                act(self.copy(distance, offset))

    def start(self):
        self.each(0, lambda copy: copy.start())

    def arrived(self, distance):
        place = self.place
        for offset in self.offsets:

            @pl.when(place.has(-offset * distance))
            def _():
                side = 0 if offset > 0 else 1
                ref = self.full(place.z - offset * distance)
                remote(
                    ref,
                    ref,
                    self.send(side, distance - 1),
                    self.recv(side, distance - 1),
                    place.beside(-offset),
                ).wait_recv()

    def hand_on(self, distance):
        self.arrived(distance)
        if distance < self.place.tp - 1:
            self.each(distance, lambda copy: copy.start())

    def finish(self):
        for distance in range(self.place.tp - 1):
            self.each(distance, lambda copy: copy.wait_send())


def turned(rows, cosine, sine):
    return rows * cosine + pltpu.roll(rows, rows.shape[1] // 2, 1) * sine


def forward_kernel(
    dp, tp, kvb_count, qb_count,
    x, seg_row, seg_col, zq, zo, zb, kvs, ff, cot,
    ff_out, cot_out, n2_out, wq_out, wo_out, wkv_out, p_out,
    res, att, n1, q, kv, cosine, sine, vectors,
    wq, wo, wkv, wb, spread, mask, probs, n2,
    plane_send, plane_recv, line_send, line_recv, local_sem, probs_sem,
):
    place = Place(dp, tp)
    d, z = place.d, place.z
    own_rows, width = x.shape
    depth, columns = zq.shape
    items = seg_row.shape[1]
    head = HEAD_DIMENSION
    kv_columns = kv.shape[1]
    my_rows = pl.ds(pl.multiple_of(d * depth, 16), depth)

    def rows_of(b):
        return pl.ds(pl.multiple_of(b * depth, 16), depth)

    def plane(item, own, full):
        return PlaneGather(
            place, own, full, lambda m: plane_send.at[item, m], lambda m: plane_recv.at[item, m]
        )

    def line(item, own, full, offsets=(1, -1)):
        return LineGather(
            place,
            own,
            full,
            lambda s, k: line_send.at[item, s, k],
            lambda s, k: line_recv.at[item, s, k],
            offsets,
        )

    starts = [
        pltpu.make_async_copy(zq, wq.at[z, my_rows], local_sem.at[0]),
        pltpu.make_async_copy(zo, wo.at[z, my_rows], local_sem.at[1]),
        pltpu.make_async_copy(zb, wb.at[d, z], local_sem.at[2]),
        pltpu.make_async_copy(kvs, wkv.at[my_rows], local_sem.at[3]),
        pltpu.make_async_copy(ff, ff_out.at[d], local_sem.at[4]),
        pltpu.make_async_copy(cot, cot_out.at[z], local_sem.at[5]),
    ]
    for copy in starts:
        copy.start()
    place.greet(True, True)
    line_q = line(0, zq, lambda t: wq.at[t, my_rows])
    line_o = line(1, zo, lambda t: wo.at[t, my_rows])
    line_b = line(2, zb, lambda t: wb.at[d, t])
    line_cot = line(3, cot, lambda t: cot_out.at[t])
    line_kv = line(
        4,
        kv.at[pl.ds(pl.multiple_of(z * own_rows, 16), own_rows)],
        lambda t: kv.at[pl.ds(pl.multiple_of(t * own_rows, 16), own_rows)],
        (1,),
    )
    line_n2 = line(5, n2, lambda t: n2_out.at[t])
    plane_kv = plane(0, kvs, lambda b: wkv.at[rows_of(b)])
    plane_q = plane(1, wq.at[:, my_rows], lambda b: wq.at[:, rows_of(b)])
    plane_o = plane(2, wo.at[:, my_rows], lambda b: wo.at[:, rows_of(b)])
    plane_b = plane(3, wb.at[d], lambda b: wb.at[b])
    plane_ff = [
        plane(4 + part, ff.at[part], lambda b, part=part: ff_out.at[b, part]) for part in (2, 0, 1)
    ]
    line_b.start()
    line_q.start()
    plane_kv.start()

    begin = z * own_rows
    row_at = begin + lax.broadcasted_iota(jnp.int32, (own_rows, items), 0)
    col_at = lax.broadcasted_iota(jnp.int32, (own_rows, items), 1)
    mine, theirs = seg_col[...], seg_row[...]
    allowed = (mine == theirs) & (col_at <= row_at)
    mask[...] = jnp.where(allowed, 0.0, NEGATIVE)
    below = jnp.sum(jnp.where(theirs < mine, 1.0, 0.0), axis=1, keepdims=True)
    lane = lax.broadcasted_iota(jnp.int32, (own_rows, head), 1)
    half = lane % (head // 2)
    index = begin + lax.broadcasted_iota(jnp.int32, (own_rows, head), 0)
    freqs = jnp.exp(half.astype(F32) * (-2.0 * math.log(THETA) / head))
    angles = (index.astype(F32) - below) * freqs
    cosine[...] = jnp.cos(angles)
    sine[...] = jnp.sin(angles) * jnp.where(lane < head // 2, -1.0, 1.0)

    for distance in range(1, tp):
        line_b.hand_on(distance)
    line_q.hand_on(1)
    line_q.hand_on(2)
    plane_kv.spread()
    for distance in range(3, tp):
        line_q.hand_on(distance)
    starts[0].wait()
    plane_q.start()
    starts[2].wait()
    plane_b.start()
    starts[3].wait()
    plane_kv.complete()

    pick_row = lax.broadcasted_iota(jnp.int32, (16, 128), 0)
    pick_col = lax.broadcasted_iota(jnp.int32, (16, 128), 1)
    pick = jnp.where(pick_row == pick_col, 1.0, 0.0).astype(BF16)
    vector_rows = dot_nt(pick, wkv[:, kv_columns:])
    vectors[...] = vector_rows
    block_row = lax.broadcasted_iota(jnp.int32, (depth, kv_columns), 0)
    block_col = lax.broadcasted_iota(jnp.int32, (depth, kv_columns), 1)
    for b in range(dp):
        hit = (block_row < kvb_count) & (block_col == block_row + b * kvb_count)
        spread[b * depth : (b + 1) * depth, :] = jnp.where(hit, 1.0, 0.0).astype(BF16)
    kv_bias = dot(vector_rows.astype(BF16), spread[...])[2:3, :]

    xs = x[...].astype(F32)
    n1[...] = (xs * rms_scale(xs) * vector_rows[0:1, :]).astype(BF16)
    kv_rows = dot(n1[...], wkv[:, :kv_columns]) + kv_bias
    at = pl.ds(pl.multiple_of(begin, 16), own_rows)
    for h in range(KEYVALUE_HEADS):
        cut = slice(h * head, (h + 1) * head)
        kv[at, cut] = turned(kv_rows[:, cut], cosine[...], sine[...]).astype(BF16)
    kv[at, KEYVALUE_HEADS * head :] = kv_rows[:, KEYVALUE_HEADS * head :].astype(BF16)
    line_kv.start()
    line_o.start()
    line_kv.hand_on(1)
    plane_b.spread()
    for mask_of in range(1, 1 << place.steps):
        if mask_of == plane_q.half - 1:
            plane_ff[0].start()
            line_kv.hand_on(2)
        plane_q.hand_on(mask_of)
    for distance in range(1, tp):
        line_o.hand_on(distance)
    starts[1].wait()
    plane_o.start()
    for distance in range(3, tp):
        line_kv.hand_on(distance)
    line_cot.start()
    plane_b.complete()
    small_row = lax.broadcasted_iota(jnp.int32, (128, columns), 0)
    small_col = lax.broadcasted_iota(jnp.int32, (128, columns), 1)
    q_bias = jnp.zeros((tp * 16, columns), F32)
    for b in range(dp):
        hit = (small_row < qb_count) & (small_col == small_row + b * qb_count)
        one = jnp.where(hit, 1.0, 0.0).astype(BF16)
        q_bias = q_bias + dot(wb[b].reshape(tp * 16, 128), one)
    plane_q.complete()
    for t in range(tp):
        rows = dot(n1[...], wq[t]) + q_bias[t * 16 : t * 16 + 1, :]
        for h in range(columns // head):
            cut = slice(h * head, (h + 1) * head)
            out = slice(t * columns + h * head, t * columns + (h + 1) * head)
            q[:, out] = turned(rows[:, cut], cosine[...], sine[...]).astype(BF16)
    outs = [
        pltpu.make_async_copy(wq, wq_out, local_sem.at[0]),
        pltpu.make_async_copy(wkv, wkv_out, local_sem.at[3]),
    ]
    for copy in outs:
        copy.start()

    scale = 1.0 / math.sqrt(head)
    group = QUERY_HEADS // tp

    def probs_copy(part, count):
        at = pl.ds(part * group, group)
        return pltpu.make_async_copy(
            probs.at[at, :, pl.ds(0, count)], p_out.at[at, :, pl.ds(0, count)], probs_sem.at[part]
        )

    for part in range(tp):
        for blocks in range(1, tp + 1):
            count = blocks * own_rows

            @pl.when(z == blocks - 1)
            def _():
                def one_head(i, carry):
                    h = part * group + i
                    at = pl.ds(pl.multiple_of(h * head, head), head)
                    shared = h // REPEAT
                    key_at = pl.ds(pl.multiple_of(shared * head, head), head)
                    value_at = pl.ds(pl.multiple_of((KEYVALUE_HEADS + shared) * head, head), head)
                    scores = dot_nt(q[:, at], kv[0:count, key_at]) * scale + mask[:, 0:count]
                    top = jnp.max(scores, axis=1, keepdims=True)
                    weights = jnp.exp(scores - top)
                    total = jnp.sum(weights, axis=1, keepdims=True)
                    low = (weights / total).astype(BF16)
                    probs[h, :, 0:count] = low
                    att[:, at] = dot(low, kv[0:count, value_at]).astype(BF16)
                    return carry

                lax.fori_loop(0, group, one_head, 0)
                probs_copy(part, count).start()

    plane_ff[1].start()
    line_cot.hand_on(1)
    plane_o.spread()
    line_cot.hand_on(2)
    plane_o.complete()
    outs.append(pltpu.make_async_copy(wo, wo_out, local_sem.at[1]))
    outs[-1].start()
    for j in range(width // 512):
        cut = slice(j * 512, (j + 1) * 512)
        acc = x[:, cut].astype(F32)
        for t in range(tp):
            acc = acc + dot_nt(att[:, t * columns : (t + 1) * columns], wo[t, cut, :])
        res[:, cut] = acc
    residual = res[...]
    n2[...] = (residual * rms_scale(residual) * vectors[1:2, :]).astype(BF16)
    line_n2.start()
    n2_copy = pltpu.make_async_copy(n2, n2_out.at[z], local_sem.at[2])
    n2_copy.start()
    plane_ff[0].spread()
    plane_ff[2].start()
    for distance in range(3, tp):
        line_cot.hand_on(distance)
    line_n2.hand_on(1)
    plane_ff[1].spread()
    line_n2.hand_on(2)
    plane_ff[2].spread()
    for distance in range(3, tp):
        line_n2.hand_on(distance)
    for item in plane_ff:
        item.complete()
    for item in [plane_kv, plane_q, plane_o, plane_b] + plane_ff:
        item.finish()
    for item in (line_q, line_o, line_b, line_cot, line_kv, line_n2):
        item.finish()
    for copy in starts[4:] + outs + [n2_copy]:
        copy.wait()
    for part in range(tp):
        for blocks in range(1, tp + 1):

            @pl.when(z == blocks - 1)
            def _():
                probs_copy(part, blocks * own_rows).wait()


def forward_part(dp, tp, kvb_count, qb_count, x, seg_row, seg_col, zq, zo, zb, kvs, ff, cot):
    def shape(*dims, kind=BF16):
        return jax.ShapeDtypeStruct(dims, kind)

    own_rows, width = x.shape
    depth, columns = zq.shape
    items = seg_row.shape[1]
    head = HEAD_DIMENSION
    kv_columns = 2 * KEYVALUE_HEADS * head
    vmem = pl.BlockSpec(memory_space=pltpu.VMEM)
    anywhere = pl.BlockSpec(memory_space=ANY)
    return pl.pallas_call(
        functools.partial(forward_kernel, dp, tp, kvb_count, qb_count),
        out_shape=(
            shape(dp, *ff.shape),
            shape(tp, *cot.shape),
            shape(tp, own_rows, width),
            shape(tp, width, columns),
            shape(tp, width, columns),
            shape(width, kvs.shape[1]),
            shape(QUERY_HEADS, own_rows, items),
            shape(own_rows, width, kind=F32),
            shape(own_rows, tp * columns),
            shape(own_rows, width),
            shape(own_rows, tp * columns),
            shape(items, kv_columns),
            shape(own_rows, head, kind=F32),
            shape(own_rows, head, kind=F32),
            shape(16, width, kind=F32),
        ),
        in_specs=[vmem] * 9,
        out_specs=(anywhere,) * 7 + (vmem,) * 8,
        scratch_shapes=[
            pltpu.VMEM((tp, width, columns), BF16),
            pltpu.VMEM((tp, width, columns), BF16),
            pltpu.VMEM((width, kvs.shape[1]), BF16),
            pltpu.VMEM((dp, tp, 16, 128), BF16),
            pltpu.VMEM((width, kv_columns), BF16),
            pltpu.VMEM((own_rows, items), F32),
            pltpu.VMEM((QUERY_HEADS, own_rows, items), BF16),
            pltpu.VMEM((own_rows, width), BF16),
            pltpu.SemaphoreType.DMA((7, dp)),
            pltpu.SemaphoreType.DMA((7, dp)),
            pltpu.SemaphoreType.DMA((6, 2, tp)),
            pltpu.SemaphoreType.DMA((6, 2, tp)),
            pltpu.SemaphoreType.DMA((6,)),
            pltpu.SemaphoreType.DMA((tp,)),
        ],
        compiler_params=pltpu.CompilerParams(
            collective_id=0, has_side_effects=True, vmem_limit_bytes=56 << 20
        ),
        name="forward_part",
    )(x, seg_row, seg_col, zq, zo, zb, kvs, ff, cot)


class PlaneReduce:
    def __init__(self, place, part, held, send, recv):
        self.place, self.part, self.held, self.send, self.recv = place, part, held, send, recv
        self.half = 1 << place.steps
        self.last = place.steps

    def count(self, level):
        return self.half >> level

    def slot(self, level, i):
        return sum(self.count(k) for k in range(level)) + i

    def copy(self, level, i):
        place = self.place
        slot = self.slot(level, i)
        if level:
            src, device = self.held(self.slot(level - 1, 2 * i + 1)), place.partners[level - 1]
        else:
            src, device = self.part(place.sibling_block(i)), place.sibling
        return remote(
            src, self.held(slot), self.send(slot), self.recv(slot), place.device(device)
        )

    def start(self, level):
        for i in range(self.count(level)):
            self.copy(level, i).start()

    def wait_send(self, level):
        for i in range(self.count(level)):
            self.copy(level, i).wait_send()

    def absorb(self, level, out=None):
        order = sorted(range(self.count(level)), key=lambda i: 1 - i % 2)
        for i in order:
            slot = self.slot(level, i)
            self.copy(level, i).wait_recv()
            if level:
                other = self.held(self.slot(level - 1, 2 * i))
            else:
                other = self.part(self.place.block(i))
            add_into(self.held(slot), other, self.held(slot) if out is None else out)
            if i % 2:
                self.copy(level + 1, i // 2).start()


def add_into(one, other, out):
    rows = one.shape[0]
    step = 48 if rows % 48 == 0 else rows

    def body(k, carry):
        at = pl.ds(pl.multiple_of(k * step, 16), step)
        out[at, :] = (one[at, :].astype(F32) + other[at, :].astype(F32)).astype(out.dtype)
        return carry

    lax.fori_loop(0, rows // step, body, 0)


FF_PARTS = 3


class LineReduce:
    def __init__(self, place, term, sent, got, send, recv):
        self.place, self.term, self.sent, self.got = place, term, sent, got
        self.send, self.recv = send, recv

    def owner(self, turn):
        place = self.place
        if turn == place.tp - 1:
            return place.z
        falling = place.tp - 1 - turn
        falling = jnp.where(falling > place.z, falling, falling - 1)
        rising = jnp.where(turn < place.z, turn, turn + 1)
        return jnp.where(place.z < place.tp // 2, falling, rising)

    def way(self, turn):
        place = self.place
        owner = self.owner(turn)
        right = jnp.where(owner > place.z, 1, 0)
        side, offset = 1 - right, 2 * right - 1
        return side, offset, (owner - place.z) * offset

    def copy(self, turn):
        side, offset, distance = self.way(turn)
        return remote(
            self.sent(turn),
            self.got(side, distance - 1),
            self.send(turn),
            self.recv(side, distance - 1),
            self.place.beside(offset),
        )

    def arrival(self, side, distance):
        ref = self.got(side, distance)
        return remote(
            ref, ref, self.send(0), self.recv(side, distance), self.place.beside(0)
        )

    def direct(self, turn):
        side, offset, distance = self.way(turn)

        @pl.when(jnp.logical_not(self.place.has(-offset)))
        def _():
            copy_into(self.term(turn), self.sent(turn))
            self.copy(turn).start()

    def added(self, turn):
        side, offset, distance = self.way(turn)

        @pl.when(self.place.has(-offset))
        def _():
            self.arrival(side, distance).wait_recv()
            add_into(self.term(turn), self.got(side, distance), self.sent(turn))
            self.copy(turn).start()

    def total(self, out):
        last = self.place.tp - 1
        copy_into(self.term(last), out)
        for side, offset in ((0, -1), (1, 1)):

            @pl.when(self.place.has(offset))
            def _():
                self.arrival(side, 0).wait_recv()
                add_into(out, self.got(side, 0), out)

    def finish(self):
        for turn in range(self.place.tp - 1):
            self.copy(turn).wait_send()


def copy_into(one, out):
    rows = one.shape[0]
    step = 32 if rows % 32 == 0 else rows

    def body(k, carry):
        at = pl.ds(pl.multiple_of(k * step, 16), step)
        out[at, :] = one[at, :].astype(out.dtype)
        return carry

    lax.fori_loop(0, rows // step, body, 0)


def ff_kernel(
    dp, tp, ff, cot, n2, act, lhs, mlp, d2,
    wg, wu, wd, x, ct, made, term, sent, got, branch, turned_rows,
    w_sem, in_sem, act_sem, lhs_sem, mlp_sem, send_sem, recv_sem,
):
    place = Place(dp, tp)
    own_rows, width = d2.shape
    depth = ff.shape[2]
    padded = ff.shape[3]
    tile = 256
    third = padded // 3
    weights = (wg, wu, wd)
    loads = [
        [
            pltpu.make_async_copy(
                ff.at[b, p, :, pl.ds(c * third, third)],
                weights[p].at[pl.ds(b * depth, depth), pl.ds(c * third, third)],
                w_sem.at[p, b, c],
            )
            for p in range(FF_PARTS)
            for b in range(dp)
        ]
        for c in range(3)
    ]
    sums = LineReduce(
        place,
        lambda turn: term.at[turn % 2],
        lambda turn: sent.at[turn],
        lambda side, k: got.at[side, k],
        lambda turn: send_sem.at[turn],
        lambda side, k: recv_sem.at[side, k],
    )

    def fetch(turn):
        owner = sums.owner(turn)
        return [
            pltpu.make_async_copy(n2.at[owner], x.at[turn % 2], in_sem.at[turn % 2, 0]),
            pltpu.make_async_copy(cot.at[owner], ct.at[turn % 2], in_sem.at[turn % 2, 1]),
        ]

    def stores(turn, kinds=(0, 1, 2)):
        return [copies() for kind, copies in enumerate(store_kinds(turn)) if kind in kinds]

    def store_kinds(turn):
        owner = sums.owner(turn)
        at = pl.ds(pl.multiple_of(owner * own_rows, 128), own_rows)
        slot = turn % 2
        return (
            lambda: [
                pltpu.make_async_copy(made.at[slot, p], act.at[p, at], act_sem.at[slot, p])
                for p in range(FF_PARTS)
            ],
            lambda: [
                pltpu.make_async_copy(
                    turned_rows.at[slot, k], lhs.at[k, :, at], lhs_sem.at[slot, k]
                )
                for k in range(2)
            ],
            lambda: [pltpu.make_async_copy(branch.at[slot], mlp.at[owner], mlp_sem.at[slot])],
        )

    for copy in fetch(0):
        copy.start()
    for part in loads:
        for copy in part:
            copy.start()
    place.greet(False, True)
    for turn in range(tp):
        slot = turn % 2
        for copy in fetch(turn):
            copy.wait()
        if turn + 1 < tp:
            for copy in fetch(turn + 1):
                copy.start()
        if turn >= 2:
            for copies in stores(turn - 2):
                for copy in copies:
                    copy.wait()
        turned_rows[slot, 0] = x[slot].T
        turned_rows[slot, 1] = ct[slot].T
        for copy in stores(turn, (1,))[0]:
            copy.start()

        def units(n, carry, slot=slot):
            for k in range(3):
                at = pl.ds(pl.multiple_of((n * 3 + k) * tile, tile), tile)
                gate = dot(x[slot], wg[:, at])
                upper = dot(x[slot], wu[:, at])
                d_hidden = dot(ct[slot], wd[:, at])
                sigmoid = 1.0 / (1.0 + jnp.exp(-gate))
                swish = gate * sigmoid
                made[slot, 2, :, at] = (swish * upper).astype(BF16)
                made[slot, 1, :, at] = (d_hidden * swish).astype(BF16)
                made[slot, 0, :, at] = (
                    d_hidden * upper * sigmoid * (1.0 + gate * (1.0 - sigmoid))
                ).astype(BF16)
            return carry

        if turn == 0:
            for c in range(3):
                for copy in loads[c]:
                    copy.wait()
                lax.fori_loop(
                    c * (third // (3 * tile)), (c + 1) * (third // (3 * tile)), units, 0
                )
        else:
            lax.fori_loop(0, padded // (3 * tile), units, 0)

        def columns(n, carry, slot=slot):
            at = pl.ds(pl.multiple_of(n * tile, tile), tile)
            term[slot, :, at] = dot_nt(made[slot, 0], wg[at, :]) + dot_nt(
                made[slot, 1], wu[at, :]
            )
            branch[slot, :, at] = dot_nt(made[slot, 2], wd[at, :]).astype(BF16)
            return carry

        lax.fori_loop(0, width // tile, columns, 0)
        if turn < tp - 1:
            sums.direct(turn)
        for copies in stores(turn, (0, 2)):
            for copy in copies:
                copy.start()
        if 0 < turn < tp - 1:
            sums.added(turn - 1)
        if turn == tp - 2:
            sums.added(turn)
    sums.total(d2)
    sums.finish()
    for turn in range(tp - 2, tp):
        for copies in stores(turn):
            for copy in copies:
                copy.wait()


def ff_part(dp, tp, ff, cot, n2):
    def shape(*dims, kind=BF16):
        return jax.ShapeDtypeStruct(dims, kind)

    own_rows, width = cot.shape[1:]
    padded = ff.shape[3]
    vmem = pl.BlockSpec(memory_space=pltpu.VMEM)
    anywhere = pl.BlockSpec(memory_space=ANY)
    return pl.pallas_call(
        functools.partial(ff_kernel, dp, tp),
        out_shape=(
            shape(FF_PARTS, tp * own_rows, padded),
            shape(2, width, tp * own_rows),
            shape(tp, own_rows, width),
            shape(own_rows, width, kind=F32),
        ),
        in_specs=[anywhere] * 3,
        out_specs=(anywhere,) * 3 + (vmem,),
        scratch_shapes=[
            pltpu.VMEM((width, padded), BF16),
            pltpu.VMEM((width, padded), BF16),
            pltpu.VMEM((width, padded), BF16),
            pltpu.VMEM((2, own_rows, width), BF16),
            pltpu.VMEM((2, own_rows, width), BF16),
            pltpu.VMEM((2, FF_PARTS, own_rows, padded), BF16),
            pltpu.VMEM((2, own_rows, width), F32),
            pltpu.VMEM((tp - 1, own_rows, width), BF16),
            pltpu.VMEM((2, tp - 1, own_rows, width), BF16),
            pltpu.VMEM((2, own_rows, width), BF16),
            pltpu.VMEM((2, 2, width, own_rows), BF16),
            pltpu.SemaphoreType.DMA((FF_PARTS, dp, 3)),
            pltpu.SemaphoreType.DMA((2, 2)),
            pltpu.SemaphoreType.DMA((2, FF_PARTS)),
            pltpu.SemaphoreType.DMA((2, 2)),
            pltpu.SemaphoreType.DMA((2,)),
            pltpu.SemaphoreType.DMA((tp - 1,)),
            pltpu.SemaphoreType.DMA((2, tp - 1)),
        ],
        compiler_params=pltpu.CompilerParams(
            collective_id=3, has_side_effects=True, vmem_limit_bytes=60 << 20
        ),
        name="ff_part",
    )(ff, cot, n2)


class DownReduce:
    def __init__(self, place, term, got, send, recv):
        self.place, self.term, self.got, self.send, self.recv = place, term, got, send, recv

    def copy(self, distance):
        return remote(
            self.term(self.place.z - distance),
            self.got(distance - 1),
            self.send(distance),
            self.recv(distance - 1),
            self.place.beside(-1),
        )

    def take(self, distance, out):
        place = self.place

        @pl.when(place.z < place.tp - 1)
        def _():
            ref = self.got(distance)
            remote(
                ref, ref, self.send(distance), self.recv(distance), place.beside(0)
            ).wait_recv()
            add_into(out, ref, out)

    def step(self, distance):
        place = self.place

        @pl.when(place.z >= distance)
        def _():
            if distance < place.tp - 1:
                self.take(distance, self.term(place.z - distance))
            self.copy(distance).start()

    def finish(self):
        for distance in range(1, self.place.tp):

            @pl.when(self.place.z >= distance)
            def _():
                self.copy(distance).wait_send()


def backward_kernel(
    dp, tp, chunk,
    res, vectors, att, q, kv, cosine, sine, d2, cot, x, lhs, act, mlp, probs, wo, wq, wkv,
    out, mlp_sent, mlp_got, d_branch, d_qkv, output, input_grad, vector_grads,
    part, taken, held, left, block, stage, weight, kv_weight, prob, d_att, d_kv, d_kv_low, kv_got,
    acc, wide, own_bf, d_res,
    act_sem, send_sem, recv_sem, left_sem, stage_sem, line_send, line_recv, out_sem, weight_sem,
    prob_sem, kv_send, kv_recv, in_sem,
):
    place = Place(dp, tp)
    z = place.z
    own_rows, width = res.shape
    depth = width // dp
    group = max(1, 384 // depth)
    tile = 256
    head = HEAD_DIMENSION
    scale = 1.0 / math.sqrt(head)
    columns = wq.shape[2]
    heads_width = tp * columns
    half_kv = KEYVALUE_HEADS * head
    per_part = act.shape[2] // chunk
    units = [(p, k) for p in (2, 0, 1) for k in range(per_part)]

    def fetch(u):
        p, k = units[u]
        return pltpu.make_async_copy(
            act.at[p, :, pl.ds(k * chunk, chunk)], taken.at[u % 2], act_sem.at[u % 2]
        )

    def fetch_left(k):
        return pltpu.make_async_copy(lhs.at[k], left, left_sem.at[0])

    def fetch_weight(n):
        source = wo if n < tp else wq
        return pltpu.make_async_copy(source.at[n % tp], weight.at[n % 2], weight_sem.at[n % 2])

    def fetch_probs(h, slot):
        return pltpu.make_async_copy(probs.at[h], prob.at[slot], prob_sem.at[slot])

    d2_copy = pltpu.make_async_copy(d2, wide, in_sem.at[0])
    cot_copy = pltpu.make_async_copy(cot, own_bf, in_sem.at[1])
    x_copy = pltpu.make_async_copy(x, own_bf, in_sem.at[2])
    kv_weight_copy = pltpu.make_async_copy(
        wkv.at[:, pl.ds(0, 2 * half_kv)], kv_weight, in_sem.at[3]
    )
    fetch_left(1).start()
    fetch(0).start()
    for copy in (d2_copy, cot_copy, fetch_weight(0), fetch_weight(1), kv_weight_copy):
        copy.start()
    for h in range(2):
        fetch_probs(h, h).start()
    place.greet(True, True)

    line = LineReduce(
        place,
        None,
        lambda turn: mlp_sent.at[turn],
        lambda side, k: mlp_got.at[side, k],
        lambda turn: line_send.at[turn],
        lambda side, k: line_recv.at[side, k],
    )

    def load_term(turn):
        return pltpu.make_async_copy(mlp.at[line.owner(turn)], stage.at[0], stage_sem.at[0])

    def load_got(side, distance):
        return pltpu.make_async_copy(mlp_got.at[side, distance], stage.at[1], stage_sem.at[1])

    def line_direct(turn):
        side, offset, distance = line.way(turn)

        @pl.when(jnp.logical_not(place.has(-offset)))
        def _():
            remote(
                mlp.at[line.owner(turn)],
                mlp_got.at[side, distance - 1],
                line_send.at[turn],
                line_recv.at[side, distance - 1],
                place.beside(offset),
            ).start()

    def line_step(turn):
        side, offset, distance = line.way(turn)

        @pl.when(place.has(-offset))
        def _():
            load_term(turn).start()
            line.arrival(side, distance).wait_recv()
            load_got(side, distance).start()
            load_term(turn).wait()
            load_got(side, distance).wait()
            add_into(stage.at[0], stage.at[1], stage.at[0])
            store = pltpu.make_async_copy(stage.at[0], mlp_sent.at[turn], stage_sem.at[0])
            store.start()
            store.wait()
            line.copy(turn).start()

    def line_total():
        load_term(tp - 1).start()
        load_term(tp - 1).wait()
        add_into(res, stage.at[0], d_res)
        for side, offset in ((0, -1), (1, 1)):

            @pl.when(place.has(offset))
            def _():
                line.arrival(side, 0).wait_recv()
                load_got(side, 0).start()
                load_got(side, 0).wait()
                add_into(d_res, stage.at[1], d_res)

        copy_into(d_res, output)

    for turn in range(tp - 1):
        line_direct(turn)
    down = DownReduce(
        place,
        lambda r: d_kv_low.at[pl.ds(pl.multiple_of(r * own_rows, 16), own_rows)],
        lambda k: kv_got.at[k],
        lambda k: kv_send.at[k],
        lambda k: kv_recv.at[k],
    )

    def second_norm():
        d2_copy.wait()
        cot_copy.wait()
        values, grad = res[...], wide[...]
        s = rms_scale(values)
        normed = values * s
        weighted = grad * vectors[1:2, :]
        inner = jnp.mean(weighted * normed, axis=1, keepdims=True)
        found = own_bf[...].astype(F32) + s * (weighted - normed * inner)
        d_res[...] = found
        d_branch[...] = found.astype(BF16)
        vector_grads[...] = jnp.zeros_like(vector_grads)
        vector_grads[1:2, :] = jnp.sum(grad * normed, axis=0, keepdims=True)
        x_copy.start()
        d_kv[...] = jnp.zeros_like(d_kv)

    def attended_grad(ts):
        for t in ts:
            fetch_weight(t).wait()
            d_att[:, t * columns : (t + 1) * columns] = dot(d_branch[...], weight[t % 2]).astype(
                BF16
            )
            fetch_weight(t + 2).start()

    def some_heads(begin, end):
        def one_head(h, carry):
            slot = h % 2
            at = pl.ds(pl.multiple_of(h * head, head), head)
            shared = h // REPEAT
            key_at = pl.ds(pl.multiple_of(shared * head, head), head)
            value_at = pl.ds(pl.multiple_of(half_kv + shared * head, head), head)
            fetch_probs(h, slot).wait()
            d_out = d_att[:, at]
            inner = jnp.sum(
                d_out.astype(F32) * att[:, at].astype(F32), axis=1, keepdims=True
            )
            acc[...] = jnp.zeros_like(acc)

            def one_block(j, carry):
                rows = pl.ds(pl.multiple_of(j * own_rows, 256), own_rows)
                low = prob[slot, :, rows]
                d_probs = dot_nt(d_out, kv[rows, value_at])
                d_scores = (low.astype(F32) * (scale * (d_probs - inner))).astype(BF16)
                acc[...] += dot(d_scores, kv[rows, key_at])
                d_kv[rows, key_at] += dot_tn(d_scores, q[:, at])
                d_kv[rows, value_at] += dot_tn(low, d_out)
                return carry

            lax.fori_loop(0, z + 1, one_block, 0)
            d_qkv[:, at] = turned(acc[...], cosine[...], -sine[...]).astype(BF16)

            @pl.when(h + 2 < QUERY_HEADS)
            def _():
                fetch_probs(h + 2, slot).start()

            return carry

        lax.fori_loop(begin, end, one_head, 0)

    def send_kv():
        def body(j, carry):
            rows = pl.ds(pl.multiple_of(j * own_rows, 256), own_rows)
            d_kv_low[rows, :] = d_kv[rows, :].astype(BF16)
            return carry

        lax.fori_loop(0, z + 1, body, 0)
        down.step(tp - 1)
        for distance in range(tp - 2, 0, -1):
            down.step(distance)

    def normed_grad(ts):
        for t in ts:
            fetch_weight(tp + t).wait()
            for j in range(width // 512):
                cut = slice(j * 512, (j + 1) * 512)
                found = dot_nt(
                    d_qkv[:, t * columns : (t + 1) * columns], weight[(tp + t) % 2, cut, :]
                )
                wide[:, cut] = found + wide[:, cut] if t else found
            if t + 2 < tp:
                fetch_weight(tp + t + 2).start()

    def first_norm():
        mine = pl.ds(pl.multiple_of(z * own_rows, 16), own_rows)
        down.take(0, d_kv.at[mine])
        for h in range(KEYVALUE_HEADS):
            cut = slice(h * head, (h + 1) * head)
            d_qkv[:, heads_width + h * head : heads_width + (h + 1) * head] = turned(
                d_kv[mine, cut], cosine[...], -sine[...]
            ).astype(BF16)
        d_qkv[:, heads_width + half_kv :] = d_kv[mine, half_kv:].astype(BF16)
        kv_weight_copy.wait()
        for j in range(width // 512):
            cut = slice(j * 512, (j + 1) * 512)
            wide[:, cut] += dot_nt(d_qkv[:, heads_width:], kv_weight[cut, :])
        x_copy.wait()
        values, grad = own_bf[...].astype(F32), wide[...]
        s = rms_scale(values)
        normed = values * s
        weighted = grad * vectors[0:1, :]
        inner = jnp.mean(weighted * normed, axis=1, keepdims=True)
        input_grad[...] = (d_res[...] + s * (weighted - normed * inner)).astype(BF16)
        vector_grads[0:1, :] = jnp.sum(grad * normed, axis=0, keepdims=True)
        sums_of = jnp.sum(d_qkv[...].astype(F32), axis=0, keepdims=True)
        vector_grads[2:3, :] = sums_of[:, :heads_width]
        vector_grads[3:4, : 2 * half_kv] = sums_of[:, heads_width:]

    per = QUERY_HEADS // tp
    pieces = [
        [second_norm, lambda: attended_grad(range(tp))],
        [lambda: some_heads(0, 2)],
        [lambda: some_heads(2, 4), lambda: line_step(0)],
        [lambda: some_heads(4, 6)],
        [lambda: some_heads(6, 8), lambda: line_step(1)],
        [lambda: some_heads(8, 10), lambda: line_step(2)],
        [lambda: some_heads(10, 12), send_kv],
        [lambda: normed_grad(range(tp))],
        [],
        [first_norm],
        [line_total],
    ]

    def stored(u):
        p, k = units[u]
        return pltpu.make_async_copy(
            block.at[u % 2], out.at[p, :, pl.ds(k * chunk, chunk)], out_sem.at[u % 2]
        )

    sums = [
        PlaneReduce(
            place,
            lambda b, u=u: part.at[u % 2, b],
            lambda s, u=u: held.at[u, s],
            lambda s, u=u: send_sem.at[u, s],
            lambda s, u=u: recv_sem.at[u, s],
        )
        for u in range(len(units))
    ]
    last = place.steps
    fetch_left(1).wait()
    for turn in range(max(len(units) + last + 1, len(pieces))):
        if turn < len(units):
            u = turn
            p, k = units[u]
            if u + 1 < len(units):
                fetch(u + 1).start()
            if u == per_part:
                fetch_left(0).wait()
            fetch(u).wait()
            if u >= 2:
                sums[u - 2].wait_send(0)

            def body(n, carry, u=u):
                i, j = n // (chunk // tile), n % (chunk // tile)
                rows = pl.ds(pl.multiple_of(i * (group * depth), 16), group * depth)
                cols = pl.ds(pl.multiple_of(j * tile, tile), tile)
                found = dot(left[rows, :], taken[u % 2, :, cols]).astype(BF16)
                for g in range(group):
                    part[u % 2, i * group + g, :, cols] = found[g * depth : (g + 1) * depth]
                return carry

            lax.fori_loop(0, dp // group * (chunk // tile), body, 0)
            sums[u].start(0)
            if u == per_part - 1:
                fetch_left(0).start()
        for level in range(last + 1):
            u = turn - 1 - level
            if 0 <= u < len(units):
                if level == last:
                    if u >= 2:
                        stored(u - 2).wait()
                    sums[u].absorb(level, block.at[u % 2])
                    stored(u).start()
                else:
                    sums[u].absorb(level)
        if turn < len(pieces):
            for piece in pieces[turn]:
                piece()
    line.finish()
    down.finish()
    for u in range(len(units)):
        if u >= len(units) - 2:
            stored(u).wait()
        for level in range(0 if u >= len(units) - 2 else 1, last + 1):
            sums[u].wait_send(level)


def backward_part(
    dp, tp, res, vectors, att, q, kv, cosine, sine, d2, cot, x, lhs, act, mlp, probs, wo, wq, wkv
):
    def shape(*dims, kind=BF16):
        return jax.ShapeDtypeStruct(dims, kind)

    own_rows, width = res.shape
    depth = width // dp
    items, padded = act.shape[1:]
    columns = wq.shape[2]
    kv_columns = kv.shape[1]
    chunk = 768
    count = FF_PARTS * padded // chunk
    vmem = pl.BlockSpec(memory_space=pltpu.VMEM)
    anywhere = pl.BlockSpec(memory_space=ANY)
    return pl.pallas_call(
        functools.partial(backward_kernel, dp, tp, chunk),
        out_shape=(
            shape(FF_PARTS, depth, padded, kind=F32),
            shape(tp - 1, own_rows, width),
            shape(2, tp - 1, own_rows, width),
            shape(own_rows, width),
            shape(own_rows, tp * columns + kv_columns),
            shape(own_rows, width),
            shape(own_rows, width),
            shape(8, width, kind=F32),
        ),
        in_specs=[vmem] * 7 + [anywhere] * 10,
        out_specs=(anywhere,) * 3 + (vmem,) * 5,
        scratch_shapes=[
            pltpu.VMEM((2, dp, depth, chunk), BF16),
            pltpu.VMEM((2, items, chunk), BF16),
            pltpu.VMEM((count, dp - 1, depth, chunk), BF16),
            pltpu.VMEM((width, items), BF16),
            pltpu.VMEM((2, depth, chunk), F32),
            pltpu.VMEM((2, own_rows, width), BF16),
            pltpu.VMEM((2, width, columns), BF16),
            pltpu.VMEM((width, kv_columns), BF16),
            pltpu.VMEM((2, own_rows, items), BF16),
            pltpu.VMEM((own_rows, tp * columns), BF16),
            pltpu.VMEM((items, kv_columns), F32),
            pltpu.VMEM((items, kv_columns), BF16),
            pltpu.VMEM((tp - 1, own_rows, kv_columns), BF16),
            pltpu.VMEM((own_rows, HEAD_DIMENSION), F32),
            pltpu.VMEM((own_rows, width), F32),
            pltpu.VMEM((own_rows, width), BF16),
            pltpu.VMEM((own_rows, width), F32),
            pltpu.SemaphoreType.DMA((2,)),
            pltpu.SemaphoreType.DMA((count, dp - 1)),
            pltpu.SemaphoreType.DMA((count, dp - 1)),
            pltpu.SemaphoreType.DMA((1,)),
            pltpu.SemaphoreType.DMA((2,)),
            pltpu.SemaphoreType.DMA((tp - 1,)),
            pltpu.SemaphoreType.DMA((2, tp - 1)),
            pltpu.SemaphoreType.DMA((2,)),
            pltpu.SemaphoreType.DMA((2,)),
            pltpu.SemaphoreType.DMA((2,)),
            pltpu.SemaphoreType.DMA((tp,)),
            pltpu.SemaphoreType.DMA((tp - 1,)),
            pltpu.SemaphoreType.DMA((4,)),
        ],
        compiler_params=pltpu.CompilerParams(
            collective_id=1, has_side_effects=True, vmem_limit_bytes=63 << 20
        ),
        name="backward_part",
    )(res, vectors, att, q, kv, cosine, sine, d2, cot, x, lhs, act, mlp, probs, wo, wq, wkv)


def attn_grad_kernel(
    dp, tp, widths, n1, d_qkv, d_branch, att, vectors, kv_out, q_out, o_out, vectors_out,
    turned_rows, part, held, own, line_kv, line_qo, vector_sum, vector_got, line_vector,
    send_sem, recv_sem, line_send, line_recv, vector_send, vector_recv,
):
    place = Place(dp, tp)
    z = place.z
    depth, columns = q_out.shape
    width = dp * depth
    heads_width = tp * columns
    barrier = pltpu.get_barrier_semaphore()
    for partner in place.partners + [place.sibling]:
        pl.semaphore_signal(barrier, inc=1, device_id=place.device(partner), device_id_type=MESH)
    for t in range(tp):

        @pl.when(t != z)
        def _():
            pl.semaphore_signal(barrier, inc=1, device_id=(place.d, t), device_id_type=MESH)

    pl.semaphore_wait(barrier, place.steps + tp)
    kinds = (0, 0, 2, 1, 1)
    halves = (0, 1, 0, 0, 1)
    count = len(widths)
    group = max(1, 384 // depth)
    sums = [
        PlaneReduce(
            place,
            lambda b, u=u: part.at[u, b, :, pl.ds(0, widths[u])],
            lambda s, u=u: held.at[u, s, :, pl.ds(0, widths[u])],
            lambda s, u=u: send_sem.at[u, s],
            lambda s, u=u: recv_sem.at[u, s],
        )
        for u in range(count)
    ]

    def make(u):
        kind, half = kinds[u], halves[u]
        left = 1 if kind == 1 else 0
        right = att if kind == 1 else d_qkv
        base = heads_width if kind == 2 else half * widths[u]

        def body(i, carry):
            rows = pl.ds(pl.multiple_of(i * (group * depth), 16), group * depth)
            for j in range(widths[u] // 256):
                found = dot(
                    turned_rows[left, rows, :], right[:, base + j * 256 : base + (j + 1) * 256]
                ).astype(BF16)
                for g in range(group):
                    part[u, i * group + g, :, j * 256 : (j + 1) * 256] = found[
                        g * depth : (g + 1) * depth
                    ]
            return carry

        lax.fori_loop(0, dp // group, body, 0)
        sums[u].start(0)

    def line_copies(u):
        found = []
        kind, half = kinds[u], halves[u]
        for t in range(tp):
            if kind == 2:
                src, dst = own.at[u, :, pl.ds(0, widths[u])], line_kv.at[z]
            elif t // 2 == half:
                src, dst = own.at[u, :, pl.ds((t % 2) * columns, columns)], line_qo.at[kind, z]
            else:
                continue
            found.append((t, remote(
                src, dst, line_send.at[u, t], line_recv.at[kind, z], (place.d, t)
            )))
        return found

    last = place.steps

    def work(turn):
        for level in range(last + 1):
            u = turn - level
            if 0 <= u < count:
                target = own.at[u, :, pl.ds(0, widths[u])] if level == last else None
                sums[u].absorb(level, target)
                if level == last:
                    for t, copy in line_copies(u):

                        @pl.when(t != z)
                        def _():
                            copy.start()

    ways = [place.sibling] + place.partners

    def vector_copy(level):
        return remote(
            vectors if level == 0 else vector_sum.at[level - 1],
            vector_got.at[level],
            vector_send.at[level],
            vector_recv.at[level],
            place.device(ways[level]),
        )

    def vector_step(level):
        vector_copy(level).wait_recv()
        mine = vectors[...] if level == 0 else vector_sum[level - 1]
        vector_sum[level] = mine + vector_got[level]
        if level < last:
            vector_copy(level + 1).start()
        else:
            for t in range(tp):

                @pl.when(t != z)
                def _():
                    vector_line(t).start()

    def vector_line(t):
        return remote(
            vector_sum.at[last],
            line_vector.at[z],
            line_send.at[count, t],
            line_recv.at[3, z],
            (place.d, t),
        )

    vector_copy(0).start()
    turned_rows[0] = n1[...].T
    make(0)
    make(1)
    turned_rows[1] = d_branch[...].T
    for turn in range(count + last):
        work(turn)
        if turn + 2 < count:
            make(turn + 2)
        if turn <= last:
            vector_step(turn)

    def arrived(ref, kind):
        for t in range(tp):

            @pl.when(t != z)
            def _():
                remote(
                    ref.at[t], ref.at[t], line_send.at[0, t], line_recv.at[kind, t], (place.d, t)
                ).wait_recv()

    def total(ref, mine, out):
        acc = mine.astype(F32)
        for t in range(tp):
            acc = acc + jnp.where(t != z, ref[t].astype(F32), 0.0)
        out[...] = acc

    at = pl.ds(pl.multiple_of((z % 2) * columns, 128), columns)
    arrived(line_vector, 3)
    total(line_vector, vector_sum[last], vectors_out)
    arrived(line_qo.at[0], 0)
    total(line_qo.at[0], own[z // 2, :, at], q_out)
    arrived(line_kv, 2)
    total(line_kv, own[2, :, : widths[2]], kv_out)
    arrived(line_qo.at[1], 1)
    total(line_qo.at[1], own[3 + z // 2, :, at], o_out)
    for u in range(count):
        for level in range(last + 1):
            sums[u].wait_send(level)
        for t, copy in line_copies(u):

            @pl.when(t != z)
            def _():
                copy.wait_send()

    for level in range(last + 1):
        vector_copy(level).wait_send()
    for t in range(tp):

        @pl.when(t != z)
        def _():
            vector_line(t).wait_send()


def attn_grads(dp, tp, n1, d_qkv, d_branch, att, vectors):
    own_rows, width = n1.shape
    depth = width // dp
    heads_width = att.shape[1]
    kv_columns = d_qkv.shape[1] - heads_width
    half = heads_width // 2
    widths = (half, half, kv_columns, half, half)
    columns = heads_width // tp
    levels = dp.bit_length() - 1
    vmem = pl.BlockSpec(memory_space=pltpu.VMEM)
    return pl.pallas_call(
        functools.partial(attn_grad_kernel, dp, tp, widths),
        out_shape=(
            jax.ShapeDtypeStruct((depth, kv_columns), F32),
            jax.ShapeDtypeStruct((depth, columns), F32),
            jax.ShapeDtypeStruct((depth, columns), F32),
            jax.ShapeDtypeStruct(vectors.shape, F32),
        ),
        in_specs=[vmem] * 5,
        out_specs=(vmem,) * 4,
        scratch_shapes=[
            pltpu.VMEM((2, width, own_rows), BF16),
            pltpu.VMEM((5, dp, depth, half), BF16),
            pltpu.VMEM((5, dp - 1, depth, half), BF16),
            pltpu.VMEM((5, depth, half), BF16),
            pltpu.VMEM((tp, depth, kv_columns), BF16),
            pltpu.VMEM((2, tp, depth, columns), BF16),
            pltpu.VMEM((levels,) + vectors.shape, F32),
            pltpu.VMEM((levels,) + vectors.shape, F32),
            pltpu.VMEM((tp,) + vectors.shape, F32),
            pltpu.SemaphoreType.DMA((5, dp - 1)),
            pltpu.SemaphoreType.DMA((5, dp - 1)),
            pltpu.SemaphoreType.DMA((6, tp)),
            pltpu.SemaphoreType.DMA((4, tp)),
            pltpu.SemaphoreType.DMA((levels,)),
            pltpu.SemaphoreType.DMA((levels,)),
        ],
        compiler_params=pltpu.CompilerParams(
            collective_id=2, has_side_effects=True, vmem_limit_bytes=56 << 20
        ),
        name="attn_grads",
    )(n1, d_qkv, d_branch, att, vectors)


def local(
    inputs,
    segment_ids,
    first_gain,
    query_weight,
    query_bias,
    key_value_weight,
    key_value_bias,
    output_weight,
    second_gain,
    gateup_weight,
    down_weight,
    cotangent,
):
    dp = lax.axis_size("dp")
    tp = lax.axis_size("tensor")
    rank = lax.axis_index("tensor")
    width = inputs.shape[1]
    own_rows = inputs.shape[0]
    depth = query_weight.shape[0]
    columns = query_weight.shape[1]
    kv_columns = key_value_weight.shape[1]
    hidden_units = gateup_weight.shape[2]
    heads_width = columns * tp
    head = HEAD_DIMENSION
    scale = 1.0 / math.sqrt(head)

    padded = -(-hidden_units // 256) * 256
    ff_own = jnp.stack([gateup_weight[0], gateup_weight[1], down_weight.T])
    ff_own = jnp.pad(ff_own, ((0, 0), (0, 0), (0, padded - hidden_units)))
    qb_count, kvb_count = query_bias.shape[0], key_value_bias.shape[0]
    own_kvbias = jnp.pad(key_value_bias, (0, depth - kvb_count))
    side = jnp.pad(jnp.stack([first_gain, second_gain, own_kvbias], axis=1), ((0, 0), (0, 125)))
    own_segments = lax.dynamic_slice_in_dim(segment_ids, rank * own_rows, own_rows, 0)
    (
        ff_all, grad_rows, second_rows, wq, wo, wkv, probs_low,
        residual, attended, normed_own, rot_query, all_kv, cosine, sine, vectors,
    ) = forward_part(
        dp,
        tp,
        kvb_count,
        qb_count,
        inputs,
        segment_ids[None, :],
        own_segments[:, None],
        query_weight,
        output_weight.T,
        jnp.pad(query_bias[None, :], ((0, 15), (0, 128 - qb_count))),
        jnp.concatenate([key_value_weight, side], axis=1),
        ff_own,
        cotangent,
    )
    act, lhs, mlp_terms, d_second = ff_part(dp, tp, ff_all, grad_rows, second_rows)
    ff_sh, _, _, d_branch, d_qkv, output, input_grad, vector_grads = backward_part(
        dp, tp, residual, vectors, attended, rot_query, all_kv, cosine, sine,
        d_second, cotangent, inputs, lhs, act, mlp_terms, probs_low, wo, wq, wkv,
    )
    kv_sh, q_sh, o_sh, small = attn_grads(
        dp, tp, normed_own, d_qkv, d_branch, attended, vector_grads
    )
    d = lax.axis_index("dp")

    def mine(row, count, index):
        return lax.dynamic_slice_in_dim(row, index * count, count, 0)

    return (
        output,
        input_grad,
        mine(small[0], depth, d),
        q_sh,
        mine(small[2], qb_count, rank * dp + d),
        kv_sh,
        mine(small[3], kvb_count, d),
        o_sh.T,
        mine(small[1], depth, d),
        ff_sh[:2, :, :hidden_units],
        ff_sh[2, :, :hidden_units].T,
    )


def solution(mesh):
    in_specs = (
        P(("dp", "tensor"), None),
        P("dp"),
        P("dp"),
        P("dp", "tensor"),
        P(("tensor", "dp")),
        P("dp", None),
        P("dp"),
        P("tensor", "dp"),
        P("dp"),
        P(None, "dp", "tensor"),
        P("tensor", "dp"),
        P(("dp", "tensor"), None),
    )
    out_specs = (
        P(("dp", "tensor"), None),
        P(("dp", "tensor"), None),
        P("dp"),
        P("dp", "tensor"),
        P(("tensor", "dp")),
        P("dp", None),
        P("dp"),
        P("tensor", "dp"),
        P("dp"),
        P(None, "dp", "tensor"),
        P("tensor", "dp"),
    )
    return jax.shard_map(local, mesh=mesh, in_specs=in_specs, out_specs=out_specs, check_vma=False)
```
